32 devices in a mesh: dp: 4 (over x, core), mp: 2 (over y), adp: 4 (over z).
Axes of the slice: x: 2, y: 2, z: 4, core: 2. Of those that a mesh axis runs over, the one named last changes fastest.
Arguments:
- inputs: bfloat16 [2, 16, 1024, 1024], P(None, ('dp', 'adp'), 'mp'), may hold values from -6 to 6
- memory: bfloat16 [2, 16, 1024, 1024], P(None, ('dp', 'adp'), 'mp'), may hold values from -6 to 6
- src_lengths: int32 [2, 16, 1], P(None, ('dp', 'adp')), may hold values from 1 to 1024, as said below
- self_qkv: bfloat16 [3, 1024, 1024], P(None, 'dp', 'mp'), may hold values from -0.1875 to 0.1875
- self_proj: bfloat16 [1024, 1024], P('mp', 'dp'), may hold values from -1.5 to 1.5
- cross_qkv: bfloat16 [3, 1024, 1024], P(None, 'dp', 'mp'), may hold values from -0.1875 to 0.1875
- cross_proj: bfloat16 [1024, 1024], P('mp', 'dp'), may hold values from -1.5 to 1.5
- ffn_in: bfloat16 [1024, 4096], P('dp', 'mp'), may hold values from -0.1875 to 0.1875
- ffn_out: bfloat16 [4096, 1024], P('mp', 'dp'), may hold values from -0.09375 to 0.09375
- norm_gains: bfloat16 [3, 1024], replicated, may hold values from 0.5 to 1.5
- prefix: bfloat16 [2, 30, 1024], P(None, None, 'mp'), may hold values from -6 to 6
- adapter_down: bfloat16 [1024, 512], P('dp', 'adp'), may hold values from -0.1875 to 0.1875
- adapter_up: bfloat16 [512, 1024], P('adp', 'dp'), may hold values from -0.125 to 0.125
- cotangent: bfloat16 [2, 16, 1024, 1024], P(None, ('dp', 'adp'), 'mp'), may hold values from -6 to 6
Outputs:
- result: bfloat16 [2, 16, 1024, 1024], P(None, ('dp', 'adp'), 'mp')
- input_grad: bfloat16 [2, 16, 1024, 1024], P(None, ('dp', 'adp'), 'mp')
- memory_grad: bfloat16 [2, 16, 1024, 1024], P(None, ('dp', 'adp'), 'mp')
- prefix_grad: float32 [2, 30, 1024], P(None, None, 'mp')
- adapter_down_grad: float32 [1024, 512], P(('dp', 'mp'), 'adp')
- adapter_up_grad: float32 [512, 1024], P('adp', ('dp', 'mp'))
The draws below stay inside these ranges and needn't reach their ends.
Inputs may be any that keep to these rules, and one draw needn't show every extreme that they name: `src_lengths`: in each micro-batch one sequence of one block has all 1024 source rows valid.
All inputs are finite; a program needn't handle non-finite values.
Results may differ from the reference program's by a relative error of at most 0.028.
Values may be sent and summed in bfloat16 or wider, within the bound.
A program may use at most 448 MiB of HBM per device.

```python
import jax
import jax.numpy as jnp
from jax import lax

D = 1024
HEADS = 16
HEAD_DIM = 64
FF = 4096
BOTTLENECK = 512
PREFIX_LEN = 30
SEQ_LEN = 1024
SRC_MAX = 1024
SEQS_BLK = 1
MICRO = 2
TOK_BLK = 1024
SRC_BLK = 1024
BLOCKS = 16


def draw_src_lengths(key, part):
    key = jax.random.fold_in(key, 7)
    split_keys = jax.random.split(key, 5)
    shape = (MICRO, BLOCKS, SEQS_BLK)
    first_draw = jax.random.randint(split_keys[0], shape, 1, SRC_MAX + 1)
    second_draw = jax.random.randint(split_keys[1], shape, 1, SRC_MAX + 1)
    third_draw = jax.random.randint(split_keys[2], shape, 1, SRC_MAX + 1)
    lengths_drawn = jnp.minimum(jnp.minimum(first_draw, second_draw), third_draw)
    chosen_block = jax.random.randint(split_keys[3], (MICRO, 1, 1), 0, BLOCKS)
    chosen_slot = jax.random.randint(split_keys[4], (MICRO, 1, 1), 0, SEQS_BLK)
    block_index = jnp.arange(BLOCKS, dtype=jnp.int32)[None, :, None]
    slot_index = jnp.arange(SEQS_BLK, dtype=jnp.int32)[None, None, :]
    full_here = (block_index == chosen_block) & (slot_index == chosen_slot)
    return jnp.where(full_here, SRC_MAX, lengths_drawn).astype(jnp.int32)


def steps_of(rng, shape, pieces, least, high):
    loudness, own = 1.0, jax.random.fold_in(rng, 6)
    for position, shards_of in pieces:
        steps = jnp.exp(jax.random.uniform(jax.random.fold_in(own, position), (shards_of,), jnp.float32, least / len(pieces), high / len(pieces)))
        loudness = loudness * jnp.repeat(steps, shape[position] // shards_of).reshape([-1 if axis == position else 1 for axis in range(len(shape))])
    return loudness


def scatter_about(stream_key, shape, width, bound, cuts=(), held_as=jnp.bfloat16):
    entries = width * jax.random.normal(stream_key, shape, jnp.float32)
    if cuts:
        entries = entries * steps_of(stream_key, shape, cuts, -0.22, 0.18)
    return jnp.clip(entries, -bound, bound).astype(held_as)


def setup_inputs(seed: int = 0) -> dict:
    arg_keys = jax.random.split(jax.random.key(seed), 15)
    return {
        "inputs": scatter_about(arg_keys[0], (MICRO, BLOCKS, TOK_BLK, D), 1.0, 6.0, ((1, 16), (2, 2))),
        "memory": scatter_about(arg_keys[1], (MICRO, BLOCKS, SRC_BLK, D), 1.0, 6.0, ((1, 16), (2, 2))),
        "src_lengths": draw_src_lengths(jax.random.fold_in(arg_keys[14], 71), 0),
        "self_qkv": scatter_about(arg_keys[3], (3, D, D), D ** -0.5, 0.1875, ((1, 4), (2, 2))),
        "self_proj": scatter_about(arg_keys[4], (D, D), 16 ** -0.5, 1.5, ((0, 2), (1, 4))),
        "cross_qkv": scatter_about(arg_keys[5], (3, D, D), D ** -0.5, 0.1875, ((1, 4), (2, 2))),
        "cross_proj": scatter_about(arg_keys[6], (D, D), 16 ** -0.5, 1.5, ((0, 2), (1, 4))),
        "ffn_in": scatter_about(arg_keys[7], (D, FF), D ** -0.5, 0.1875, ((0, 4), (1, 2))),
        "ffn_out": scatter_about(arg_keys[8], (FF, D), FF ** -0.5, 0.09375, ((0, 2), (1, 4))),
        "norm_gains": jnp.clip(1.0 + 0.1 * jax.random.normal(arg_keys[9], (3, D), jnp.float32), 0.5, 1.5).astype(jnp.bfloat16),
        "prefix": scatter_about(arg_keys[10], (2, PREFIX_LEN, D), 1.0, 6.0, ((2, 2),)),
        "adapter_down": scatter_about(arg_keys[11], (D, BOTTLENECK), D ** -0.5, 0.1875, ((0, 4), (1, 4))),
        "adapter_up": scatter_about(arg_keys[12], (BOTTLENECK, D), (4 * BOTTLENECK) ** -0.5, 0.125, ((0, 4), (1, 4))),
        "cotangent": scatter_about(arg_keys[13], (MICRO, BLOCKS, TOK_BLK, D), 1.0, 6.0, ((1, 16), (2, 2))),
    }


@jax.custom_vjp
def low(v):
    return lax.optimization_barrier(v.astype(jnp.bfloat16)).astype(jnp.float32)

@jax.custom_vjp
def low_back(v):
    return v

def low_keep(v):
    return (low(v), None)

def low_pass(kept, grad):
    return (grad,)

def back_keep(v):
    return (v, None)

def back_low(kept, grad):
    return (low(grad),)
low.defvjp(low_keep, low_pass)
low_back.defvjp(back_keep, back_low)
eps = 1e-05

def exact_gelu(values):
    return jax.nn.gelu(values, approximate=False)

def matmul_high(left_mat, right_mat):
    return jnp.dot(left_mat, right_mat, precision=lax.Precision.HIGHEST, preferred_element_type=jnp.float32)

def layer_norm(residual, gain_row):
    centered = residual - lax.optimization_barrier(jnp.mean(residual, axis=-1, keepdims=True))
    return centered * lax.rsqrt(lax.optimization_barrier(jnp.mean(centered * centered, axis=-1, keepdims=True)) + eps) * gain_row

def both_round(tensor):
    return low_back(low(tensor))

def to_heads(rows_mat, seq_count, length):
    return rows_mat.reshape(seq_count, length, HEADS, HEAD_DIM).transpose(0, 2, 1, 3)

def from_heads(split_mat):
    seq_count, heads_here, length, head_width = split_mat.shape
    return split_mat.transpose(0, 2, 1, 3).reshape(seq_count * length, heads_here * head_width)

def attention(queries, keys_all, values_all, allowed):
    scores = low_back(jnp.einsum('hqd,hkd->hqk', queries, keys_all, precision=lax.Precision.HIGHEST))
    scores = jnp.where(allowed, scores, -1e+30)
    weights_low = low(jax.nn.softmax(scores, axis=-1))
    return jnp.einsum('hqk,hkd->hqd', weights_low, values_all, precision=lax.Precision.HIGHEST)

def block_forward(frozen, lengths_blk, inputs_blk, memory_blk, prefix_all, down_mat, up_mat):
    self_w, self_o, cross_w, cross_o, ffn_first, ffn_second, gains = frozen
    scale = HEAD_DIM ** (-0.5)
    query_pos = lax.broadcasted_iota(jnp.int32, (SEQ_LEN, PREFIX_LEN + SEQ_LEN), 0)
    key_pos = lax.broadcasted_iota(jnp.int32, (SEQ_LEN, PREFIX_LEN + SEQ_LEN), 1)
    causal = (key_pos < PREFIX_LEN) | (key_pos - PREFIX_LEN <= query_pos)
    prefix_heads = prefix_all.reshape(2, PREFIX_LEN, HEADS, HEAD_DIM).transpose(0, 2, 1, 3)
    query_self = both_round(matmul_high(inputs_blk, self_w[0]) * scale)
    key_self = both_round(matmul_high(inputs_blk, self_w[1]))
    value_self = both_round(matmul_high(inputs_blk, self_w[2]))

    def self_seq(packed):
        query_seq, key_seq, value_seq = packed
        keys_all = jnp.concatenate([prefix_heads[0], key_seq], axis=1)
        values_all = jnp.concatenate([prefix_heads[1], value_seq], axis=1)
        return attention(query_seq, keys_all, values_all, causal)
    self_heads = lax.map(jax.checkpoint(self_seq), (to_heads(query_self, SEQS_BLK, SEQ_LEN), to_heads(key_self, SEQS_BLK, SEQ_LEN), to_heads(value_self, SEQS_BLK, SEQ_LEN)))
    attn_rows = both_round(from_heads(self_heads))
    resid_one = inputs_blk + low_back(matmul_high(attn_rows, self_o))
    normed_one = layer_norm(resid_one, gains[0])
    one_low = low(normed_one)
    cross_query = both_round(matmul_high(one_low, cross_w[0]) * scale)
    cross_keys = both_round(matmul_high(memory_blk, cross_w[1]))
    cross_values = both_round(matmul_high(memory_blk, cross_w[2]))

    def cross_seq(packed):
        query_seq, key_seq, value_seq, length = packed
        allowed = lax.broadcasted_iota(jnp.int32, (SEQ_LEN, SRC_MAX), 1) < length
        return attention(query_seq, key_seq, value_seq, allowed)
    cross_heads = lax.map(jax.checkpoint(cross_seq), (to_heads(cross_query, SEQS_BLK, SEQ_LEN), to_heads(cross_keys, SEQS_BLK, SRC_MAX), to_heads(cross_values, SEQS_BLK, SRC_MAX), lengths_blk))
    cross_rows = both_round(from_heads(cross_heads))
    resid_two = normed_one + low_back(matmul_high(cross_rows, cross_o))
    normed_two = layer_norm(resid_two, gains[1])
    two_low = low(normed_two)
    hidden_pre = low_back(matmul_high(two_low, ffn_first))
    hidden_act = low(exact_gelu(hidden_pre))
    adapter_pre = low_back(matmul_high(two_low, down_mat))
    adapter_act = low(exact_gelu(adapter_pre))
    branch = low_back(matmul_high(hidden_act, ffn_second) + 4.0 * matmul_high(adapter_act, up_mat))
    return layer_norm(normed_two + branch, gains[2])

def reference(inputs, memory, src_lengths, self_qkv, self_proj, cross_qkv, cross_proj, ffn_in, ffn_out, norm_gains, prefix, adapter_down, adapter_up, cotangent):
    frozen = tuple((weight_arr.astype(jnp.float32) for weight_arr in (self_qkv, self_proj, cross_qkv, cross_proj, ffn_in, ffn_out, norm_gains)))
    prefix_f = prefix.astype(jnp.float32)
    down_f = adapter_down.astype(jnp.float32)
    up_f = adapter_up.astype(jnp.float32)
    block_count = MICRO * BLOCKS
    flat_inputs = inputs.reshape(block_count, TOK_BLK, D)
    flat_memory = memory.reshape(block_count, SRC_BLK, D)
    flat_lengths = src_lengths.reshape(block_count, SEQS_BLK).astype(jnp.int32)
    flat_cotangent = cotangent.reshape(block_count, TOK_BLK, D)

    def one_block(carry, packed):
        inputs_blk, memory_blk, lengths_blk, cotangent_blk = packed

        def forward(inputs_f, memory_f, prefix_in, down_in, up_in):
            return block_forward(frozen, lengths_blk, inputs_f, memory_f, prefix_in, down_in, up_in)
        output_blk, pullback = jax.vjp(forward, inputs_blk.astype(jnp.float32), memory_blk.astype(jnp.float32), prefix_f, down_f, up_f)
        grad_inputs, grad_memory, grad_prefix, grad_down, grad_up = pullback(cotangent_blk.astype(jnp.float32))
        new_carry = (carry[0] + grad_prefix, carry[1] + grad_down, carry[2] + grad_up)
        return (new_carry, (output_blk.astype(jnp.bfloat16), grad_inputs.astype(jnp.bfloat16), grad_memory.astype(jnp.bfloat16)))
    start_carry = (jnp.zeros((2, PREFIX_LEN, D), jnp.float32), jnp.zeros((D, BOTTLENECK), jnp.float32), jnp.zeros((BOTTLENECK, D), jnp.float32))
    totals, stacked = lax.scan(one_block, start_carry, (flat_inputs, flat_memory, flat_lengths, flat_cotangent))
    result = stacked[0].reshape(MICRO, BLOCKS, TOK_BLK, D)
    input_grad = stacked[1].reshape(MICRO, BLOCKS, TOK_BLK, D)
    memory_grad = stacked[2].reshape(MICRO, BLOCKS, SRC_BLK, D)
    return (result, input_grad, memory_grad, totals[0], totals[1], totals[2])
```

```python
import functools
import math

import jax
import jax.numpy as jnp
from jax import lax
from jax.experimental import pallas as pl
from jax.experimental.pallas import tpu as pltpu
from jax.sharding import PartitionSpec as P

HEAD_DIM = 64
PREFIX_LEN = 30
SEQ_LEN = 1024
SRC_MAX = 1024
SEQS_BLK = 1
MICRO = 2


eps = 1e-05


def exact_gelu(values):
    return jax.nn.gelu(values, approximate=False)


def norm_forward(residual, gain_row):
    centered = residual - jnp.mean(residual, axis=-1, keepdims=True)
    inv_std = lax.rsqrt(jnp.mean(centered * centered, axis=-1, keepdims=True) + eps)
    return centered * inv_std * gain_row


def norm_backward(upstream, residual, gain_row):
    centered = residual - jnp.mean(residual, axis=-1, keepdims=True)
    inv_std = lax.rsqrt(jnp.mean(centered * centered, axis=-1, keepdims=True) + eps)
    normed = centered * inv_std
    scaled = upstream * gain_row
    inner_mean = jnp.mean(scaled * normed, axis=-1, keepdims=True)
    return inv_std * (scaled - jnp.mean(scaled, axis=-1, keepdims=True) - normed * inner_mean)


def gelu_back(pre_act, upstream):
    return jax.vjp(exact_gelu, pre_act)[1](upstream)[0]


def matmul(left_mat, right_mat):
    return jnp.dot(left_mat, right_mat, preferred_element_type=jnp.float32)


def matmul_nt(left_mat, right_mat):
    return lax.dot_general(
        left_mat, right_mat, (((1,), (1,)), ((), ())), preferred_element_type=jnp.float32
    )


def matmul_tn(left_mat, right_mat):
    return lax.dot_general(
        left_mat, right_mat, (((0,), (0,)), ((), ())), preferred_element_type=jnp.float32
    )


def to_heads(rows_mat, seq_count, length):
    heads_here = rows_mat.shape[-1] // HEAD_DIM
    return rows_mat.reshape(seq_count, length, heads_here, HEAD_DIM).transpose(0, 2, 1, 3)


def from_heads(split_mat):
    seq_count, heads_here, length, head_width = split_mat.shape
    return split_mat.transpose(0, 2, 1, 3).reshape(seq_count * length, heads_here * head_width)


def causal_allowed():
    query_pos = lax.broadcasted_iota(jnp.int32, (SEQ_LEN, PREFIX_LEN + SEQ_LEN), 0)
    key_pos = lax.broadcasted_iota(jnp.int32, (SEQ_LEN, PREFIX_LEN + SEQ_LEN), 1)
    return (key_pos < PREFIX_LEN) | (key_pos - PREFIX_LEN <= query_pos)


def source_allowed(length):
    return lax.broadcasted_iota(jnp.int32, (SEQ_LEN, SRC_MAX), 1) < length


def attend_forward(queries, keys_all, values_all, allowed):
    scores = jnp.einsum("hqd,hkd->hqk", queries, keys_all, preferred_element_type=jnp.float32)
    scores = jnp.where(allowed, scores, -1e30)
    top_score = jnp.max(scores, axis=-1, keepdims=True)
    expo_scores = jnp.exp(scores - top_score)
    row_total = jnp.sum(expo_scores, axis=-1, keepdims=True)
    weights_low = (expo_scores / row_total).astype(jnp.bfloat16)
    mixed = jnp.einsum("hqk,hkd->hqd", weights_low, values_all, preferred_element_type=jnp.float32)
    return (mixed.astype(jnp.bfloat16), top_score + jnp.log(row_total))


def attend_backward(queries, keys_all, values_all, allowed, log_total, grad_out):
    scores = jnp.einsum("hqd,hkd->hqk", queries, keys_all, preferred_element_type=jnp.float32)
    scores = jnp.where(allowed, scores, -1e30)
    soft_weights = jnp.exp(scores - log_total)
    grad_soft = jnp.einsum("hqd,hkd->hqk", grad_out, values_all, preferred_element_type=jnp.float32)
    inner_sum = jnp.sum(soft_weights * grad_soft, axis=-1, keepdims=True)
    grad_scores = (soft_weights * (grad_soft - inner_sum)).astype(jnp.bfloat16)
    grad_query = jnp.einsum(
        "hqk,hkd->hqd", grad_scores, keys_all, preferred_element_type=jnp.float32
    )
    grad_keys = jnp.einsum("hqk,hqd->hkd", grad_scores, queries, preferred_element_type=jnp.float32)
    grad_values = jnp.einsum(
        "hqk,hqd->hkd",
        soft_weights.astype(jnp.bfloat16),
        grad_out,
        preferred_element_type=jnp.float32,
    )
    return (grad_query, grad_keys, grad_values)


def gather_rows(rows_low):
    return lax.all_gather(rows_low, "mp", axis=0, tiled=True)


def reduce_rows(term_fn, own_count):
    return lax.psum_scatter(
        term_fn(jnp.int32(0), own_count * lax.axis_size("mp")).astype(jnp.bfloat16),
        "mp",
        scatter_dimension=0,
        tiled=True,
    ).astype(jnp.float32)


def gather_adapter(rows_low):
    return lax.all_gather(rows_low, "adp", axis=0, tiled=True)


def reduce_adapter(term_fn, own_count):
    return lax.psum_scatter(
        term_fn(jnp.int32(0), own_count * lax.axis_size("adp")).astype(jnp.bfloat16),
        "adp",
        scatter_dimension=0,
        tiled=True,
    ).astype(jnp.float32)


def reduce_prefix(grad_prefix):
    return lax.psum(grad_prefix, ("dp", "adp"))


def reduce_adapter_grads(grad_down, grad_up):
    return (
        lax.psum_scatter(grad_down, ("dp", "mp"), scatter_dimension=0, tiled=True),
        lax.psum_scatter(grad_up, ("dp", "mp"), scatter_dimension=1, tiled=True),
    )


def shards(
    inputs,
    memory,
    src_lengths,
    self_qkv,
    self_proj,
    cross_qkv,
    cross_proj,
    ffn_in,
    ffn_out,
    norm_gains,
    prefix,
    adapter_down,
    adapter_up,
    cotangent,
):
    scale = HEAD_DIM ** (-0.5)
    own_rows = inputs.shape[2]
    gains = norm_gains.astype(jnp.float32)
    causal = causal_allowed()
    prefix_heads = to_heads(prefix, 2, PREFIX_LEN)
    prefix_keys = prefix_heads[0]
    prefix_values = prefix_heads[1]
    results = []
    input_grads = []
    memory_grads = []
    prefix_acc = None
    down_acc = None
    up_acc = None
    for micro_index in range(MICRO):
        self_w, self_o, cross_w, cross_o, down_w, up_w = (
            lax.all_gather(self_qkv, "dp", axis=1, tiled=True),
            lax.all_gather(self_proj, "dp", axis=1, tiled=True),
            lax.all_gather(cross_qkv, "dp", axis=1, tiled=True),
            lax.all_gather(cross_proj, "dp", axis=1, tiled=True),
            lax.all_gather(adapter_down, "dp", axis=0, tiled=True),
            lax.all_gather(adapter_up, "dp", axis=1, tiled=True),
        )
        ffn_first, ffn_second = (
            lax.all_gather(ffn_in, "dp", axis=0, tiled=True),
            lax.all_gather(ffn_out, "dp", axis=1, tiled=True),
        )
        x_rows = inputs[micro_index, 0]
        lengths_here = src_lengths[micro_index, 0]
        x_full = gather_rows(x_rows)
        mem_full = lax.all_gather(memory[micro_index, 0], "mp", axis=0, tiled=True)
        projected = jnp.einsum("td,cde->cte", x_full, self_w, preferred_element_type=jnp.float32)
        query_self = to_heads((projected[0] * scale).astype(jnp.bfloat16), SEQS_BLK, SEQ_LEN)
        key_self = to_heads(projected[1].astype(jnp.bfloat16), SEQS_BLK, SEQ_LEN)
        value_self = to_heads(projected[2].astype(jnp.bfloat16), SEQS_BLK, SEQ_LEN)

        def self_forward(packed):
            query_seq, key_seq, value_seq = packed
            keys_all = jnp.concatenate([prefix_keys, key_seq], axis=1)
            values_all = jnp.concatenate([prefix_values, value_seq], axis=1)
            return attend_forward(query_seq, keys_all, values_all, causal)

        attn_self, lse_self = lax.map(self_forward, (query_self, key_self, value_self))
        attn_rows = from_heads(attn_self)

        def self_term(first_row, row_count):
            return matmul(attn_rows, self_o)

        resid_one = x_rows.astype(jnp.float32) + reduce_rows(self_term, own_rows)
        normed_one = norm_forward(resid_one, gains[0])
        one_full = gather_rows(normed_one.astype(jnp.bfloat16))
        cross_query = to_heads(
            (matmul(one_full, cross_w[0]) * scale).astype(jnp.bfloat16), SEQS_BLK, SEQ_LEN
        )
        memory_proj = jnp.einsum(
            "td,cde->cte", mem_full, cross_w[1:], preferred_element_type=jnp.float32
        )
        cross_keys = to_heads(memory_proj[0].astype(jnp.bfloat16), SEQS_BLK, SRC_MAX)
        cross_values = to_heads(memory_proj[1].astype(jnp.bfloat16), SEQS_BLK, SRC_MAX)

        def cross_forward(packed):
            query_seq, key_seq, value_seq, length = packed
            return attend_forward(query_seq, key_seq, value_seq, source_allowed(length))

        attn_cross, lse_cross = lax.map(
            cross_forward, (cross_query, cross_keys, cross_values, lengths_here)
        )
        cross_rows = from_heads(attn_cross)

        def cross_term(first_row, row_count):
            return matmul(cross_rows, cross_o)

        resid_two = normed_one + reduce_rows(cross_term, own_rows)
        normed_two = norm_forward(resid_two, gains[1])
        two_low = normed_two.astype(jnp.bfloat16)
        two_full = gather_rows(two_low)
        hidden_pre = matmul(two_full, ffn_first)
        hidden_act = exact_gelu(hidden_pre).astype(jnp.bfloat16)

        def ffn_term(first_row, row_count):
            return matmul(hidden_act, ffn_second)

        ffn_rows = reduce_rows(ffn_term, own_rows)
        adapter_in = gather_adapter(two_low)
        adapter_pre = matmul(adapter_in, down_w)
        adapter_act = exact_gelu(adapter_pre).astype(jnp.bfloat16)

        def adapter_term(first_row, row_count):
            return matmul(adapter_act, up_w)

        adapter_rows = reduce_adapter(adapter_term, own_rows)
        resid_three = normed_two + ffn_rows + 4.0 * adapter_rows
        results.append(norm_forward(resid_three, gains[2]).astype(jnp.bfloat16))
        grad_three = norm_backward(
            cotangent[micro_index, 0].astype(jnp.float32), resid_three, gains[2]
        )
        grad_branch = grad_three.astype(jnp.bfloat16)
        grad_adapter = gather_adapter(grad_branch) * 4.0
        up_term = matmul_tn(adapter_act, grad_adapter)
        grad_adapter_pre = gelu_back(adapter_pre, matmul_nt(grad_adapter, up_w)).astype(
            jnp.bfloat16
        )
        down_term = matmul_tn(adapter_in, grad_adapter_pre)

        def adapter_back_term(first_row, row_count):
            return matmul_nt(grad_adapter_pre, down_w)

        adapter_back = reduce_adapter(adapter_back_term, own_rows)
        branch_full = gather_rows(grad_branch)
        grad_pre = gelu_back(hidden_pre, matmul_nt(branch_full, ffn_second)).astype(jnp.bfloat16)

        def ffn_back_term(first_row, row_count):
            return matmul_nt(grad_pre, ffn_first)

        ffn_back = reduce_rows(ffn_back_term, own_rows)
        grad_mid = norm_backward(grad_three + ffn_back + adapter_back, resid_two, gains[1])
        mid_full = gather_rows(grad_mid.astype(jnp.bfloat16))
        grad_cross_out = to_heads(
            matmul_nt(mid_full, cross_o).astype(jnp.bfloat16), SEQS_BLK, SEQ_LEN
        )

        def cross_backward(packed):
            query_seq, key_seq, value_seq, lse_seq, grad_seq, length = packed
            return attend_backward(
                query_seq, key_seq, value_seq, source_allowed(length), lse_seq, grad_seq
            )

        cross_gq, cross_gk, cross_gv = lax.map(
            cross_backward,
            (cross_query, cross_keys, cross_values, lse_cross, grad_cross_out, lengths_here),
        )
        cross_gq_rows = from_heads(cross_gq).astype(jnp.bfloat16) * scale

        def cross_query_term(first_row, row_count):
            return matmul_nt(cross_gq_rows, cross_w[0])

        grad_one = grad_mid + reduce_rows(cross_query_term, own_rows)
        memory_stack = jnp.stack(
            [from_heads(cross_gk).astype(jnp.bfloat16), from_heads(cross_gv).astype(jnp.bfloat16)]
        )
        memory_grads.append(
            lax.psum_scatter(
                jnp.einsum(
                    "cte,cde->td", memory_stack, cross_w[1:], preferred_element_type=jnp.float32
                ).astype(jnp.bfloat16),
                "mp",
                scatter_dimension=0,
                tiled=True,
            )
        )
        grad_first = norm_backward(grad_one, resid_one, gains[0])
        first_full = gather_rows(grad_first.astype(jnp.bfloat16))
        grad_self_out = to_heads(
            matmul_nt(first_full, self_o).astype(jnp.bfloat16), SEQS_BLK, SEQ_LEN
        )

        def self_backward(packed):
            query_seq, key_seq, value_seq, lse_seq, grad_seq = packed
            keys_all = jnp.concatenate([prefix_keys, key_seq], axis=1)
            values_all = jnp.concatenate([prefix_values, value_seq], axis=1)
            return attend_backward(query_seq, keys_all, values_all, causal, lse_seq, grad_seq)

        self_gq, self_gk, self_gv = lax.map(
            self_backward, (query_self, key_self, value_self, lse_self, grad_self_out)
        )
        prefix_key_grad = from_heads(jnp.sum(self_gk[:, :, :PREFIX_LEN], axis=0)[None])
        prefix_value_grad = from_heads(jnp.sum(self_gv[:, :, :PREFIX_LEN], axis=0)[None])
        prefix_term = jnp.stack([prefix_key_grad, prefix_value_grad])
        self_stack = jnp.stack(
            [
                from_heads(self_gq).astype(jnp.bfloat16) * scale,
                from_heads(self_gk[:, :, PREFIX_LEN:]).astype(jnp.bfloat16),
                from_heads(self_gv[:, :, PREFIX_LEN:]).astype(jnp.bfloat16),
            ]
        )

        def input_term(first_row, row_count):
            return jnp.einsum("cte,cde->td", self_stack, self_w, preferred_element_type=jnp.float32)

        input_grads.append((grad_first + reduce_rows(input_term, own_rows)).astype(jnp.bfloat16))
        prefix_term = reduce_prefix(prefix_term)
        down_term, up_term = reduce_adapter_grads(down_term, up_term)
        prefix_acc = prefix_term if prefix_acc is None else prefix_acc + prefix_term
        down_acc = down_term if down_acc is None else down_acc + down_term
        up_acc = up_term if up_acc is None else up_acc + up_term
    return (
        jnp.stack(results)[:, None],
        jnp.stack(input_grads)[:, None],
        jnp.stack(memory_grads)[:, None],
        prefix_acc,
        down_acc,
        up_acc,
    )


F32 = jnp.float32
BF = jnp.bfloat16
EPS = 1e-05
LOG2E = 1.4426950408889634

BQF = 512
BQ = 512
PRE = 32
VMEM_BYTES = 60 * 2**20
NEG = -1e30
LN2 = 0.6931471805599453


def dot_mm(a, b, ca, cb):
    return lax.dot_general(a, b, (((ca,), (cb,)), ((), ())), preferred_element_type=jnp.float32)


def pick_head(h, mat):
    rows = lax.broadcasted_iota(jnp.int32, mat.shape, 0)
    return jnp.where((rows // HEAD_DIM) == h, mat, jnp.zeros_like(mat))


def attn_fwd_body(causal, n_ref, q_ref, k_ref, v_ref, pk_ref, pvt_ref, a_ref, p_ref, pp_ref, l_ref):
    t = q_ref.shape[0]
    s = k_ref.shape[0]
    nb = t // BQF
    qt = q_ref[...].T
    vt = v_ref[...].T
    ones = jnp.ones((16, s), jnp.bfloat16)
    work = [(h, j) for h in range(2) for j in range(nb)]

    def scores(h, j):
        kk = (j + 1) * BQF if causal else s
        qb = pick_head(h, qt[:, j * BQF:(j + 1) * BQF])
        st = dot_mm(k_ref[:kk], qb, 1, 0)
        return st, dot_mm(pk_ref[...], qb, 1, 0) if causal else None

    res = {}
    ahead = scores(*work[0])
    for w, (h, j) in enumerate(work):
        st, sp = ahead
        if w + 1 < len(work):
            ahead = scores(*work[w + 1])
        kk = st.shape[0]
        js = slice(j * BQF, (j + 1) * BQF)
        if causal:
            krow = lax.broadcasted_iota(jnp.int32, (BQF, BQF), 0)
            qcol = lax.broadcasted_iota(jnp.int32, (BQF, BQF), 1)
            diag = jnp.where(krow <= qcol, st[kk - BQF:], NEG)
            st = jnp.concatenate([st[:kk - BQF], diag], axis=0) if kk > BQF else diag
            prow = lax.broadcasted_iota(jnp.int32, sp.shape, 0)
            sp = jnp.where(prow < n_ref[0], sp, NEG)
            m = jnp.maximum(jnp.max(st, axis=0, keepdims=True), jnp.max(sp, axis=0, keepdims=True))
            pp = jnp.exp2(sp - m).astype(jnp.bfloat16)
            pp_ref[h, :, js] = pp
        else:
            krow = lax.broadcasted_iota(jnp.int32, st.shape, 0)
            st = jnp.where(krow < n_ref[0], st, NEG)
            m = jnp.max(st, axis=0, keepdims=True)
        p = jnp.exp2(st - m).astype(jnp.bfloat16)
        p_ref[h, :kk, js] = p
        hs = slice(h * HEAD_DIM, (h + 1) * HEAD_DIM)
        ot = dot_mm(jnp.concatenate([vt[hs, :kk], ones[:, :kk]], axis=0), p, 1, 0)
        if causal:
            ot += dot_mm(jnp.concatenate([pvt_ref[hs], ones[:, :PRE]], axis=0), pp, 1, 0)
        il = 1.0 / ot[HEAD_DIM:HEAD_DIM + 1]
        res[h, j] = (ot[:HEAD_DIM] * il, il)
    for h in range(2):
        l_ref[0, h:h + 1] = jnp.concatenate([res[h, j][1] for j in range(nb)], axis=1)
    at = jnp.concatenate([jnp.concatenate([res[h, j][0] for j in range(nb)], axis=1) for h in range(2)], axis=0)
    a_ref[...] = at.astype(jnp.bfloat16).T


def attn_fwd(n, q, k, v, pk=None, pvt=None):
    t, w = q.shape
    s = k.shape[0]
    pairs = w // 128
    causal = pk is not None
    if not causal:
        pk = jnp.zeros((PRE, w), jnp.bfloat16)
        pvt = jnp.zeros((w, PRE), jnp.bfloat16)
    col = lambda g: (0, g)
    lead = lambda g: (g, 0, 0)
    bf = jnp.bfloat16
    return pl.pallas_call(
        functools.partial(attn_fwd_body, causal),
        grid=(pairs,),
        in_specs=[
            pl.BlockSpec(memory_space=pltpu.SMEM),
            pl.BlockSpec((t, 128), col), pl.BlockSpec((s, 128), col), pl.BlockSpec((s, 128), col),
            pl.BlockSpec((PRE, 128), col), pl.BlockSpec((128, PRE), lambda g: (g, 0)),
        ],
        out_specs=[
            pl.BlockSpec((t, 128), col), pl.BlockSpec((2, s, t), lead),
            pl.BlockSpec((2, PRE, t), lead), pl.BlockSpec((1, 2, t), lead),
        ],
        out_shape=[
            jax.ShapeDtypeStruct((t, w), bf), jax.ShapeDtypeStruct((2 * pairs, s, t), bf),
            jax.ShapeDtypeStruct((2 * pairs, PRE, t), bf), jax.ShapeDtypeStruct((pairs, 2, t), jnp.float32),
        ],
        compiler_params=pltpu.CompilerParams(vmem_limit_bytes=VMEM_BYTES),
        cost_estimate=pl.CostEstimate(
            flops=24 * t * s * w, bytes_accessed=4 * t * s * pairs, transcendentals=t * s * 2 * pairs),
    )(n, q, k, v, pk, pvt)


def attn_bwd_body(causal, q_ref, k_ref, v_ref, a_ref, da_ref, l_ref, p_ref, pp_ref, pk_ref, pv_ref,
                  dq_ref, dk_ref, dv_ref, dpk_ref, dpv_ref):
    t = q_ref.shape[0]
    s = k_ref.shape[0]
    nb = t // BQ
    qt = q_ref[...].T
    kt = k_ref[...].T
    dat = da_ref[...].T.astype(jnp.float32)
    prod = dat * a_ref[...].T.astype(jnp.float32)
    pkt = pk_ref[...].T
    work = [(h, j) for h in range(2) for j in range(nb)]
    head = {}
    for h in range(2):
        hs = slice(h * HEAD_DIM, (h + 1) * HEAD_DIM)
        il = l_ref[0, h:h + 1]
        head[h] = ((dat * il).astype(jnp.bfloat16), jnp.sum(prod[hs], axis=0, keepdims=True) * il)

    def soft_grad(h, j):
        js = slice(j * BQ, (j + 1) * BQ)
        kk = (j + 1) * BQ if causal else s
        dab = pick_head(h, head[h][0][:, js])
        return dot_mm(v_ref[:kk], dab, 1, 0), dot_mm(pv_ref[...], dab, 1, 0) if causal else None

    def add(tot, new):
        return new if tot is None else tot + new

    res = {}
    dpk = [None, None]
    dpv = [None, None]
    dkb = [[None] * nb, [None] * nb]
    dvb = [[None] * nb, [None] * nb]
    ahead = soft_grad(*work[0])
    for w, (h, j) in enumerate(work):
        dp, dpp = ahead
        if w + 1 < len(work):
            ahead = soft_grad(*work[w + 1])
        hs = slice(h * HEAD_DIM, (h + 1) * HEAD_DIM)
        js = slice(j * BQ, (j + 1) * BQ)
        kk = dp.shape[0]
        dl = head[h][1][:, js]
        dah = head[h][0][hs, js]
        p = p_ref[h, :kk, js]
        ds = (p.astype(jnp.float32) * (dp - dl)).astype(jnp.bfloat16)
        dq = dot_mm(kt[hs, :kk], ds, 1, 0)
        if causal:
            pp = pp_ref[h, :, js]
            dsp = (pp.astype(jnp.float32) * (dpp - dl)).astype(jnp.bfloat16)
            dq += dot_mm(pkt[hs], dsp, 1, 0)
            dpk[h] = add(dpk[h], dot_mm(qt[hs, js], dsp, 1, 1))
            dpv[h] = add(dpv[h], dot_mm(dah, pp, 1, 1))
        res[h, j] = dq
        dv = dot_mm(dah, p, 1, 1)
        dk = dot_mm(qt[hs, js], ds, 1, 1)
        if causal:
            for i in range(kk // BQ):
                dvb[h][i] = add(dvb[h][i], dv[:, i * BQ:(i + 1) * BQ])
                dkb[h][i] = add(dkb[h][i], dk[:, i * BQ:(i + 1) * BQ])
        else:
            dvb[h] = [add(dvb[h][0], dv)]
            dkb[h] = [add(dkb[h][0], dk)]
    both = lambda f: jnp.concatenate([f(0), f(1)], axis=0)
    dq_ref[...] = (both(lambda h: jnp.concatenate([res[h, j] for j in range(nb)], axis=1))
                   * HEAD_DIM ** -0.5).astype(jnp.bfloat16).T
    dk_ref[...] = (both(lambda h: jnp.concatenate(dkb[h], axis=1)) * LN2).astype(jnp.bfloat16).T
    dv_ref[...] = both(lambda h: jnp.concatenate(dvb[h], axis=1)).astype(jnp.bfloat16).T
    if causal:
        dpk_ref[...] = both(lambda h: dpk[h]) * LN2
        dpv_ref[...] = both(lambda h: dpv[h])
    else:
        dpk_ref[...] = jnp.zeros_like(dpk_ref)
        dpv_ref[...] = jnp.zeros_like(dpv_ref)


def attn_bwd(q, k, v, a, da, il, p, pp, pk=None, pv=None):
    t, w = q.shape
    s = k.shape[0]
    pairs = w // 128
    causal = pk is not None
    if not causal:
        pk = jnp.zeros((PRE, w), jnp.bfloat16)
        pv = pk
    col = lambda g: (0, g)
    lead = lambda g: (g, 0, 0)
    f32, bf = jnp.float32, jnp.bfloat16
    return pl.pallas_call(
        functools.partial(attn_bwd_body, causal),
        grid=(pairs,),
        in_specs=[
            pl.BlockSpec((t, 128), col), pl.BlockSpec((s, 128), col), pl.BlockSpec((s, 128), col),
            pl.BlockSpec((t, 128), col), pl.BlockSpec((t, 128), col),
            pl.BlockSpec((1, 2, t), lead), pl.BlockSpec((2, s, t), lead), pl.BlockSpec((2, PRE, t), lead),
            pl.BlockSpec((PRE, 128), col), pl.BlockSpec((PRE, 128), col),
        ],
        out_specs=[
            pl.BlockSpec((t, 128), col), pl.BlockSpec((s, 128), col), pl.BlockSpec((s, 128), col),
            pl.BlockSpec((128, PRE), lambda g: (g, 0)), pl.BlockSpec((128, PRE), lambda g: (g, 0)),
        ],
        out_shape=[
            jax.ShapeDtypeStruct((t, w), bf), jax.ShapeDtypeStruct((s, w), bf), jax.ShapeDtypeStruct((s, w), bf),
            jax.ShapeDtypeStruct((w, PRE), f32), jax.ShapeDtypeStruct((w, PRE), f32),
        ],
        compiler_params=pltpu.CompilerParams(vmem_limit_bytes=VMEM_BYTES),
        cost_estimate=pl.CostEstimate(flops=40 * t * s * w, bytes_accessed=4 * t * s * pairs, transcendentals=0),
    )(q, k, v, a, da, il, p, pp, pk, pv)


def erf_parts(v):
    mag = jnp.abs(v)
    expo = jnp.exp2(v * v * (-0.5 * LOG2E))
    t = 1.0 / (1.0 + (0.3275911 * 0.5 ** 0.5) * mag)
    poly = t * (0.254829592 + t * (-0.284496736 + t * (1.421413741 + t * (-1.453152027 + t * 1.061405429))))
    half = 0.5 * poly * expo
    return jnp.where(v < 0.0, half, 1.0 - half), expo * (2.0 * math.pi) ** -0.5


def gelu_pair(v):
    cdf, pdf = erf_parts(v)
    return v * cdf, cdf + v * pdf


def normalize(z):
    centered = z - jnp.mean(z, axis=-1, keepdims=True)
    inv = lax.rsqrt(jnp.mean(centered * centered, axis=-1, keepdims=True) + EPS)
    return centered * inv, inv


def norm_back(e, u, inv, gain):
    w = e * gain
    return inv * (w - jnp.mean(w, axis=-1, keepdims=True) - u * jnp.mean(w * u, axis=-1, keepdims=True))


def glue(pieces):
    rows = [jnp.concatenate(list(row), axis=1) if len(row) > 1 else row[0] for row in pieces]
    return jnp.concatenate(rows, axis=0) if len(rows) > 1 else rows[0]


def fused(terms, rows, consts, outs, body, tile, pick=None, dp=None, steps=None):
    t = rows[0].shape[0]
    steps = t // tile if steps is None else steps
    flat, place = [], []
    for term in terms:
        grid_of = []
        for row in term:
            line = []
            for piece in row:
                known = [i for i, f in enumerate(flat) if f is piece]
                if not known:
                    flat.append(piece)
                    known = [len(flat) - 1]
                line.append(known[0])
            grid_of.append(line)
        place.append(grid_of)
    nf, nr, nc = len(flat), len(rows), len(consts)

    def kernel(sc_ref, *refs):
        mats = [[[refs[i] for i in line] for line in grid_of] for grid_of in place]
        body(mats, refs[nf:nf + nr], refs[nf + nr:nf + nr + nc], refs[nf + nr + nc:], sc_ref[1])

    scal = jnp.stack([jnp.int32(0) if pick is None else pick, jnp.int32(0) if dp is None else dp])
    whole = lambda a: pl.BlockSpec(a.shape, lambda i, sc: (0,) * a.ndim, pipeline_mode=pl.Buffered(1))
    flops = 2 * sum(p.size for term in terms for row in term for p in row) * tile * steps
    nbytes = sum(2 * f.size for f in flat) + sum(r.size * r.dtype.itemsize for r in rows)
    return pl.pallas_call(
        kernel,
        grid_spec=pltpu.PrefetchScalarGridSpec(
            num_scalar_prefetch=1,
            grid=(steps,),
            in_specs=[whole(f) for f in flat]
            + [pl.BlockSpec((tile, r.shape[1]), lambda i, sc: (i + sc[0], 0)) for r in rows]
            + [whole(c) for c in consts],
            out_specs=[pl.BlockSpec((tile, c), lambda i, sc: (i, 0)) for _, c, _ in outs],
        ),
        out_shape=[jax.ShapeDtypeStruct((r, c), d) for r, c, d in outs],
        compiler_params=pltpu.CompilerParams(vmem_limit_bytes=VMEM_BYTES),
        cost_estimate=pl.CostEstimate(flops=flops, bytes_accessed=nbytes, transcendentals=0),
    )(scal, *flat, *rows, *consts)


def load(mat):
    return glue([[ref[...] for ref in line] for line in mat])


def project(lhs, mats, scales):
    t = lhs.shape[0]

    def body(ms, rows, consts, outs, dp):
        x = rows[0][...]
        for m, scale, out in zip(ms, scales, outs):
            y = dot_mm(x, load(m), 1, 0)
            out[...] = (y if scale == 1.0 else y * scale).astype(BF)

    width = sum(p.shape[1] for p in mats[0][0])
    return fused(mats, [lhs], [], [(t, width, BF)] * len(mats), body, min(512, t))


def project_back(lhs, mats):
    t = lhs.shape[0]

    def body(ms, rows, consts, outs, dp):
        x = rows[0][...]
        for m, out in zip(ms, outs):
            out[...] = dot_mm(x, load(m), 1, 1).astype(BF)

    return fused(mats, [lhs], [], [(t, sum(line[0].shape[0] for line in m), BF) for m in mats], body, min(512, t))


def add_norm(resid, gain_in, lhss, mats, gain):
    t, d = resid.shape

    def body(ms, rows, consts, outs, dp):
        z = rows[0][...].astype(F32)
        if gain_in is not None:
            z = z * consts[1][...]
        for lhs, m in zip(rows[1:], ms):
            z = z + dot_mm(lhs[...], load(m), 1, 0)
        u, inv = normalize(z)
        outs[0][...] = u
        outs[1][...] = inv
        outs[2][...] = (u * consts[0][...]).astype(BF)

    consts = [gain] + ([] if gain_in is None else [gain_in])
    return fused(mats, [resid] + lhss, consts, [(t, d, F32), (t, 1, F32), (t, d, BF)], body, min(512, t))


def hidden_forward(lhs, mat, trans):
    t = lhs.shape[0]
    width = sum(line[0].shape[0] for line in mat) if trans else sum(p.shape[1] for p in mat[0])

    def body(ms, rows, consts, outs, dp):
        x = rows[0][...]
        w = load(ms[0])
        for c in range(width // 256):
            cs = slice(c * 256, (c + 1) * 256)
            g = dot_mm(x, w[cs], 1, 1) if trans else dot_mm(x, w[:, cs], 1, 0)
            act, slope = gelu_pair(g)
            outs[0][:, cs] = act.astype(BF)
            outs[1][:, cs] = slope.astype(BF)

    return fused([mat], [lhs], [], [(t, width, BF)] * 2, body, min(512, t))


def hidden_backward(lhs, mat, slope, scale):
    t, width = slope.shape

    def body(ms, rows, consts, outs, dp):
        g = dot_mm(rows[0][...], load(ms[0]), 1, 1)
        outs[0][...] = (g * scale * rows[1][...].astype(F32)).astype(BF)

    return fused([mat], [lhs, slope], [], [(t, width, BF)], body, min(512, t))[0]


def unpermute_store(out, value, dp):
    for r in range(value.shape[1] // 256):
        out[:, pl.ds(pl.multiple_of((dp ^ r) * 256, 256), 256)] = value[:, r * 256:(r + 1) * 256].astype(out.dtype)


def last_norm(u2, gain2, acts, mats, adapt, up, gain3, cot, dp):
    t, d = u2.shape
    na = len(acts)

    def body(ms, rows, consts, outs, dp):
        z = rows[0][...] * consts[0][...]
        for lhs, m in zip(rows[1:1 + na], ms[:na]):
            z = z + dot_mm(lhs[...], load(m), 1, 0)
        z = z + 4.0 * dot_mm(rows[1 + na][...], load(ms[na]), 1, 0)
        u, inv = normalize(z)
        unpermute_store(outs[0], u * consts[1][...], dp)
        dz = norm_back(rows[2 + na][...].astype(F32), u, inv, consts[1][...])
        outs[1][...] = dz
        outs[2][...] = dz.astype(BF)

    return fused(mats + [up], [u2] + acts + [adapt, cot], [gain2, gain3],
                 [(t, d, BF), (t, d, F32), (t, d, BF)], body, min(256, t), dp=dp)


def back_norm(resid, lhss, mats, trans, u, inv, gain):
    t, d = resid.shape
    nl = len(lhss)

    def body(ms, rows, consts, outs, dp):
        e = rows[0][...]
        for lhs, m, tr in zip(rows[1:1 + nl], ms, trans):
            e = e + dot_mm(lhs[...], load(m), 1, 1 if tr else 0)
        dz = norm_back(e, rows[1 + nl][...], rows[2 + nl][...], consts[0][...])
        outs[0][...] = dz
        outs[1][...] = dz.astype(BF)

    return fused(mats, [resid] + lhss + [u, inv], [gain], [(t, d, F32), (t, d, BF)], body, min(256, t))


def half_rows(resid, lhss, mats, pick, dp, half):
    d = sum(line[0].shape[0] for line in mats[0])

    def body(ms, rows, consts, outs, dp):
        off = 0 if resid is None else 1
        e = rows[0][...] if off else None
        for lhs, m in zip(rows[off:], ms):
            y = dot_mm(lhs[...], load(m), 1, 1)
            e = y if e is None else e + y
        unpermute_store(outs[0], e, dp)

    return fused(mats, ([] if resid is None else [resid]) + lhss, [], [(half, d, BF)], body, half,
                 pick=pick, dp=dp, steps=1)[0]


def whole_sequences(inputs, memory, src_lengths, self_qkv, self_proj, cross_qkv, cross_proj, ffn_in, ffn_out,
                    norm_gains, prefix, adapter_down, adapter_up, cotangent):
    dp, y, z = lax.axis_index("dp"), lax.axis_index("mp"), lax.axis_index("adp")
    nz = lax.axis_size("adp")
    half, d = inputs.shape[2], inputs.shape[3]
    chunk = self_qkv.shape[1]
    flip = [(i, 1 - i) for i in range(2)]
    ring = [(i, (i + 1) % nz) for i in range(nz)]
    pc = lambda a: lax.ppermute(a, "dp", [(i, i ^ 1) for i in range(4)])
    px = lambda a: lax.ppermute(a, "dp", [(i, i ^ 2) for i in range(4)])
    py = lambda a: lax.ppermute(a, "mp", flip)
    pz = lambda a: lax.ppermute(a, "adp", ring)

    def rel(a):
        return jnp.concatenate(
            [lax.dynamic_slice_in_dim(a, (dp ^ r) * chunk, chunk, axis=a.ndim - 1) for r in range(4)], axis=-1)

    def swap_rows(a):
        own = lax.dynamic_index_in_dim(a, y, 0, keepdims=False)[0]
        got = py(lax.dynamic_index_in_dim(a, 1 - y, 0, keepdims=False)[0])
        return rel(jnp.concatenate([jnp.where(y == 0, own, got), jnp.where(y == 0, got, own)], axis=0))

    def plane(own):
        across = px(own)
        beside = py(own)
        diagonal = px(beside)
        return [[own, pc(own), across, pc(across)], [beside, pc(beside), diagonal, pc(diagonal)]]

    x_full = swap_rows(inputs)
    sq = plane(self_qkv)
    quarter_h = ffn_in.shape[1] // nz
    own_q = []
    for k in range(nz):
        at = ((z - k) % nz) * quarter_h
        fi = lax.dynamic_slice_in_dim(ffn_in, at, quarter_h, axis=1)
        fo = lax.dynamic_slice_in_dim(ffn_out, at, quarter_h, axis=0)
        own_q.append(jnp.concatenate([fi[:, :chunk], fi[:, chunk:], fo], axis=0))
    own_all = jnp.stack(own_q)
    sib_all = pc(own_all)
    fx = px(own_q[0])
    fy = py(own_q[0])
    fd = px(fy)
    ad = jnp.concatenate([adapter_down.T, adapter_up], axis=0)
    hops = [jnp.concatenate([fx, fy, fd, ad], axis=0)]
    for k in range(1, nz):
        hops.append(pz(hops[-1]))
    hops_sib = [pc(h) for h in hops]
    qrows = own_q[0].shape[0]
    adapters = jnp.stack([h[3 * qrows:] for h in hops])
    adapters_x = px(adapters)
    adapters_sib = pc(jnp.stack([adapters, adapters_x]))
    pre_own = jnp.pad(prefix, ((0, 0), (0, PRE - PREFIX_LEN), (0, 0)))
    pre = [pre_own, py(pre_own)]
    mem_full = swap_rows(memory)
    so = plane(self_proj)
    cq = plane(cross_qkv)
    co = plane(cross_proj)
    cot_full = swap_rows(cotangent)

    def in_block(k):
        def part(p):
            return [p[:chunk], p[chunk:2 * chunk], p[2 * chunk:]]
        h, hs = hops[k], hops_sib[k]
        cut = lambda a, i: part(a[i * qrows:(i + 1) * qrows])
        s0 = [part(own_all[k]), part(sib_all[k]), cut(h, 0), cut(hs, 0)]
        s1 = [cut(h, 1), cut(hs, 1), cut(h, 2), cut(hs, 2)]
        w_in = [[s0[r][0], s0[r][1], s1[r][0], s1[r][1]] for r in range(4)]
        w_out = [[s[r][2] for r in range(4)] for s in (s0, s1)]
        return w_in, w_out

    gains = rel(norm_gains.astype(F32))
    gain = [gains[i:i + 1] for i in range(3)]
    pad_n = jnp.full((1,), PREFIX_LEN, jnp.int32)
    src_n = lax.dynamic_index_in_dim(src_lengths, y, 0, keepdims=False).reshape(1)
    qscale = HEAD_DIM ** -0.5 * LOG2E
    w_of = lambda pieces, s, c: [[pieces[s][r][c]] for r in range(4)]

    self_kept, attn_self = [], []
    for s in range(2):
        q, k, v = project(x_full, [w_of(sq, s, c) for c in range(3)], (qscale, 1.0, 1.0))
        a, p, pp, il = attn_fwd(pad_n, q, k, v, pre[s][0], pre[s][1].T)
        self_kept.append((q, k, v, a, il, p, pp))
        attn_self.append(a)
    so_s = [[[so[s][r] for r in range(4)]] for s in range(2)]
    u1, inv1, h1b = add_norm(x_full, None, attn_self, so_s, gain[0])
    cross_w = lambda c: [[cq[s][r][c] for s in range(2)] for r in range(4)]
    (qc,) = project(h1b, [cross_w(0)], (qscale,))
    kc, vc = project(mem_full, [cross_w(1), cross_w(2)], (1.0, 1.0))
    ac, p_c, pp_c, il_c = attn_fwd(src_n, qc, kc, vc)
    co_w = [[co[s][r] for r in range(4)] for s in range(2)]
    u2, inv2, h2b = add_norm(u1, gain[0], [ac], [co_w], gain[1])
    w_in, w_out = zip(*[in_block(k) for k in range(nz)])
    rows_a = adapter_up.shape[0]
    pieces_a = [adapters, adapters_sib[0], adapters_x, adapters_sib[1]]
    down_t = [[pieces_a[r][k][:rows_a] for r in range(4)] for k in range(nz)]
    up_w = [[pieces_a[r][k][rows_a:] for r in range(4)] for k in range(nz)]
    acts, slopes = [], []
    for k in range(nz):
        act, slope = hidden_forward(h2b, w_in[k], False)
        acts.append(act)
        slopes.append(slope)
    act_a, slope_a = hidden_forward(h2b, down_t, True)
    res, dz3, b3 = last_norm(u2, gain[1], acts, list(w_out), act_a, up_w, gain[2], cot_full, dp)

    def hand_back(full):
        mine = lax.dynamic_slice_in_dim(full, y * half, half, axis=0)
        theirs = py(lax.dynamic_slice_in_dim(full, (1 - y) * half, half, axis=0))
        return join(mine, theirs)

    def join(mine, theirs):
        return jnp.stack([jnp.where(y == 0, mine, theirs), jnp.where(y == 0, theirs, mine)])[:, None]

    result = hand_back(res)

    dga = hidden_backward(b3, up_w, slope_a, 4.0)
    tn = lambda a, b: dot_mm(a, b, 0, 0)
    up_term = tn(act_a, b3) * 4.0
    down_term = tn(h2b, dga)
    order_z = lambda a, axis: jnp.concatenate(
        [lax.dynamic_slice_in_dim(a, ((z - j) % nz) * rows_a, rows_a, axis=axis) for j in range(nz)], axis=axis)
    down_abs = rel(order_z(down_term, 1).T)
    up_abs = rel(order_z(up_term, 0))
    both = jnp.stack([down_abs, up_abs])
    both = lax.psum_scatter(both, "adp", scatter_dimension=1, tiled=True)
    both = lax.psum_scatter(both, ("dp", "mp"), scatter_dimension=2, tiled=True)
    down_grad, up_grad = both[0].T, both[1]
    dgs = [hidden_backward(b3, w_out[k], slopes[k], 1.0) for k in range(nz)]
    dz2, dz2b = back_norm(dz3, dgs + [dga], list(w_in) + [down_t], [True] * nz + [False], u2, inv2, gain[1])
    (dac,) = project_back(dz2b, [co_w])
    dqc, dkc, dvc, _, _ = attn_bwd(qc, kc, vc, ac, dac, il_c, p_c, pp_c)
    mem_mats = [cross_w(1), cross_w(2)]
    mem_send = half_rows(None, [dkc, dvc], mem_mats, 1 - y, dp, half)
    mem_mine = half_rows(None, [dkc, dvc], mem_mats, y, dp, half)
    memory_grad = join(mem_mine, py(mem_send))
    dz1, dz1b = back_norm(dz2, [dqc], [cross_w(0)], [True], u1, inv1, gain[0])
    das = project_back(dz1b, [[[so[s][r] for r in range(4)]] for s in range(2)])
    lhss, mats, pre_terms = [], [], []
    for s in range(2):
        q, k, v, a, il, p, pp = self_kept[s]
        dq, dk, dv, dpk, dpv = attn_bwd(q, k, v, a, das[s], il, p, pp, pre[s][0], pre[s][1])
        lhss += [dq, dk, dv]
        mats += [w_of(sq, s, c) for c in range(3)]
        pre_terms.append(jnp.stack([dpk.T, dpv.T])[:, :PREFIX_LEN])
    prefix_grad = lax.psum(pre_terms[0] + py(pre_terms[1]), ("dp", "adp"))
    in_send = half_rows(dz1, lhss, mats, 1 - y, dp, half)
    in_mine = half_rows(dz1, lhss, mats, y, dp, half)
    input_grad = join(in_mine, py(in_send))
    return result, input_grad, memory_grad, prefix_grad, down_grad, up_grad


def solution(mesh):
    by_sequence = mesh.shape["mp"] == MICRO and mesh.shape["dp"] == 4
    return jax.shard_map(
        whole_sequences if by_sequence else shards,
        mesh=mesh,
        in_specs=(
            P(None, ("dp", "adp"), "mp", None),
            P(None, ("dp", "adp"), "mp", None),
            P(None, ("dp", "adp"), None),
            P(None, "dp", "mp"),
            P("mp", "dp"),
            P(None, "dp", "mp"),
            P("mp", "dp"),
            P("dp", "mp"),
            P("mp", "dp"),
            P(),
            P(None, None, "mp"),
            P("dp", "adp"),
            P("adp", "dp"),
            P(None, ("dp", "adp"), "mp", None),
        ),
        out_specs=(
            P(None, ("dp", "adp"), "mp", None),
            P(None, ("dp", "adp"), "mp", None),
            P(None, ("dp", "adp"), "mp", None),
            P(None, None, "mp"),
            P(("dp", "mp"), "adp"),
            P("adp", ("dp", "mp")),
        ),
        check_vma=False,
    )
```

```python
import functools
import math

import jax
import jax.numpy as jnp
from jax import lax
from jax.experimental import pallas as pl
from jax.experimental.pallas import tpu as pltpu
from jax.sharding import PartitionSpec as P

HEAD_DIM = 64
PREFIX_LEN = 30
SEQ_LEN = 1024
SRC_MAX = 1024
SEQS_BLK = 1
MICRO = 2


eps = 1e-05


def exact_gelu(values):
    return jax.nn.gelu(values, approximate=False)


def norm_forward(residual, gain_row):
    centered = residual - jnp.mean(residual, axis=-1, keepdims=True)
    inv_std = lax.rsqrt(jnp.mean(centered * centered, axis=-1, keepdims=True) + eps)
    return centered * inv_std * gain_row


def norm_backward(upstream, residual, gain_row):
    centered = residual - jnp.mean(residual, axis=-1, keepdims=True)
    inv_std = lax.rsqrt(jnp.mean(centered * centered, axis=-1, keepdims=True) + eps)
    normed = centered * inv_std
    scaled = upstream * gain_row
    inner_mean = jnp.mean(scaled * normed, axis=-1, keepdims=True)
    return inv_std * (scaled - jnp.mean(scaled, axis=-1, keepdims=True) - normed * inner_mean)


def gelu_back(pre_act, upstream):
    return jax.vjp(exact_gelu, pre_act)[1](upstream)[0]


def matmul(left_mat, right_mat):
    return jnp.dot(left_mat, right_mat, preferred_element_type=jnp.float32)


def matmul_nt(left_mat, right_mat):
    return lax.dot_general(
        left_mat, right_mat, (((1,), (1,)), ((), ())), preferred_element_type=jnp.float32
    )


def matmul_tn(left_mat, right_mat):
    return lax.dot_general(
        left_mat, right_mat, (((0,), (0,)), ((), ())), preferred_element_type=jnp.float32
    )


def to_heads(rows_mat, seq_count, length):
    heads_here = rows_mat.shape[-1] // HEAD_DIM
    return rows_mat.reshape(seq_count, length, heads_here, HEAD_DIM).transpose(0, 2, 1, 3)


def from_heads(split_mat):
    seq_count, heads_here, length, head_width = split_mat.shape
    return split_mat.transpose(0, 2, 1, 3).reshape(seq_count * length, heads_here * head_width)


def causal_allowed():
    query_pos = lax.broadcasted_iota(jnp.int32, (SEQ_LEN, PREFIX_LEN + SEQ_LEN), 0)
    key_pos = lax.broadcasted_iota(jnp.int32, (SEQ_LEN, PREFIX_LEN + SEQ_LEN), 1)
    return (key_pos < PREFIX_LEN) | (key_pos - PREFIX_LEN <= query_pos)


def source_allowed(length):
    return lax.broadcasted_iota(jnp.int32, (SEQ_LEN, SRC_MAX), 1) < length


def attend_forward(queries, keys_all, values_all, allowed):
    scores = jnp.einsum("hqd,hkd->hqk", queries, keys_all, preferred_element_type=jnp.float32)
    scores = jnp.where(allowed, scores, -1e30)
    top_score = jnp.max(scores, axis=-1, keepdims=True)
    expo_scores = jnp.exp(scores - top_score)
    row_total = jnp.sum(expo_scores, axis=-1, keepdims=True)
    weights_low = (expo_scores / row_total).astype(jnp.bfloat16)
    mixed = jnp.einsum("hqk,hkd->hqd", weights_low, values_all, preferred_element_type=jnp.float32)
    return (mixed.astype(jnp.bfloat16), top_score + jnp.log(row_total))


def attend_backward(queries, keys_all, values_all, allowed, log_total, grad_out):
    scores = jnp.einsum("hqd,hkd->hqk", queries, keys_all, preferred_element_type=jnp.float32)
    scores = jnp.where(allowed, scores, -1e30)
    soft_weights = jnp.exp(scores - log_total)
    grad_soft = jnp.einsum("hqd,hkd->hqk", grad_out, values_all, preferred_element_type=jnp.float32)
    inner_sum = jnp.sum(soft_weights * grad_soft, axis=-1, keepdims=True)
    grad_scores = (soft_weights * (grad_soft - inner_sum)).astype(jnp.bfloat16)
    grad_query = jnp.einsum(
        "hqk,hkd->hqd", grad_scores, keys_all, preferred_element_type=jnp.float32
    )
    grad_keys = jnp.einsum("hqk,hqd->hkd", grad_scores, queries, preferred_element_type=jnp.float32)
    grad_values = jnp.einsum(
        "hqk,hqd->hkd",
        soft_weights.astype(jnp.bfloat16),
        grad_out,
        preferred_element_type=jnp.float32,
    )
    return (grad_query, grad_keys, grad_values)


def gather_rows(rows_low):
    return lax.all_gather(rows_low, "mp", axis=0, tiled=True)


def reduce_rows(term_fn, own_count):
    return lax.psum_scatter(
        term_fn(jnp.int32(0), own_count * lax.axis_size("mp")).astype(jnp.bfloat16),
        "mp",
        scatter_dimension=0,
        tiled=True,
    ).astype(jnp.float32)


def gather_adapter(rows_low):
    return lax.all_gather(rows_low, "adp", axis=0, tiled=True)


def reduce_adapter(term_fn, own_count):
    return lax.psum_scatter(
        term_fn(jnp.int32(0), own_count * lax.axis_size("adp")).astype(jnp.bfloat16),
        "adp",
        scatter_dimension=0,
        tiled=True,
    ).astype(jnp.float32)


def reduce_prefix(grad_prefix):
    return lax.psum(grad_prefix, ("dp", "adp"))


def reduce_adapter_grads(grad_down, grad_up):
    return (
        lax.psum_scatter(grad_down, ("dp", "mp"), scatter_dimension=0, tiled=True),
        lax.psum_scatter(grad_up, ("dp", "mp"), scatter_dimension=1, tiled=True),
    )


def shards(
    inputs,
    memory,
    src_lengths,
    self_qkv,
    self_proj,
    cross_qkv,
    cross_proj,
    ffn_in,
    ffn_out,
    norm_gains,
    prefix,
    adapter_down,
    adapter_up,
    cotangent,
):
    scale = HEAD_DIM ** (-0.5)
    own_rows = inputs.shape[2]
    gains = norm_gains.astype(jnp.float32)
    causal = causal_allowed()
    prefix_heads = to_heads(prefix, 2, PREFIX_LEN)
    prefix_keys = prefix_heads[0]
    prefix_values = prefix_heads[1]
    results = []
    input_grads = []
    memory_grads = []
    prefix_acc = None
    down_acc = None
    up_acc = None
    for micro_index in range(MICRO):
        self_w, self_o, cross_w, cross_o, down_w, up_w = (
            lax.all_gather(self_qkv, "dp", axis=1, tiled=True),
            lax.all_gather(self_proj, "dp", axis=1, tiled=True),
            lax.all_gather(cross_qkv, "dp", axis=1, tiled=True),
            lax.all_gather(cross_proj, "dp", axis=1, tiled=True),
            lax.all_gather(adapter_down, "dp", axis=0, tiled=True),
            lax.all_gather(adapter_up, "dp", axis=1, tiled=True),
        )
        ffn_first, ffn_second = (
            lax.all_gather(ffn_in, "dp", axis=0, tiled=True),
            lax.all_gather(ffn_out, "dp", axis=1, tiled=True),
        )
        x_rows = inputs[micro_index, 0]
        lengths_here = src_lengths[micro_index, 0]
        x_full = gather_rows(x_rows)
        mem_full = lax.all_gather(memory[micro_index, 0], "mp", axis=0, tiled=True)
        projected = jnp.einsum("td,cde->cte", x_full, self_w, preferred_element_type=jnp.float32)
        query_self = to_heads((projected[0] * scale).astype(jnp.bfloat16), SEQS_BLK, SEQ_LEN)
        key_self = to_heads(projected[1].astype(jnp.bfloat16), SEQS_BLK, SEQ_LEN)
        value_self = to_heads(projected[2].astype(jnp.bfloat16), SEQS_BLK, SEQ_LEN)

        def self_forward(packed):
            query_seq, key_seq, value_seq = packed
            keys_all = jnp.concatenate([prefix_keys, key_seq], axis=1)
            values_all = jnp.concatenate([prefix_values, value_seq], axis=1)
            return attend_forward(query_seq, keys_all, values_all, causal)

        attn_self, lse_self = lax.map(self_forward, (query_self, key_self, value_self))
        attn_rows = from_heads(attn_self)

        def self_term(first_row, row_count):
            return matmul(attn_rows, self_o)

        resid_one = x_rows.astype(jnp.float32) + reduce_rows(self_term, own_rows)
        normed_one = norm_forward(resid_one, gains[0])
        one_full = gather_rows(normed_one.astype(jnp.bfloat16))
        cross_query = to_heads(
            (matmul(one_full, cross_w[0]) * scale).astype(jnp.bfloat16), SEQS_BLK, SEQ_LEN
        )
        memory_proj = jnp.einsum(
            "td,cde->cte", mem_full, cross_w[1:], preferred_element_type=jnp.float32
        )
        cross_keys = to_heads(memory_proj[0].astype(jnp.bfloat16), SEQS_BLK, SRC_MAX)
        cross_values = to_heads(memory_proj[1].astype(jnp.bfloat16), SEQS_BLK, SRC_MAX)

        def cross_forward(packed):
            query_seq, key_seq, value_seq, length = packed
            return attend_forward(query_seq, key_seq, value_seq, source_allowed(length))

        attn_cross, lse_cross = lax.map(
            cross_forward, (cross_query, cross_keys, cross_values, lengths_here)
        )
        cross_rows = from_heads(attn_cross)

        def cross_term(first_row, row_count):
            return matmul(cross_rows, cross_o)

        resid_two = normed_one + reduce_rows(cross_term, own_rows)
        normed_two = norm_forward(resid_two, gains[1])
        two_low = normed_two.astype(jnp.bfloat16)
        two_full = gather_rows(two_low)
        hidden_pre = matmul(two_full, ffn_first)
        hidden_act = exact_gelu(hidden_pre).astype(jnp.bfloat16)

        def ffn_term(first_row, row_count):
            return matmul(hidden_act, ffn_second)

        ffn_rows = reduce_rows(ffn_term, own_rows)
        adapter_in = gather_adapter(two_low)
        adapter_pre = matmul(adapter_in, down_w)
        adapter_act = exact_gelu(adapter_pre).astype(jnp.bfloat16)

        def adapter_term(first_row, row_count):
            return matmul(adapter_act, up_w)

        adapter_rows = reduce_adapter(adapter_term, own_rows)
        resid_three = normed_two + ffn_rows + 4.0 * adapter_rows
        results.append(norm_forward(resid_three, gains[2]).astype(jnp.bfloat16))
        grad_three = norm_backward(
            cotangent[micro_index, 0].astype(jnp.float32), resid_three, gains[2]
        )
        grad_branch = grad_three.astype(jnp.bfloat16)
        grad_adapter = gather_adapter(grad_branch) * 4.0
        up_term = matmul_tn(adapter_act, grad_adapter)
        grad_adapter_pre = gelu_back(adapter_pre, matmul_nt(grad_adapter, up_w)).astype(
            jnp.bfloat16
        )
        down_term = matmul_tn(adapter_in, grad_adapter_pre)

        def adapter_back_term(first_row, row_count):
            return matmul_nt(grad_adapter_pre, down_w)

        adapter_back = reduce_adapter(adapter_back_term, own_rows)
        branch_full = gather_rows(grad_branch)
        grad_pre = gelu_back(hidden_pre, matmul_nt(branch_full, ffn_second)).astype(jnp.bfloat16)

        def ffn_back_term(first_row, row_count):
            return matmul_nt(grad_pre, ffn_first)

        ffn_back = reduce_rows(ffn_back_term, own_rows)
        grad_mid = norm_backward(grad_three + ffn_back + adapter_back, resid_two, gains[1])
        mid_full = gather_rows(grad_mid.astype(jnp.bfloat16))
        grad_cross_out = to_heads(
            matmul_nt(mid_full, cross_o).astype(jnp.bfloat16), SEQS_BLK, SEQ_LEN
        )

        def cross_backward(packed):
            query_seq, key_seq, value_seq, lse_seq, grad_seq, length = packed
            return attend_backward(
                query_seq, key_seq, value_seq, source_allowed(length), lse_seq, grad_seq
            )

        cross_gq, cross_gk, cross_gv = lax.map(
            cross_backward,
            (cross_query, cross_keys, cross_values, lse_cross, grad_cross_out, lengths_here),
        )
        cross_gq_rows = from_heads(cross_gq).astype(jnp.bfloat16) * scale

        def cross_query_term(first_row, row_count):
            return matmul_nt(cross_gq_rows, cross_w[0])

        grad_one = grad_mid + reduce_rows(cross_query_term, own_rows)
        memory_stack = jnp.stack(
            [from_heads(cross_gk).astype(jnp.bfloat16), from_heads(cross_gv).astype(jnp.bfloat16)]
        )
        memory_grads.append(
            lax.psum_scatter(
                jnp.einsum(
                    "cte,cde->td", memory_stack, cross_w[1:], preferred_element_type=jnp.float32
                ).astype(jnp.bfloat16),
                "mp",
                scatter_dimension=0,
                tiled=True,
            )
        )
        grad_first = norm_backward(grad_one, resid_one, gains[0])
        first_full = gather_rows(grad_first.astype(jnp.bfloat16))
        grad_self_out = to_heads(
            matmul_nt(first_full, self_o).astype(jnp.bfloat16), SEQS_BLK, SEQ_LEN
        )

        def self_backward(packed):
            query_seq, key_seq, value_seq, lse_seq, grad_seq = packed
            keys_all = jnp.concatenate([prefix_keys, key_seq], axis=1)
            values_all = jnp.concatenate([prefix_values, value_seq], axis=1)
            return attend_backward(query_seq, keys_all, values_all, causal, lse_seq, grad_seq)

        self_gq, self_gk, self_gv = lax.map(
            self_backward, (query_self, key_self, value_self, lse_self, grad_self_out)
        )
        prefix_key_grad = from_heads(jnp.sum(self_gk[:, :, :PREFIX_LEN], axis=0)[None])
        prefix_value_grad = from_heads(jnp.sum(self_gv[:, :, :PREFIX_LEN], axis=0)[None])
        prefix_term = jnp.stack([prefix_key_grad, prefix_value_grad])
        self_stack = jnp.stack(
            [
                from_heads(self_gq).astype(jnp.bfloat16) * scale,
                from_heads(self_gk[:, :, PREFIX_LEN:]).astype(jnp.bfloat16),
                from_heads(self_gv[:, :, PREFIX_LEN:]).astype(jnp.bfloat16),
            ]
        )

        def input_term(first_row, row_count):
            return jnp.einsum("cte,cde->td", self_stack, self_w, preferred_element_type=jnp.float32)

        input_grads.append((grad_first + reduce_rows(input_term, own_rows)).astype(jnp.bfloat16))
        prefix_term = reduce_prefix(prefix_term)
        down_term, up_term = reduce_adapter_grads(down_term, up_term)
        prefix_acc = prefix_term if prefix_acc is None else prefix_acc + prefix_term
        down_acc = down_term if down_acc is None else down_acc + down_term
        up_acc = up_term if up_acc is None else up_acc + up_term
    return (
        jnp.stack(results)[:, None],
        jnp.stack(input_grads)[:, None],
        jnp.stack(memory_grads)[:, None],
        prefix_acc,
        down_acc,
        up_acc,
    )


F32 = jnp.float32
BF = jnp.bfloat16
EPS = 1e-05
LOG2E = 1.4426950408889634
TILE = 256
FEED_SPLIT = 2

BQF = 512
BQ = 512
PRE = 32
VMEM_BYTES = 60 * 2**20
NEG = -1e30
HBM = pl.BlockSpec(memory_space=pl.ANY)
LN2 = 0.6931471805599453


def dot_mm(a, b, ca, cb):
    return lax.dot_general(a, b, (((ca,), (cb,)), ((), ())), preferred_element_type=jnp.float32)


def pick_head(h, mat):
    rows = lax.broadcasted_iota(jnp.int32, mat.shape, 0)
    return jnp.where((rows // HEAD_DIM) == h, mat, jnp.zeros_like(mat))


def attend_pair(causal, n, q, k, v, pk, pv, p_ref, pp_ref):
    t = q.shape[0]
    s = k.shape[0]
    nb = t // BQF
    qt = q.T
    vt = v.T
    ones = jnp.ones((16, s), jnp.bfloat16)
    work = [(h, j) for h in range(2) for j in range(nb)]

    def scores(h, j):
        kk = (j + 1) * BQF if causal else s
        qb = pick_head(h, qt[:, j * BQF:(j + 1) * BQF])
        return dot_mm(k[:kk], qb, 1, 0), dot_mm(pk, qb, 1, 0) if causal else None

    res = {}
    ahead = scores(*work[0])
    for w, (h, j) in enumerate(work):
        st, sp = ahead
        if w + 1 < len(work):
            ahead = scores(*work[w + 1])
        kk = st.shape[0]
        js = slice(j * BQF, (j + 1) * BQF)
        if causal:
            krow = lax.broadcasted_iota(jnp.int32, (BQF, BQF), 0)
            qcol = lax.broadcasted_iota(jnp.int32, (BQF, BQF), 1)
            diag = jnp.where(krow <= qcol, st[kk - BQF:], NEG)
            st = jnp.concatenate([st[:kk - BQF], diag], axis=0) if kk > BQF else diag
            prow = lax.broadcasted_iota(jnp.int32, sp.shape, 0)
            sp = jnp.where(prow < n, sp, NEG)
            m = jnp.maximum(jnp.max(st, axis=0, keepdims=True), jnp.max(sp, axis=0, keepdims=True))
            pp = jnp.exp2(sp - m).astype(jnp.bfloat16)
            pp_ref[h, :, js] = pp
        else:
            krow = lax.broadcasted_iota(jnp.int32, st.shape, 0)
            st = jnp.where(krow < n, st, NEG)
            m = jnp.max(st, axis=0, keepdims=True)
        p = jnp.exp2(st - m).astype(jnp.bfloat16)
        p_ref[h, :kk, js] = p
        hs = slice(h * HEAD_DIM, (h + 1) * HEAD_DIM)
        ot = dot_mm(jnp.concatenate([vt[hs, :kk], ones[:, :kk]], axis=0), p, 1, 0)
        if causal:
            ot += dot_mm(jnp.concatenate([pv.T[hs], ones[:, :PRE]], axis=0), pp, 1, 0)
        il = 1.0 / ot[HEAD_DIM:HEAD_DIM + 1]
        res[h, j] = (ot[:HEAD_DIM] * il, il)
    ils = [jnp.concatenate([res[h, j][1] for j in range(nb)], axis=1) for h in range(2)]
    at = jnp.concatenate([jnp.concatenate([res[h, j][0] for j in range(nb)], axis=1) for h in range(2)], axis=0)
    return at.astype(jnp.bfloat16).T, jnp.concatenate(ils, axis=0)


def sum_terms(keep_hbm, give_hbm, down_ref, up_ref, keep, part, first, second, third, fourth, out2, out3, out4, near, send, recv):
    g = pl.program_id(0)
    last = pl.num_programs(0) - 1
    dp, y, z, side, over, up = axes_here()
    nz = lax.axis_size("adp")
    rows = part.shape[1] // nz
    wide = out3.shape[2]

    def far(src, dst, peer, i):
        return pltpu.make_async_remote_copy(src_ref=src, dst_ref=dst, send_sem=send.at[i], recv_sem=recv.at[i],
                                            device_id=peer, device_id_type=pl.DeviceIdType.MESH)

    load = pltpu.make_async_copy(keep_hbm, keep, near.at[0])
    core = far(give_hbm, first, side, 0)
    across = far(out2, second, over, 1)
    beside = far(out3, third, up, 2)
    along = [far(out4.at[k - 1], fourth.at[k - 1], {"adp": lax.rem(z + nz - k, nz)}, 2 + k) for k in range(1, nz)]

    @pl.when(g == 0)
    def _():
        meet([side, over, up] + [{"adp": lax.rem(z + k, nz)} for k in range(1, nz)])
        load.start()
        core.start()

    @pl.when(g == 1)
    def _():
        load.wait()
        core.wait_recv()
        out2[...] = (keep[:, 1] + first[:, 1].astype(jnp.float32)).astype(jnp.bfloat16)
        across.start()

    @pl.when(g == last // 2 + 1)
    def _():
        across.wait_recv()
        keep[:, 0] = keep[:, 0] + first[:, 0].astype(jnp.float32) + second[...].astype(jnp.float32)
        mine = pl.ds(pl.multiple_of(y * wide, wide), wide)
        other = pl.ds(pl.multiple_of((1 - y) * wide, wide), wide)
        out3[...] = keep[:, 0, :, other].astype(jnp.bfloat16)
        part[...] = keep[:, 0, :, mine]
        beside.start()

    @pl.when(g == last - 1)
    def _():
        beside.wait_recv()
        part[...] = part[...] + third[...].astype(jnp.float32)
        for k in range(1, nz):
            out4[k - 1] = part[:, k * rows:(k + 1) * rows].astype(jnp.bfloat16)
            along[k - 1].start()

    @pl.when(g == last)
    def _():
        total = part[:, :rows]
        for k in range(1, nz):
            along[k - 1].wait_recv()
            total = total + fourth[k - 1].astype(jnp.float32)
        down_ref[...] = total[0].T
        up_ref[...] = total[1]
        for c in [core, across, beside] + along:
            c.wait_send()


def attn_bwd_body(causal, q_ref, k_ref, v_ref, a_ref, da_ref, l_ref, p_ref, *rest):
    if causal:
        pp_ref, pre_ref, moved, _, dq_ref, dk_ref, dv_ref, dpre_ref, landed, sems = rest
        y = lax.axis_index("mp")
        carry = pltpu.make_async_remote_copy(
            src_ref=moved, dst_ref=landed.at[y], send_sem=sems.at[0], recv_sem=sems.at[1],
            device_id={"mp": 1 - y}, device_id_type=pl.DeviceIdType.MESH)

        @pl.when(pl.program_id(0) == 0)
        def _():
            meet([{"mp": 1 - y}])
            carry.start()
    else:
        pp_ref, pre_ref, dpre_ref = None, None, None
        keep_ref, give_ref, dq_ref, dk_ref, dv_ref, down_ref, up_ref = rest[:7]
        sum_terms(keep_ref, give_ref, down_ref, up_ref, *rest[7:])
    t = q_ref.shape[0]
    s = k_ref.shape[0]
    nb = t // BQ
    qt = q_ref[...].T
    kt = k_ref[...].T
    dat = da_ref[...].T.astype(jnp.float32)
    prod = dat * a_ref[...].T.astype(jnp.float32)
    pkt = pre_ref[0].T if causal else None
    work = [(h, j) for h in range(2) for j in range(nb)]
    head = {}
    for h in range(2):
        hs = slice(h * HEAD_DIM, (h + 1) * HEAD_DIM)
        il = l_ref[0, h:h + 1]
        head[h] = ((dat * il).astype(jnp.bfloat16), jnp.sum(prod[hs], axis=0, keepdims=True) * il)

    def soft_grad(h, j):
        js = slice(j * BQ, (j + 1) * BQ)
        kk = (j + 1) * BQ if causal else s
        dab = pick_head(h, head[h][0][:, js])
        return dot_mm(v_ref[:kk], dab, 1, 0), dot_mm(pre_ref[1], dab, 1, 0) if causal else None

    def add(tot, new):
        return new if tot is None else tot + new

    res = {}
    dpk = [None, None]
    dpv = [None, None]
    dkb = [[None] * nb, [None] * nb]
    dvb = [[None] * nb, [None] * nb]
    ahead = soft_grad(*work[0])
    for w, (h, j) in enumerate(work):
        dp, dpp = ahead
        if w + 1 < len(work):
            ahead = soft_grad(*work[w + 1])
        hs = slice(h * HEAD_DIM, (h + 1) * HEAD_DIM)
        js = slice(j * BQ, (j + 1) * BQ)
        kk = dp.shape[0]
        dl = head[h][1][:, js]
        dah = head[h][0][hs, js]
        p = p_ref[h, :kk, js]
        ds = (p.astype(jnp.float32) * (dp - dl)).astype(jnp.bfloat16)
        dq = dot_mm(kt[hs, :kk], ds, 1, 0)
        if causal:
            pp = pp_ref[h, :, js]
            dsp = (pp.astype(jnp.float32) * (dpp - dl)).astype(jnp.bfloat16)
            dq += dot_mm(pkt[hs], dsp, 1, 0)
            dpk[h] = add(dpk[h], dot_mm(qt[hs, js], dsp, 1, 1))
            dpv[h] = add(dpv[h], dot_mm(dah, pp, 1, 1))
        res[h, j] = dq
        dv = dot_mm(dah, p, 1, 1)
        dk = dot_mm(qt[hs, js], ds, 1, 1)
        if causal:
            for i in range(kk // BQ):
                dvb[h][i] = add(dvb[h][i], dv[:, i * BQ:(i + 1) * BQ])
                dkb[h][i] = add(dkb[h][i], dk[:, i * BQ:(i + 1) * BQ])
        else:
            dvb[h] = [add(dvb[h][0], dv)]
            dkb[h] = [add(dkb[h][0], dk)]
    both = lambda f: jnp.concatenate([f(0), f(1)], axis=0)
    dq_ref[...] = (both(lambda h: jnp.concatenate([res[h, j] for j in range(nb)], axis=1))
                   * HEAD_DIM ** -0.5).astype(jnp.bfloat16).T
    dk_ref[...] = (both(lambda h: jnp.concatenate(dkb[h], axis=1)) * LN2).astype(jnp.bfloat16).T
    dv_ref[...] = both(lambda h: jnp.concatenate(dvb[h], axis=1)).astype(jnp.bfloat16).T
    if causal:
        dpre_ref[0] = both(lambda h: dpk[h]).T * LN2
        dpre_ref[1] = both(lambda h: dpv[h]).T

        @pl.when(pl.program_id(0) == pl.num_programs(0) - 1)
        def _():
            carry.wait()


def attn_bwd(q, k, v, a, da, il, p, pp=None, pre=None, moved=None, landed=None, keep=None, give=None):
    t, w = q.shape
    s = k.shape[0]
    pairs = w // 128
    causal = pre is not None
    col = lambda g: (0, g)
    lead = lambda g: (g, 0, 0)
    tail = lambda g: (0, 0, g)
    fixed = lambda g: (0, 0)
    f32, bf = jnp.float32, jnp.bfloat16
    vm = pltpu.VMEM
    if not causal:
        nz = lax.axis_size("adp")
        bott = keep.shape[2]
        rows, wide = bott // nz, TILE // 2
    return pl.pallas_call(
        functools.partial(attn_bwd_body, causal),
        grid=(pairs,),
        in_specs=[
            pl.BlockSpec((t, 128), col), pl.BlockSpec((s, 128), col), pl.BlockSpec((s, 128), col),
            pl.BlockSpec((t, 128), col), pl.BlockSpec((t, 128), col),
            pl.BlockSpec((1, 2, t), lead), pl.BlockSpec((2, s, t), lead),
        ] + ([pl.BlockSpec((2, PRE, t), lead), pl.BlockSpec((2, PRE, 128), tail), HBM, HBM] if causal else [HBM, HBM]),
        out_specs=[
            pl.BlockSpec((t, 128), col), pl.BlockSpec((s, 128), col), pl.BlockSpec((s, 128), col),
        ] + ([pl.BlockSpec((2, PRE, 128), tail), HBM] if causal else [pl.BlockSpec((rows, wide), fixed)] * 2),
        out_shape=[
            jax.ShapeDtypeStruct((t, w), bf), jax.ShapeDtypeStruct((s, w), bf), jax.ShapeDtypeStruct((s, w), bf),
        ] + ([jax.ShapeDtypeStruct((2, PRE, w), f32), jax.ShapeDtypeStruct(landed.shape, bf)] if causal
           else [jax.ShapeDtypeStruct((rows, wide), f32)] * 2),
        scratch_shapes=[pltpu.SemaphoreType.DMA((2,))] if causal else [
            vm(keep.shape, f32), vm((2, bott, wide), f32), vm(keep.shape, bf), vm((2, bott, TILE), bf), vm((2, bott, wide), bf),
            vm((nz - 1, 2, rows, wide), bf), vm((2, bott, TILE), bf), vm((2, bott, wide), bf), vm((nz - 1, 2, rows, wide), bf),
            pltpu.SemaphoreType.DMA((1,)), pltpu.SemaphoreType.DMA((nz + 2,)), pltpu.SemaphoreType.DMA((nz + 2,))],
        input_output_aliases={10: 4} if causal else {},
        compiler_params=pltpu.CompilerParams(
            vmem_limit_bytes=VMEM_BYTES, collective_id=3 if causal else 5, has_side_effects=True),
        cost_estimate=pl.CostEstimate(flops=40 * t * s * w, bytes_accessed=4 * t * s * pairs, transcendentals=0),
    )(q, k, v, a, da, il, p, *((pp, pre, moved, landed) if causal else (keep, give)))


def erf_parts(v):
    mag = jnp.abs(v)
    expo = jnp.exp2(v * v * (-0.5 * LOG2E))
    t = 1.0 / (1.0 + (0.3275911 * 0.5 ** 0.5) * mag)
    poly = t * (0.254829592 + t * (-0.284496736 + t * (1.421413741 + t * (-1.453152027 + t * 1.061405429))))
    half = 0.5 * poly * expo
    return jnp.where(v < 0.0, half, 1.0 - half), expo * (2.0 * math.pi) ** -0.5


def gelu_pair(v):
    cdf, pdf = erf_parts(v)
    return v * cdf, cdf + v * pdf


def normalize(z):
    centered = z - jnp.mean(z, axis=-1, keepdims=True)
    inv = lax.rsqrt(jnp.mean(centered * centered, axis=-1, keepdims=True) + EPS)
    return centered * inv, inv


def norm_back(e, u, inv, gain):
    w = e * gain
    return inv * (w - jnp.mean(w, axis=-1, keepdims=True) - u * jnp.mean(w * u, axis=-1, keepdims=True))


def stack_rows(refs):
    return jnp.concatenate([r[...] for r in refs], axis=0)


def stack_cols(refs):
    return jnp.concatenate([r[...] for r in refs], axis=1)


def nn(lhs, tiles):
    return dot_mm(lhs, stack_rows(tiles), 1, 0)


def nt(lhs, tiles):
    return dot_mm(lhs, stack_cols(tiles), 1, 1)


def place_cols(value_ref, dp):
    n = value_ref.shape[1] // TILE
    return jnp.concatenate(
        [value_ref[:, pl.ds(pl.multiple_of((dp ^ r) * TILE, TILE), TILE)] for r in range(n)], axis=1)


def unplace_store(out, value, dp):
    for r in range(value.shape[1] // TILE):
        out[:, pl.ds(pl.multiple_of((dp ^ r) * TILE, TILE), TILE)] = (
            value[:, r * TILE:(r + 1) * TILE].astype(out.dtype))


class Exchange:
    def __init__(self, buf, out, local, send, recv, half):
        self.refs = buf, out, local, send, recv
        self.count, self.tile = buf.shape[0], buf.shape[1]
        self.half = half
        self.y = lax.axis_index("mp")

    def copies(self, i):
        buf, out, local, send, recv = self.refs
        rows = pl.ds(i * self.tile % self.half, self.tile)
        dst = out.at[self.y, rows]
        far = pltpu.make_async_remote_copy(src_ref=buf.at[i], dst_ref=dst, send_sem=send.at[i], recv_sem=recv.at[i],
                                           device_id={"mp": 1 - self.y}, device_id_type=pl.DeviceIdType.MESH)
        return pltpu.make_async_copy(buf.at[i], dst, local.at[i]), far

    def here(self, i):
        return self.y == i * self.tile // self.half

    def buffer(self, i):
        return self.refs[0].at[i]

    def send(self, i):
        near, far = self.copies(i)

        @pl.when(self.here(i))
        def _():
            near.start()

        @pl.when(jnp.logical_not(self.here(i)))
        def _():
            far.start()

    def finish(self):
        for i in range(self.count):
            near, far = self.copies(i)

            @pl.when(self.here(i))
            def _():
                near.wait()
                far.wait_recv()

            @pl.when(jnp.logical_not(self.here(i)))
            def _():
                far.wait_send()


def tiled(weights, rows, consts, outs, body, tile, steps, exchange=None, scratch=(), flops=0):
    nw, nr, nc, no = len(weights), len(rows), len(consts), len(outs)
    picks = [c for _, _, c in weights]
    piece = [own.shape if c is None else own.shape[1:] for own, _, c in weights]
    more = 1 if exchange else 0

    def kernel(*refs):
        srcs, refs = refs[:2 * nw], refs[2 * nw:]
        row_refs, const_refs, out_refs = refs[:nr], refs[nr:nr + nc], refs[nr + nc:nr + nc + no]
        refs = refs[nr + nc + no:]
        result, refs = refs[:more], refs[more:]
        wv, sems, refs = refs[:nw], refs[nw], refs[nw + 1:]
        step = pl.program_id(0)
        ex = Exchange(refs[0], result[0], *refs[1:4], exchange[1]) if exchange else None
        own_scratch = refs[4 * more:]

        def copies(i):
            own, far, c = srcs[2 * i], srcs[2 * i + 1], picks[i]
            own = own if c is None else own.at[c]
            some = lambda s, rs: far.at[s, rs] if c is None else far.at[s, rs, c]
            yield pltpu.make_async_copy(own, wv[i].at[0, 0], sems.at[i, 0])
            yield pltpu.make_async_copy(some(0, pl.ds(1, 3)), wv[i].at[0, pl.ds(1, 3)], sems.at[i, 1])
            yield pltpu.make_async_copy(some(1, pl.ds(0, 4)), wv[i].at[1], sems.at[i, 2])

        @pl.when(step == 0)
        def _():
            for i in range(nw):
                for copy in copies(i):
                    copy.start()
            if exchange:
                meet([{"mp": 1 - lax.axis_index("mp")}])

        def need(i):
            @pl.when(step == 0)
            def _():
                for copy in copies(i):
                    copy.wait()

        def put(value):
            dp = lax.axis_index("dp")
            unplace_store(ex.buffer(step), value, dp)
            for i in range(steps):
                @pl.when(step == i)
                def _():
                    ex.send(i)

        body(wv, need, row_refs, const_refs, out_refs, own_scratch, put)
        if exchange:
            @pl.when(step == steps - 1)
            def _():
                ex.finish()

    whole = lambda a: pl.BlockSpec(a.shape, lambda i: (0,) * a.ndim, pipeline_mode=pl.Buffered(1))
    ex_out, ex_shape, ex_scratch = [], [], []
    if exchange:
        _, half, cols = exchange
        ex_out, ex_shape = [HBM], [jax.ShapeDtypeStruct((2, half, cols), BF)]
        ex_scratch = [pltpu.VMEM((steps, tile, cols), BF)] + [pltpu.SemaphoreType.DMA((steps,))] * 3
    return pl.pallas_call(
        kernel,
        grid=(steps,),
        in_specs=[HBM] * (2 * nw) + [spec for _, spec in rows] + [whole(c) for c in consts],
        out_specs=[pl.BlockSpec(shape, index) for _, _, shape, index in outs] + ex_out,
        out_shape=[jax.ShapeDtypeStruct(shape, dtype) for shape, dtype, _, _ in outs] + ex_shape,
        scratch_shapes=[pltpu.VMEM((2, 4) + tuple(p), BF) for p in piece] + [pltpu.SemaphoreType.DMA((nw, 3))]
        + ex_scratch + list(scratch),
        compiler_params=pltpu.CompilerParams(
            vmem_limit_bytes=VMEM_BYTES, **(dict(collective_id=exchange[0], has_side_effects=True) if exchange else {})),
        cost_estimate=pl.CostEstimate(flops=flops, bytes_accessed=16 * 2**20, transcendentals=0),
    )(*[a for own, far, _ in weights for a in (own, far)], *[r[0] for r in rows], *consts)


def last_gradient(wq, dz1, dq, dk, dv, dpre, own_w):
    t, d = dz1.shape
    half = t // 2
    nz = lax.axis_size("adp")
    tile = half // 2
    count = t // tile
    hw = d // 2

    def kernel(wq_ref, dz_ref, dq_ref, dk_ref, dv_ref, dpre_ref, out, sum_ref,
               wv, zv, lv, buf, pv, got, tot, zbuf, sems, local, send, recv, psend, precv):
        dp, y, z, side, over, up = axes_here()
        along = [{"adp": lax.rem(z + k, nz)} for k in range(1, nz)]

        def rows_of(i):
            return pl.multiple_of(jnp.where(i < count // 2, 1 - y, y) * half + (i % 2) * tile, tile)

        def loads(i):
            rows = pl.ds(rows_of(i), tile)
            yield pltpu.make_async_copy(dz_ref.at[rows], zv.at[i], sems.at[4 * i])
            for c, ref in enumerate((dq_ref, dk_ref, dv_ref)):
                yield pltpu.make_async_copy(ref.at[rows], lv.at[i, :, pl.ds(c * d, d)], sems.at[4 * i + 1 + c])

        weight = pltpu.make_async_copy(wq_ref, wv, sems.at[4 * count])
        pre = pltpu.make_async_copy(dpre_ref, pv, sems.at[4 * count + 1])
        pre.start()
        weight.start()
        for i in range(count):
            for c in loads(i):
                c.start()
        meet([side, over, up] + along)

        def far(src, dst, peer, i):
            return pltpu.make_async_remote_copy(src_ref=src, dst_ref=dst, send_sem=psend.at[i], recv_sem=precv.at[i],
                                                device_id=peer, device_id_type=pl.DeviceIdType.MESH)

        first = far(pv.at[:, :, pl.ds(hw, hw)], got.at[0], up, 0)
        second = far(tot.at[0], got.at[1], side, 1)
        third = far(tot.at[1], got.at[2], over, 2)
        ring = [far(zbuf.at[z], zbuf.at[z], peer, 3 + k) for k, peer in enumerate(along)]

        def fold(k):
            if k == 0:
                first.wait_recv()
                tot[0] = pv[:, :, :hw] + got[0]
                second.start()
            elif k == 1:
                second.wait_recv()
                tot[1] = tot[0] + got[1]
                third.start()
            elif k == 2:
                third.wait_recv()
                zbuf[z] = tot[1] + got[2]
                for c in ring:
                    c.start()
            else:
                for c in ring:
                    c.wait_recv()
                total = zbuf[0]
                for j in range(1, nz):
                    total = total + zbuf[j]
                sum_ref[...] = total

        pre.wait()
        first.start()
        weight.wait()
        moves = []
        for i in range(count):
            for c in loads(i):
                c.wait()
            lhs = lv[i]
            e = jnp.concatenate(
                [dot_mm(lhs, jnp.concatenate([wv[s, r, c] for c in range(3) for s in range(2)], axis=1), 1, 1)
                 for r in range(d // TILE)], axis=1)
            unplace_store(buf.at[i], zv[i] + e, dp)
            dst = out.at[y, pl.ds((i % 2) * tile, tile)]
            if i < count // 2:
                move = pltpu.make_async_remote_copy(
                    src_ref=buf.at[i], dst_ref=dst, send_sem=send.at[i], recv_sem=recv.at[i],
                    device_id=up, device_id_type=pl.DeviceIdType.MESH)
            else:
                move = pltpu.make_async_copy(buf.at[i], dst, local.at[i])
            move.start()
            moves.append(move)
            if 1 <= i:
                fold(i - 1)
        fold(3)
        for c in [first, second, third] + ring:
            c.wait_send()
        for c in moves:
            c.wait()

    vm = pltpu.VMEM
    shape = jax.ShapeDtypeStruct
    dma = pltpu.SemaphoreType.DMA
    return pl.pallas_call(
        kernel,
        in_specs=[HBM] * 6,
        out_specs=[HBM, pl.BlockSpec(memory_space=pltpu.VMEM)],
        out_shape=[shape((2, half, d), BF), shape((2, PRE, hw), F32)],
        scratch_shapes=[vm(wq.shape, BF), vm((count, tile, d), F32), vm((count, tile, 3 * d), BF), vm((count, tile, d), BF),
                        vm((2, PRE, d), F32), vm((3, 2, PRE, hw), F32), vm((2, 2, PRE, hw), F32), vm((nz, 2, PRE, hw), F32),
                        dma((4 * count + 2,)), dma((count,)), dma((count,)), dma((count,)), dma((2 + nz,)), dma((2 + nz,))],
        compiler_params=pltpu.CompilerParams(collective_id=4, has_side_effects=True, vmem_limit_bytes=VMEM_BYTES),
        cost_estimate=pl.CostEstimate(flops=6 * t * d * d, bytes_accessed=2**24, transcendentals=0),
    )(wq, dz1, dq, dk, dv, dpre)


def by_rows(ref):
    return lambda s, r, j: ref.at[s, r, pl.ds(j * TILE, TILE)]


def by_cols(ref):
    return lambda s, r, j: ref.at[s, r, slice(None), pl.ds(j * TILE, TILE)]


def meet(peers):
    barrier = pltpu.get_barrier_semaphore()
    for peer in peers:
        pl.semaphore_signal(barrier, inc=1, device_id=peer, device_id_type=pl.DeviceIdType.MESH)
    pl.semaphore_wait(barrier, len(peers))


class Moves:
    def __init__(self, table, send, recv, local):
        self.table, self.send, self.recv, self.local = table, send, recv, local
        self.place = {}
        far = near = 0
        for name, (src, dst, peer) in table.items():
            if peer is None:
                self.place[name] = near
                near += 1
            else:
                self.place[name] = far
                far += 1

    def copy(self, name):
        src, dst, peer = self.table[name]
        i = self.place[name]
        if peer is None:
            return pltpu.make_async_copy(src, dst, self.local.at[i])
        return pltpu.make_async_remote_copy(src_ref=src, dst_ref=dst, send_sem=self.send.at[i], recv_sem=self.recv.at[i],
                                            device_id=peer, device_id_type=pl.DeviceIdType.MESH)

    def start(self, *names):
        for name in names:
            self.copy(name).start()

    def got(self, *names):
        for name in names:
            if self.table[name][2] is None:
                self.copy(name).wait()
            else:
                self.copy(name).wait_recv()

    def sent(self, *names):
        for name in names:
            self.copy(name).wait_send()


def axes_here():
    dp, y, z = lax.axis_index("dp"), lax.axis_index("mp"), lax.axis_index("adp")
    return dp, y, z, {"dp": dp ^ 1}, {"dp": dp ^ 2}, {"mp": 1 - y}


SPOTS = {"x": (0, 2), "y": (1, 0), "d": (1, 2)}


def plane_moves(table, tag, own, far, part, side, over, up):
    table[tag, "y"] = (part(own), part(far(1, 0)), up)
    table[tag, "x"] = (part(own), part(far(0, 2)), over)
    table[tag, "d"] = (part(far(1, 0)), part(far(1, 2)), over)
    for spot in "xyd":
        s, r = SPOTS[spot]
        table[tag, spot, "side"] = (part(far(s, r)), part(far(s, r ^ 1)), side)


def ring_moves(table, tag, own, far, quarter, z, nz, side, over, up, onward):
    first = quarter(z)
    table[tag, "y"] = (first(own), first(far(1, 0)), up)
    table[tag, "x"] = (first(own), first(far(0, 2)), over)
    table[tag, "d"] = (first(far(1, 0)), first(far(1, 2)), over)
    for spot in "xyd":
        s, r = SPOTS[spot]
        for k in range(nz):
            part = quarter(lax.rem(z + nz - k, nz))
            table[tag, spot, k, "side"] = (part(far(s, r)), part(far(s, r ^ 1)), side)
            if k + 1 < nz:
                table[tag, spot, k, "on"] = (part(far(s, r)), part(far(s, r)), onward)


def self_forward(inputs, memory, self_qkv, self_proj, cross_qkv, cross_proj, pre_own, ad_own):
    _, _, half, d = inputs.shape
    t = 2 * half
    nq, wrows, hw = self_qkv.shape
    nz = lax.axis_size("adp")
    prow = self_proj.shape[0]
    pairs = d // 128
    chunks = d // TILE
    qscale = HEAD_DIM ** -0.5 * LOG2E
    ring_tags = ("cq12", "co")
    plane_tags = ("so", "cq0")

    def moves(refs):
        (in_ref, mem_ref, own_ref, so_ref, cq_ref, co_ref, pre_ref, ad_ref,
         q_out, k_out, v_out, w_out, x_out, pre_out, bso, bcq, bco, mem_out, ada_ref, wv, xv, qs, ks, vs, pv) = refs
        dp, y, z, side, over, up = axes_here()
        onward = {"adp": lax.rem(z + 1, nz)}
        along = [{"adp": lax.rem(z + k, nz)} for k in range(1, nz)]
        rows = pl.ds(pl.multiple_of(y * half, half), half)
        table = {}
        table["w own"] = (own_ref, wv.at[0, 0], None)
        table["pre own"] = (pre_ref, pv.at[:, :, pl.ds(0, hw)], None)
        for r in range(chunks):
            cols = pl.ds(pl.multiple_of((dp ^ r) * TILE, TILE), TILE)
            table["x own", r] = (in_ref.at[y, 0, :, cols], xv.at[rows, pl.ds(r * TILE, TILE)], None)
            table["x up", r] = (in_ref.at[1 - y, 0, :, cols], xv.at[rows, pl.ds(r * TILE, TILE)], up)
        table["pre up"] = (pre_ref, pv.at[:, :, pl.ds(hw, hw)], up)
        plane_moves(table, "w", own_ref, lambda s, r: wv.at[s, r], lambda ref: ref, side, over, up)
        table["w", "side"] = (own_ref, wv.at[0, 1], side)
        for k in range(1, nz):
            table["ad", k] = (ad_ref, ada_ref.at[k], along[k - 1])
        plane_moves(table, "so", so_ref, lambda s, r: bso.at[s, r], lambda ref: ref, side, over, up)
        plane_moves(table, "cq0", cq_ref, lambda s, r: bcq.at[s, r], lambda ref: ref.at[0], side, over, up)
        ring_moves(table, "cq12", cq_ref, lambda s, r: bcq.at[s, r],
                   lambda qz: lambda ref: ref.at[pl.ds(1, 2), pl.ds(pl.multiple_of(qz * (wrows // nz), wrows // nz), wrows // nz)],
                   z, nz, side, over, up, onward)
        ring_moves(table, "co", co_ref, lambda s, r: bco.at[s, r],
                   lambda qz: lambda ref: ref.at[pl.ds(pl.multiple_of(qz * (prow // nz), prow // nz), prow // nz)],
                   z, nz, side, over, up, onward)
        table["so", "side"] = (so_ref, bso.at[0, 1], side)
        table["cq", "side"] = (cq_ref, bcq.at[0, 1], side)
        table["co", "side"] = (co_ref, bco.at[0, 1], side)
        table["mem up"] = (mem_ref.at[1 - y, 0], mem_out, up)
        for name, s_, o_ in (("q", qs, q_out), ("k", ks, k_out), ("v", vs, v_out), ("w", wv, w_out), ("x", xv, x_out), ("pre", pv, pre_out)):
            table[name + " out"] = (s_, o_, None)
        return table, (side, over, up), along

    def count():
        rings = len(ring_tags) * (3 + 3 * nz + 3 * (nz - 1))
        planes = (1 + len(plane_tags)) * 6
        return chunks + planes + rings + nz + 5, chunks + 8

    def kernel(in_ref, mem_ref, own_ref, so_ref, cq_ref, co_ref, pre_ref, ad_ref,
               a_ref, p_ref, pp_ref, l_ref, q_out, k_out, v_out, w_out, x_out, pre_out, bso, bcq, bco, mem_out, ada_ref,
               wv, xv, qs, ks, vs, pv, send, recv, local):
        g = pl.program_id(0)
        table, near_peers, along = moves((in_ref, mem_ref, own_ref, so_ref, cq_ref, co_ref, pre_ref, ad_ref,
                                          q_out, k_out, v_out, w_out, x_out, pre_out, bso, bcq, bco, mem_out, ada_ref,
                                          wv, xv, qs, ks, vs, pv))
        mv = Moves(table, send, recv, local)
        done = set()

        def got(*names):
            done.update(names)
            mv.got(*names)

        xs_up = [("x up", r) for r in range(chunks)]
        xs_own = [("x own", r) for r in range(chunks)]
        ads = [("ad", k) for k in range(1, nz)]
        outs = [n + " out" for n in ("q", "k", "v", "w", "x", "pre")]

        def pass_on(spot, k):
            for tag in ring_tags:
                got((tag, spot) if k == 0 else (tag, spot, k - 1, "on"))
                if k + 1 < nz:
                    mv.start((tag, spot, k, "on"))
                mv.start((tag, spot, k, "side"))

        @pl.when(g == 0)
        def _():
            meet(list(near_peers) + along)
            mv.start(("w", "y"), ("w", "x"), "pre up")
            mv.start(*[(tag, spot) for tag in ring_tags for spot in "yx"])
            mv.start(*xs_up)
            mv.start(("w", "side"), *ads)
            mv.start("w own", "pre own", *xs_own)
            got(("w", "y"))
            mv.start(("w", "d"), ("w", "y", "side"))
            got(("w", "x"))
            mv.start(("w", "x", "side"))
            pass_on("y", 0)
            mv.start(*[(tag, "d") for tag in ring_tags])
            pass_on("x", 0)
            mv.start(*[(tag, spot) for tag in plane_tags for spot in "xy"])
            mv.start("mem up", ("so", "side"), ("cq", "side"), ("co", "side"))
            for k in range(1, nz):
                pass_on("y", k)
                pass_on("x", k)
            got(("w", "d"))
            mv.start(("w", "d", "side"))
            pass_on("d", 0)
            got("w own", "pre own", "pre up", ("w", "side"), ("w", "y", "side"), ("w", "x", "side"), ("w", "d", "side"))
            got(*xs_own)
            got(*xs_up)
            for i in range(2):
                x = xv[i * half:(i + 1) * half]
                for c, out in ((0, qs), (1, ks), (2, vs)):
                    for s in range(2):
                        w = jnp.concatenate([wv[s, r, c] for r in range(4)], axis=0)
                        o = dot_mm(x, w, 1, 0)
                        out[i * half:(i + 1) * half, s * hw:(s + 1) * hw] = (o * qscale if c == 0 else o).astype(BF)
                if i + 1 < nz:
                    pass_on("d", i + 1)
            mv.start(*outs)

        for k in range(3, nz):
            @pl.when(g == k - 2)
            def _():
                pass_on("d", k)

        @pl.when(g == 3)
        def _():
            for tag in plane_tags:
                got((tag, "y"), (tag, "x"))
                mv.start((tag, "d"), (tag, "y", "side"), (tag, "x", "side"))

        @pl.when(g > 0)
        def _():
            cs = pl.ds(pl.multiple_of((g - 1) * 128, 128), 128)
            a, il = attend_pair(True, PREFIX_LEN, qs[:, cs], ks[:, cs], vs[:, cs], pv[0, :, cs], pv[1, :, cs], p_ref, pp_ref)
            a_ref[...] = a
            l_ref[0] = il

        @pl.when(g == pairs)
        def _():
            for tag in plane_tags:
                got((tag, "d"))
                mv.start((tag, "d", "side"))
            far = [n for n, (_, _, peer) in table.items() if peer is not None]
            got(*[n for n in far if n not in done])
            got(*outs)
            mv.sent(*far)

    lead = lambda g: (jnp.maximum(g - 1, 0), 0, 0)
    col = lambda g: (0, jnp.maximum(g - 1, 0))
    shape = jax.ShapeDtypeStruct
    remotes, near = count()
    vm = pltpu.VMEM
    return pl.pallas_call(
        kernel,
        grid=(pairs + 1,),
        in_specs=[HBM] * 8,
        out_specs=[pl.BlockSpec((t, 128), col), pl.BlockSpec((2, t, t), lead), pl.BlockSpec((2, PRE, t), lead),
                   pl.BlockSpec((1, 2, t), lead)] + [HBM] * 11,
        out_shape=[
            shape((t, d), BF), shape((2 * pairs, t, t), BF), shape((2 * pairs, PRE, t), BF), shape((pairs, 2, t), F32),
            shape((t, d), BF), shape((t, d), BF), shape((t, d), BF), shape((2, 4) + self_qkv.shape, BF),
            shape((t, d), BF), shape((2, PRE, d), BF), shape((2, 4) + self_proj.shape, BF), shape((2, 4) + cross_qkv.shape, BF),
            shape((2, 4) + cross_proj.shape, BF), shape((half, d), BF), shape((nz,) + ad_own.shape, BF),
        ],
        scratch_shapes=[vm((2, 4) + self_qkv.shape, BF), vm((t, d), BF), vm((t, d), BF), vm((t, d), BF), vm((t, d), BF),
                        vm((2, PRE, d), BF), pltpu.SemaphoreType.DMA((remotes,)),
                        pltpu.SemaphoreType.DMA((remotes,)), pltpu.SemaphoreType.DMA((near,))],
        compiler_params=pltpu.CompilerParams(collective_id=0, has_side_effects=True, vmem_limit_bytes=VMEM_BYTES),
        cost_estimate=pl.CostEstimate(flops=10**11, bytes_accessed=10**8, transcendentals=0),
    )(inputs, memory, self_qkv, self_proj, cross_qkv, cross_proj, pre_own, ad_own)


def cross_forward(src_n, x_full, a, mem_mine, mem_got, self_proj, b_so, cross_qkv, b_cq, ad_col, cotangent, ffn_in, ffn_out, gain):
    t, d = x_full.shape
    half = t // 2
    nz = lax.axis_size("adp")
    pairs = d // 128
    chunks = d // TILE
    khead = self_proj.shape[0] // TILE
    kcol = cross_qkv.shape[2] // TILE
    nq = cross_qkv.shape[0]
    orow = ffn_out.shape[0]
    icol = ffn_in.shape[1]
    ihalf = icol // 2
    qscale = HEAD_DIM ** -0.5 * LOG2E

    def moves(refs):
        ad_ref, cot_ref, fi_ref, fo_ref, q_out, k_out, v_out, cin, cout, ada_ref, cot_out, qs, ks, vs = refs
        dp, y, z, side, over, up = axes_here()
        onward = {"adp": lax.rem(z + 1, nz)}
        before = {"adp": lax.rem(z + nz - 1, nz)}
        table = {}
        for name, s_, o_ in (("q", qs, q_out), ("k", ks, k_out), ("v", vs, v_out)):
            table[name + " out"] = (s_, o_, None)
        ring_moves(table, "o", fo_ref, lambda s, r: cout.at[s, r],
                   lambda qz: lambda ref: ref.at[pl.ds(pl.multiple_of(qz * (orow // nz), orow // nz), orow // nz)],
                   z, nz, side, over, up, onward)
        table["o", "side"] = (fo_ref, cout.at[0, 1], side)
        table["i", "side"] = (fi_ref, cin.at[0, 1], side)
        table["i", "y"] = (fi_ref, cin.at[1, 0], up)
        table["i", "x"] = (fi_ref, cin.at[0, 2], over)
        one, two = pl.ds(0, ihalf), pl.ds(ihalf, ihalf)
        table["i", "d1"] = (cin.at[1, 0, :, one], cin.at[1, 2, :, one], over)
        table["i", "d2"] = (cin.at[0, 2, :, two], cin.at[1, 2, :, two], up)
        table["i", "y", "side"] = (cin.at[1, 0], cin.at[1, 1], side)
        table["i", "x", "side"] = (cin.at[0, 2], cin.at[0, 3], side)
        table["i", "d1", "side"] = (cin.at[1, 2, :, one], cin.at[1, 3, :, one], side)
        table["i", "d2", "side"] = (cin.at[1, 2, :, two], cin.at[1, 3, :, two], side)
        table["ad side"] = (ad_ref, ada_ref.at[1], side)
        table["ad over"] = (ad_ref, ada_ref.at[2], over)
        table["ad over side"] = (ada_ref.at[2], ada_ref.at[3], side)
        table["cot"] = (cot_ref.at[1 - y, 0], cot_out, up)
        return table, [side, over, up, onward, before]

    def kernel(n_ref, x_ref, a_in, gain_ref, memo_ref, memg_ref, so_ref, bso, cq_ref, bcq, ad_ref, cot_ref, fi_ref, fo_ref,
               ac_ref, p_ref, l_ref, u_ref, inv_ref, q_out, k_out, v_out, cin, cout, ada_ref, cot_out,
               sov, cqv, qs, ks, vs, send, recv, local, wsem):
        g = pl.program_id(0)
        dp, y = lax.axis_index("dp"), lax.axis_index("mp")
        table, peers = moves((ad_ref, cot_ref, fi_ref, fo_ref, q_out, k_out, v_out, cin, cout, ada_ref, cot_out, qs, ks, vs))
        mv = Moves(table, send, recv, local)
        done = set()

        def got(*names):
            done.update(names)
            mv.got(*names)

        def pass_on(spot, k):
            got(("o", spot) if k == 0 else ("o", spot, k - 1, "on"))
            if k + 1 < nz:
                mv.start(("o", spot, k, "on"))
            mv.start(("o", spot, k, "side"))

        outs = [n + " out" for n in ("q", "k", "v")]

        def loads():
            for i, (own, far, dst) in enumerate(((so_ref, bso, sov), (cq_ref, bcq, cqv))):
                yield pltpu.make_async_copy(own, dst.at[0, 0], wsem.at[i, 0])
                yield pltpu.make_async_copy(far.at[0, pl.ds(1, 3)], dst.at[0, pl.ds(1, 3)], wsem.at[i, 1])
                yield pltpu.make_async_copy(far.at[1], dst.at[1], wsem.at[i, 2])

        so = by_rows(sov)

        def project(i):
            rs = slice(i * half, (i + 1) * half)
            att = a_in[rs]
            z1 = x_ref[rs].astype(F32) + jnp.concatenate(
                [nn(att, [so(s, r, j) for s in range(2) for j in range(khead)]) for r in range(chunks)], axis=1)
            u, inv = normalize(z1)
            u_ref[rs] = u
            inv_ref[rs] = inv
            h = (u * gain_ref[...]).astype(BF)
            xm = jnp.where(y == i, place_cols(memo_ref, dp), place_cols(memg_ref, dp))
            for lhs, c, out in ((h, 0, qs), (xm, 1, ks), (xm, 2, vs)):
                for s in range(2):
                    for j in range(kcol):
                        o = nn(lhs, [cqv.at[s, r, c, :, pl.ds(j * TILE, TILE)] for r in range(4)])
                        cs = slice((s * kcol + j) * TILE, (s * kcol + j + 1) * TILE)
                        out[rs, cs] = (o * qscale if c == 0 else o).astype(BF)

        @pl.when(g == 0)
        def _():
            for c in loads():
                c.start()
            meet(peers)
            mv.start(("o", "y"), ("o", "x"), ("i", "y"), ("i", "side"), ("o", "side"), "ad side")
            for c in loads():
                c.wait()
            project(0)
            pass_on("y", 0)
            mv.start(("o", "d"), ("i", "x"), "ad over", "cot")
            pass_on("x", 0)
            project(1)
            pass_on("d", 0)
            mv.start(*outs)

        for k in range(1, nz):
            @pl.when(g == 3 * k - 2)
            def _():
                pass_on("y", k)
                pass_on("x", k)

            @pl.when(g == 3 * k - 1)
            def _():
                pass_on("d", k)

        @pl.when(g == 3)
        def _():
            got(("i", "y"))
            mv.start(("i", "d1"), ("i", "y", "side"))

        @pl.when(g == 6)
        def _():
            got(("i", "x"))
            mv.start(("i", "d2"), ("i", "x", "side"))

        @pl.when(g > 0)
        def _():
            cs = pl.ds(pl.multiple_of((g - 1) * 128, 128), 128)
            av, il = attend_pair(False, n_ref[0], qs[:, cs], ks[:, cs], vs[:, cs], None, None, p_ref, None)
            ac_ref[...] = av
            l_ref[0] = il

        @pl.when(g == pairs)
        def _():
            got("ad over")
            mv.start("ad over side")
            got(("i", "d1"))
            mv.start(("i", "d1", "side"))
            got(("i", "d2"))
            mv.start(("i", "d2", "side"))
            far = [n for n, (_, _, peer) in table.items() if peer is not None]
            got(*[n for n in far if n not in done])
            got(*outs)
            mv.sent(*far)

    lead = lambda g: (jnp.maximum(g - 1, 0), 0, 0)
    col = lambda g: (0, jnp.maximum(g - 1, 0))
    fixed = lambda g: (0, 0)
    shape = jax.ShapeDtypeStruct
    once = pl.Buffered(1)
    remotes = 3 + 3 * nz + 3 * (nz - 1) + 10 + 4
    near = 3
    vm = pltpu.VMEM
    whole = lambda *s: pl.BlockSpec(s, fixed, pipeline_mode=once)
    return pl.pallas_call(
        kernel,
        grid=(pairs + 1,),
        in_specs=[pl.BlockSpec(memory_space=pltpu.SMEM), whole(t, d), whole(t, d), whole(1, d), whole(half, d), whole(half, d)]
        + [HBM] * 8,
        out_specs=[pl.BlockSpec((t, 128), col), pl.BlockSpec((2, t, t), lead), pl.BlockSpec((1, 2, t), lead),
                   pl.BlockSpec((t, d), fixed), pl.BlockSpec((t, 1), fixed)] + [HBM] * 7,
        out_shape=[
            shape((t, d), BF), shape((2 * pairs, t, t), BF), shape((pairs, 2, t), F32), shape((t, d), F32), shape((t, 1), F32),
            shape((t, d), BF), shape((t, d), BF), shape((t, d), BF), shape((2, 4) + ffn_in.shape, BF), shape((2, 4) + ffn_out.shape, BF),
            shape((4,) + ad_col.shape, BF), shape((half, d), BF),
        ],
        scratch_shapes=[vm((2, 4) + self_proj.shape, BF), vm((2, 4) + cross_qkv.shape, BF), vm((t, d), BF), vm((t, d), BF), vm((t, d), BF),
                        pltpu.SemaphoreType.DMA((remotes,)), pltpu.SemaphoreType.DMA((remotes,)),
                        pltpu.SemaphoreType.DMA((near,)), pltpu.SemaphoreType.DMA((2, 3))],
        compiler_params=pltpu.CompilerParams(collective_id=1, has_side_effects=True, vmem_limit_bytes=VMEM_BYTES),
        cost_estimate=pl.CostEstimate(flops=10**11, bytes_accessed=10**8, transcendentals=0),
    )(src_n, x_full, a, gain, mem_mine, mem_got, self_proj, b_so, cross_qkv, b_cq, ad_col, cotangent, ffn_in, ffn_out)


def whole_sequences(inputs, memory, src_lengths, self_qkv, self_proj, cross_qkv, cross_proj, ffn_in, ffn_out,
                    norm_gains, prefix, adapter_down, adapter_up, cotangent):
    dp, y, z = lax.axis_index("dp"), lax.axis_index("mp"), lax.axis_index("adp")
    nz = lax.axis_size("adp")
    half, d = inputs.shape[2], inputs.shape[3]
    t = 2 * half
    chunks = d // TILE
    mine = lambda a: lax.dynamic_index_in_dim(a, y, 0, keepdims=False)[0]
    rel = lambda a: jnp.concatenate(
        [lax.dynamic_slice_in_dim(a, (dp ^ r) * TILE, TILE, axis=a.ndim - 1) for r in range(chunks)], axis=-1)

    ad_own = jnp.concatenate([adapter_down.T, adapter_up], axis=0)
    pre_own = jnp.pad(prefix, ((0, 0), (0, PRE - PREFIX_LEN), (0, 0)))
    src_n = lax.dynamic_index_in_dim(src_lengths, y, 0, keepdims=False).reshape(1)
    khead, kcol = self_proj.shape[0] // TILE, cross_qkv.shape[2] // TILE
    kin = ffn_in.shape[1] // TILE

    gains = rel(norm_gains.astype(F32))
    gain = [gains[i:i + 1] for i in range(3)]
    row = lambda i: (i, 0)
    hw = self_qkv.shape[2]

    a, p, pp, il, q, k, v, wq, x_full, pre_w, b_so, b_cq, b_co, mem_got, ad_col = self_forward(
        inputs, memory, self_qkv, self_proj, cross_qkv, cross_proj, pre_own, ad_own)
    ad_col = lax.dynamic_update_slice_in_dim(ad_col, ad_own[None], 0, axis=0)
    w_so, w_co = (self_proj, b_so, None), (cross_proj, b_co, None)
    w_cq = lambda c: (cross_qkv, b_cq, c)
    out_rows = lambda T, r, n: [T(s, r, j) for s in range(2) for j in range(n)]
    ac, p_c, il_c, u1, inv1, qc, kc, vc, c_in, c_out, ad_all, cot_got = cross_forward(
        src_n, x_full, a, mine(memory), mem_got, self_proj, b_so, cross_qkv, b_cq, ad_col, cotangent, ffn_in, ffn_out, gain[0])
    fixed = lambda i: (0, 0)
    spec = lambda shape, index: pl.BlockSpec(shape, index)
    held = lambda *shape: pl.BlockSpec(shape, lambda i: (0,) * len(shape), pipeline_mode=pl.Buffered(1))

    n_ad = ad_own.shape[0] // 2
    tile = half // FEED_SPLIT
    hid = 2 * kin

    def feed(W, need, rows, consts, outs, scr, put):
        dp, y = lax.axis_index("dp"), lax.axis_index("mp")
        ac_ref, u1_ref, cot_a, cot_b = rows
        act_ref, slope_ref, terms = scr
        g1, g2, g3 = consts[:3]
        co, fi, fo = by_rows(W[0]), by_cols(W[1]), by_rows(W[2])
        down = lambda r, kk: (consts[3].at[kk] if r == 0 else consts[4].at[r, kk]).at[pl.ds(0, n_ad)]
        upw = lambda r, kk: (consts[3].at[kk] if r == 0 else consts[4].at[r, kk]).at[pl.ds(n_ad, n_ad)]
        need(0)
        att = ac_ref[...]
        z2 = u1_ref[...] * g1[...] + jnp.concatenate(
            [nn(att, out_rows(co, r, khead)) for r in range(chunks)], axis=1)
        u2, inv2 = normalize(z2)
        h2 = u2 * g2[...]
        h2b = h2.astype(BF)
        need(1)
        order = [(s, j) for s in range(2) for j in range(kin)]
        ahead = nn(h2b, [fi(0, r, 0) for r in range(4)])
        for i in range(hid):
            g = ahead
            if i + 1 < hid:
                s, j = order[i + 1]
                ahead = nn(h2b, [fi(s, r, j) for r in range(4)])
            act, slope = gelu_pair(g)
            act_ref[:, i * TILE:(i + 1) * TILE] = act.astype(BF)
            slope_ref[:, i * TILE:(i + 1) * TILE] = slope.astype(BF)
        down_t = jnp.concatenate([stack_cols([down(r, kk) for r in range(4)]) for kk in range(nz)], axis=0)
        up_m = jnp.concatenate([stack_cols([upw(r, kk) for r in range(4)]) for kk in range(nz)], axis=0)
        act_a, slope_a = gelu_pair(dot_mm(h2b, down_t, 1, 1))
        act_a = act_a.astype(BF)
        need(2)
        acts = act_ref[...]
        z3 = h2 + 4.0 * dot_mm(act_a, up_m, 1, 0) + jnp.concatenate(
            [nn(acts, out_rows(fo, r, kin)) for r in range(chunks)], axis=1)
        u3, inv3 = normalize(z3)
        put(u3 * g3[...])
        in_own = pl.program_id(0) // (half // tile) == y
        cot = jnp.where(in_own, place_cols(cot_a, dp), place_cols(cot_b, dp)).astype(F32)
        dz3 = norm_back(cot, u3, inv3, g3[...])
        b3 = dz3.astype(BF)
        dga = (4.0 * dot_mm(b3, up_m, 1, 1) * slope_a).astype(BF)
        up_term = 4.0 * dot_mm(act_a, b3, 0, 0)
        down_term = dot_mm(dga, h2b, 0, 0)

        @pl.when(pl.program_id(0) == 0)
        def _():
            terms[0] = down_term
            terms[1] = up_term

        @pl.when(pl.program_id(0) > 0)
        def _():
            terms[0] += down_term
            terms[1] += up_term

        @pl.when(pl.program_id(0) == pl.num_programs(0) - 1)
        def _():
            for i in range(2):
                outs[2][:, i] = terms[:, :, 2 * i * TILE:(2 * i + 1) * TILE]
                outs[3][:, i] = terms[:, :, (2 * i + 1) * TILE:(2 * i + 2) * TILE].astype(BF)

        for i, (s, j) in enumerate(order):
            cs = slice(i * TILE, (i + 1) * TILE)
            df = nt(b3, [fo(s, r, j) for r in range(4)])
            slope_ref[:, cs] = (df * slope_ref[:, cs].astype(F32)).astype(BF)
        dg = slope_ref[...]
        dh2 = dz3 + dot_mm(dga, down_t, 1, 0) + jnp.concatenate(
            [nt(dg, out_rows(fi, r, kin)) for r in range(chunks)], axis=1)
        dz2 = norm_back(dh2, u2, inv2, g2[...])
        outs[0][...] = dz2
        dz2b = dz2.astype(BF)
        for s in range(2):
            for j in range(khead):
                i = s * khead + j
                outs[1][:, i * TILE:(i + 1) * TILE] = nt(dz2b, [co(s, r, j) for r in range(4)]).astype(BF)

    part = lambda i: (i % (half // tile), 0)
    dz2, dac, keep, give, result = tiled(
        [w_co, (ffn_in, c_in, None), (ffn_out, c_out, None)],
        [(ac, spec((tile, d), row)), (u1, spec((tile, d), row)), (mine(cotangent), spec((tile, d), part)),
         (cot_got, spec((tile, d), part))],
        gain + [ad_col, ad_all],
        [((t, d), F32, (tile, d), row), ((t, d), BF, (tile, d), row),
         ((2, 2, nz * n_ad, TILE), F32, (2, 2, nz * n_ad, TILE), lambda i: (0, 0, 0, 0)),
         ((2, 2, nz * n_ad, TILE), BF, (2, 2, nz * n_ad, TILE), lambda i: (0, 0, 0, 0))],
        feed, tile, t // tile, exchange=(2, half, d),
        scratch=[pltpu.VMEM((tile, hid * TILE), BF)] * 2 + [pltpu.VMEM((2, nz * n_ad, d), F32)], flops=4 * 2 * t * d * hid * TILE)

    dqc, dkc, dvc, down_grad, up_grad = attn_bwd(qc, kc, vc, ac, dac, il_c, p_c, keep=keep, give=give)

    def memory_back(sc, own, far, dk_ref, dv_ref, mine_ref, send_ref, wv, sems):
        def loads():
            yield pltpu.make_async_copy(own.at[pl.ds(1, 2)], wv.at[0, 0], sems.at[0])
            yield pltpu.make_async_copy(far.at[0, pl.ds(1, 3), pl.ds(1, 2)], wv.at[0, pl.ds(1, 3)], sems.at[1])
            yield pltpu.make_async_copy(far.at[1, pl.ds(0, 4), pl.ds(1, 2)], wv.at[1], sems.at[2])

        step = pl.program_id(0)

        @pl.when(step == 0)
        def _():
            for c in loads():
                c.start()
            for c in loads():
                c.wait()

        lhs = jnp.concatenate([dk_ref[...], dv_ref[...]], axis=1)
        e = jnp.concatenate(
            [dot_mm(lhs, jnp.concatenate([wv[s, r, c] for c in range(2) for s in range(2)], axis=1), 1, 1)
             for r in range(chunks)], axis=1)

        @pl.when(step == 0)
        def _():
            unplace_store(send_ref, e, sc[0])

        @pl.when(step == 1)
        def _():
            unplace_store(mine_ref.at[0], e, sc[0])

    turned = lambda i, sc: (jnp.where(i == 0, 1 - sc[1], sc[1]), 0)
    mem_mine, mem_send = pl.pallas_call(
        memory_back,
        grid_spec=pltpu.PrefetchScalarGridSpec(
            num_scalar_prefetch=1, grid=(2,),
            in_specs=[HBM, HBM, pl.BlockSpec((half, d), turned), pl.BlockSpec((half, d), turned)],
            out_specs=[pl.BlockSpec((1, half, d), lambda i, sc: (sc[1], 0, 0)), pl.BlockSpec((half, d), lambda i, sc: (0, 0))],
            scratch_shapes=[pltpu.VMEM((2, 4, 2) + cross_qkv.shape[1:], BF), pltpu.SemaphoreType.DMA((3,))]),
        out_shape=[jax.ShapeDtypeStruct((2, half, d), BF), jax.ShapeDtypeStruct((half, d), BF)],
        compiler_params=pltpu.CompilerParams(vmem_limit_bytes=VMEM_BYTES),
        cost_estimate=pl.CostEstimate(flops=4 * t * d * d, bytes_accessed=2**24, transcendentals=0),
    )(jnp.stack([dp, y]).astype(jnp.int32), cross_qkv, b_cq, dkc, dvc)

    def norm_back_self(W, need, rows, consts, outs, scr, put):
        dz2_ref, dqc_ref, u1_ref, inv_ref = rows
        cq, so = by_cols(W[0]), by_rows(W[1])
        need(0)
        dq_c = dqc_ref[...]
        e = dz2_ref[...] + jnp.concatenate([nt(dq_c, out_rows(cq, r, kcol)) for r in range(chunks)], axis=1)
        dz1 = norm_back(e, u1_ref[...], inv_ref[...], consts[0][...])
        outs[0][...] = dz1
        dz1b = dz1.astype(BF)
        need(1)
        for s in range(2):
            for j in range(khead):
                i = s * khead + j
                outs[1][:, i * TILE:(i + 1) * TILE] = nt(dz1b, [so(s, r, j) for r in range(4)]).astype(BF)

    dz1, da = tiled(
        [w_cq(0), w_so],
        [(dz2, spec((half, d), row)), (dqc, spec((half, d), row)), (u1, spec((half, d), row)), (inv1, spec((half, 1), row))],
        [gain[0]],
        [((t, d), F32, (half, d), row), ((t, d), BF, (half, d), row)], norm_back_self, half, 2,
        flops=4 * t * d * d)

    dq, dk, dv, dpre, memory_grad = attn_bwd(q, k, v, a, da, il, p, pp, pre_w, mem_send, mem_mine)
    input_grad, pre_sum = last_gradient(wq, dz1, dq, dk, dv, dpre, self_qkv)
    return result[:, None], input_grad[:, None], memory_grad[:, None], pre_sum[:, :PREFIX_LEN], down_grad, up_grad


def solution(mesh):
    by_sequence = mesh.shape["mp"] == MICRO and mesh.shape["dp"] == 4
    return jax.shard_map(
        whole_sequences if by_sequence else shards,
        mesh=mesh,
        in_specs=(
            P(None, ("dp", "adp"), "mp", None),
            P(None, ("dp", "adp"), "mp", None),
            P(None, ("dp", "adp"), None),
            P(None, "dp", "mp"),
            P("mp", "dp"),
            P(None, "dp", "mp"),
            P("mp", "dp"),
            P("dp", "mp"),
            P("mp", "dp"),
            P(),
            P(None, None, "mp"),
            P("dp", "adp"),
            P("adp", "dp"),
            P(None, ("dp", "adp"), "mp", None),
        ),
        out_specs=(
            P(None, ("dp", "adp"), "mp", None),
            P(None, ("dp", "adp"), "mp", None),
            P(None, ("dp", "adp"), "mp", None),
            P(None, None, "mp"),
            P(("dp", "mp"), "adp"),
            P("adp", ("dp", "mp")),
        ),
        check_vma=False,
    )
```

```python
import functools
import math

import jax
import jax.numpy as jnp
from jax import lax
from jax.experimental import pallas as pl
from jax.experimental.pallas import tpu as pltpu
from jax.sharding import PartitionSpec as P

HEAD_DIM = 64
PREFIX_LEN = 30
SEQ_LEN = 1024
SRC_MAX = 1024
SEQS_BLK = 1
MICRO = 2


eps = 1e-05


def exact_gelu(values):
    return jax.nn.gelu(values, approximate=False)


def norm_forward(residual, gain_row):
    centered = residual - jnp.mean(residual, axis=-1, keepdims=True)
    inv_std = lax.rsqrt(jnp.mean(centered * centered, axis=-1, keepdims=True) + eps)
    return centered * inv_std * gain_row


def norm_backward(upstream, residual, gain_row):
    centered = residual - jnp.mean(residual, axis=-1, keepdims=True)
    inv_std = lax.rsqrt(jnp.mean(centered * centered, axis=-1, keepdims=True) + eps)
    normed = centered * inv_std
    scaled = upstream * gain_row
    inner_mean = jnp.mean(scaled * normed, axis=-1, keepdims=True)
    return inv_std * (scaled - jnp.mean(scaled, axis=-1, keepdims=True) - normed * inner_mean)


def gelu_back(pre_act, upstream):
    return jax.vjp(exact_gelu, pre_act)[1](upstream)[0]


def matmul(left_mat, right_mat):
    return jnp.dot(left_mat, right_mat, preferred_element_type=jnp.float32)


def matmul_nt(left_mat, right_mat):
    return lax.dot_general(
        left_mat, right_mat, (((1,), (1,)), ((), ())), preferred_element_type=jnp.float32
    )


def matmul_tn(left_mat, right_mat):
    return lax.dot_general(
        left_mat, right_mat, (((0,), (0,)), ((), ())), preferred_element_type=jnp.float32
    )


def to_heads(rows_mat, seq_count, length):
    heads_here = rows_mat.shape[-1] // HEAD_DIM
    return rows_mat.reshape(seq_count, length, heads_here, HEAD_DIM).transpose(0, 2, 1, 3)


def from_heads(split_mat):
    seq_count, heads_here, length, head_width = split_mat.shape
    return split_mat.transpose(0, 2, 1, 3).reshape(seq_count * length, heads_here * head_width)


def causal_allowed():
    query_pos = lax.broadcasted_iota(jnp.int32, (SEQ_LEN, PREFIX_LEN + SEQ_LEN), 0)
    key_pos = lax.broadcasted_iota(jnp.int32, (SEQ_LEN, PREFIX_LEN + SEQ_LEN), 1)
    return (key_pos < PREFIX_LEN) | (key_pos - PREFIX_LEN <= query_pos)


def source_allowed(length):
    return lax.broadcasted_iota(jnp.int32, (SEQ_LEN, SRC_MAX), 1) < length


def attend_forward(queries, keys_all, values_all, allowed):
    scores = jnp.einsum("hqd,hkd->hqk", queries, keys_all, preferred_element_type=jnp.float32)
    scores = jnp.where(allowed, scores, -1e30)
    top_score = jnp.max(scores, axis=-1, keepdims=True)
    expo_scores = jnp.exp(scores - top_score)
    row_total = jnp.sum(expo_scores, axis=-1, keepdims=True)
    weights_low = (expo_scores / row_total).astype(jnp.bfloat16)
    mixed = jnp.einsum("hqk,hkd->hqd", weights_low, values_all, preferred_element_type=jnp.float32)
    return (mixed.astype(jnp.bfloat16), top_score + jnp.log(row_total))


def attend_backward(queries, keys_all, values_all, allowed, log_total, grad_out):
    scores = jnp.einsum("hqd,hkd->hqk", queries, keys_all, preferred_element_type=jnp.float32)
    scores = jnp.where(allowed, scores, -1e30)
    soft_weights = jnp.exp(scores - log_total)
    grad_soft = jnp.einsum("hqd,hkd->hqk", grad_out, values_all, preferred_element_type=jnp.float32)
    inner_sum = jnp.sum(soft_weights * grad_soft, axis=-1, keepdims=True)
    grad_scores = (soft_weights * (grad_soft - inner_sum)).astype(jnp.bfloat16)
    grad_query = jnp.einsum(
        "hqk,hkd->hqd", grad_scores, keys_all, preferred_element_type=jnp.float32
    )
    grad_keys = jnp.einsum("hqk,hqd->hkd", grad_scores, queries, preferred_element_type=jnp.float32)
    grad_values = jnp.einsum(
        "hqk,hqd->hkd",
        soft_weights.astype(jnp.bfloat16),
        grad_out,
        preferred_element_type=jnp.float32,
    )
    return (grad_query, grad_keys, grad_values)


def gather_rows(rows_low):
    return lax.all_gather(rows_low, "mp", axis=0, tiled=True)


def reduce_rows(term_fn, own_count):
    return lax.psum_scatter(
        term_fn(jnp.int32(0), own_count * lax.axis_size("mp")).astype(jnp.bfloat16),
        "mp",
        scatter_dimension=0,
        tiled=True,
    ).astype(jnp.float32)


def gather_adapter(rows_low):
    return lax.all_gather(rows_low, "adp", axis=0, tiled=True)


def reduce_adapter(term_fn, own_count):
    return lax.psum_scatter(
        term_fn(jnp.int32(0), own_count * lax.axis_size("adp")).astype(jnp.bfloat16),
        "adp",
        scatter_dimension=0,
        tiled=True,
    ).astype(jnp.float32)


def reduce_prefix(grad_prefix):
    return lax.psum(grad_prefix, ("dp", "adp"))


def reduce_adapter_grads(grad_down, grad_up):
    return (
        lax.psum_scatter(grad_down, ("dp", "mp"), scatter_dimension=0, tiled=True),
        lax.psum_scatter(grad_up, ("dp", "mp"), scatter_dimension=1, tiled=True),
    )


def shards(
    inputs,
    memory,
    src_lengths,
    self_qkv,
    self_proj,
    cross_qkv,
    cross_proj,
    ffn_in,
    ffn_out,
    norm_gains,
    prefix,
    adapter_down,
    adapter_up,
    cotangent,
):
    scale = HEAD_DIM ** (-0.5)
    own_rows = inputs.shape[2]
    gains = norm_gains.astype(jnp.float32)
    causal = causal_allowed()
    prefix_heads = to_heads(prefix, 2, PREFIX_LEN)
    prefix_keys = prefix_heads[0]
    prefix_values = prefix_heads[1]
    results = []
    input_grads = []
    memory_grads = []
    prefix_acc = None
    down_acc = None
    up_acc = None
    for micro_index in range(MICRO):
        self_w, self_o, cross_w, cross_o, down_w, up_w = (
            lax.all_gather(self_qkv, "dp", axis=1, tiled=True),
            lax.all_gather(self_proj, "dp", axis=1, tiled=True),
            lax.all_gather(cross_qkv, "dp", axis=1, tiled=True),
            lax.all_gather(cross_proj, "dp", axis=1, tiled=True),
            lax.all_gather(adapter_down, "dp", axis=0, tiled=True),
            lax.all_gather(adapter_up, "dp", axis=1, tiled=True),
        )
        ffn_first, ffn_second = (
            lax.all_gather(ffn_in, "dp", axis=0, tiled=True),
            lax.all_gather(ffn_out, "dp", axis=1, tiled=True),
        )
        x_rows = inputs[micro_index, 0]
        lengths_here = src_lengths[micro_index, 0]
        x_full = gather_rows(x_rows)
        mem_full = lax.all_gather(memory[micro_index, 0], "mp", axis=0, tiled=True)
        projected = jnp.einsum("td,cde->cte", x_full, self_w, preferred_element_type=jnp.float32)
        query_self = to_heads((projected[0] * scale).astype(jnp.bfloat16), SEQS_BLK, SEQ_LEN)
        key_self = to_heads(projected[1].astype(jnp.bfloat16), SEQS_BLK, SEQ_LEN)
        value_self = to_heads(projected[2].astype(jnp.bfloat16), SEQS_BLK, SEQ_LEN)

        def self_forward(packed):
            query_seq, key_seq, value_seq = packed
            keys_all = jnp.concatenate([prefix_keys, key_seq], axis=1)
            values_all = jnp.concatenate([prefix_values, value_seq], axis=1)
            return attend_forward(query_seq, keys_all, values_all, causal)

        attn_self, lse_self = lax.map(self_forward, (query_self, key_self, value_self))
        attn_rows = from_heads(attn_self)

        def self_term(first_row, row_count):
            return matmul(attn_rows, self_o)

        resid_one = x_rows.astype(jnp.float32) + reduce_rows(self_term, own_rows)
        normed_one = norm_forward(resid_one, gains[0])
        one_full = gather_rows(normed_one.astype(jnp.bfloat16))
        cross_query = to_heads(
            (matmul(one_full, cross_w[0]) * scale).astype(jnp.bfloat16), SEQS_BLK, SEQ_LEN
        )
        memory_proj = jnp.einsum(
            "td,cde->cte", mem_full, cross_w[1:], preferred_element_type=jnp.float32
        )
        cross_keys = to_heads(memory_proj[0].astype(jnp.bfloat16), SEQS_BLK, SRC_MAX)
        cross_values = to_heads(memory_proj[1].astype(jnp.bfloat16), SEQS_BLK, SRC_MAX)

        def cross_forward(packed):
            query_seq, key_seq, value_seq, length = packed
            return attend_forward(query_seq, key_seq, value_seq, source_allowed(length))

        attn_cross, lse_cross = lax.map(
            cross_forward, (cross_query, cross_keys, cross_values, lengths_here)
        )
        cross_rows = from_heads(attn_cross)

        def cross_term(first_row, row_count):
            return matmul(cross_rows, cross_o)

        resid_two = normed_one + reduce_rows(cross_term, own_rows)
        normed_two = norm_forward(resid_two, gains[1])
        two_low = normed_two.astype(jnp.bfloat16)
        two_full = gather_rows(two_low)
        hidden_pre = matmul(two_full, ffn_first)
        hidden_act = exact_gelu(hidden_pre).astype(jnp.bfloat16)

        def ffn_term(first_row, row_count):
            return matmul(hidden_act, ffn_second)

        ffn_rows = reduce_rows(ffn_term, own_rows)
        adapter_in = gather_adapter(two_low)
        adapter_pre = matmul(adapter_in, down_w)
        adapter_act = exact_gelu(adapter_pre).astype(jnp.bfloat16)

        def adapter_term(first_row, row_count):
            return matmul(adapter_act, up_w)

        adapter_rows = reduce_adapter(adapter_term, own_rows)
        resid_three = normed_two + ffn_rows + 4.0 * adapter_rows
        results.append(norm_forward(resid_three, gains[2]).astype(jnp.bfloat16))
        grad_three = norm_backward(
            cotangent[micro_index, 0].astype(jnp.float32), resid_three, gains[2]
        )
        grad_branch = grad_three.astype(jnp.bfloat16)
        grad_adapter = gather_adapter(grad_branch) * 4.0
        up_term = matmul_tn(adapter_act, grad_adapter)
        grad_adapter_pre = gelu_back(adapter_pre, matmul_nt(grad_adapter, up_w)).astype(
            jnp.bfloat16
        )
        down_term = matmul_tn(adapter_in, grad_adapter_pre)

        def adapter_back_term(first_row, row_count):
            return matmul_nt(grad_adapter_pre, down_w)

        adapter_back = reduce_adapter(adapter_back_term, own_rows)
        branch_full = gather_rows(grad_branch)
        grad_pre = gelu_back(hidden_pre, matmul_nt(branch_full, ffn_second)).astype(jnp.bfloat16)

        def ffn_back_term(first_row, row_count):
            return matmul_nt(grad_pre, ffn_first)

        ffn_back = reduce_rows(ffn_back_term, own_rows)
        grad_mid = norm_backward(grad_three + ffn_back + adapter_back, resid_two, gains[1])
        mid_full = gather_rows(grad_mid.astype(jnp.bfloat16))
        grad_cross_out = to_heads(
            matmul_nt(mid_full, cross_o).astype(jnp.bfloat16), SEQS_BLK, SEQ_LEN
        )

        def cross_backward(packed):
            query_seq, key_seq, value_seq, lse_seq, grad_seq, length = packed
            return attend_backward(
                query_seq, key_seq, value_seq, source_allowed(length), lse_seq, grad_seq
            )

        cross_gq, cross_gk, cross_gv = lax.map(
            cross_backward,
            (cross_query, cross_keys, cross_values, lse_cross, grad_cross_out, lengths_here),
        )
        cross_gq_rows = from_heads(cross_gq).astype(jnp.bfloat16) * scale

        def cross_query_term(first_row, row_count):
            return matmul_nt(cross_gq_rows, cross_w[0])

        grad_one = grad_mid + reduce_rows(cross_query_term, own_rows)
        memory_stack = jnp.stack(
            [from_heads(cross_gk).astype(jnp.bfloat16), from_heads(cross_gv).astype(jnp.bfloat16)]
        )
        memory_grads.append(
            lax.psum_scatter(
                jnp.einsum(
                    "cte,cde->td", memory_stack, cross_w[1:], preferred_element_type=jnp.float32
                ).astype(jnp.bfloat16),
                "mp",
                scatter_dimension=0,
                tiled=True,
            )
        )
        grad_first = norm_backward(grad_one, resid_one, gains[0])
        first_full = gather_rows(grad_first.astype(jnp.bfloat16))
        grad_self_out = to_heads(
            matmul_nt(first_full, self_o).astype(jnp.bfloat16), SEQS_BLK, SEQ_LEN
        )

        def self_backward(packed):
            query_seq, key_seq, value_seq, lse_seq, grad_seq = packed
            keys_all = jnp.concatenate([prefix_keys, key_seq], axis=1)
            values_all = jnp.concatenate([prefix_values, value_seq], axis=1)
            return attend_backward(query_seq, keys_all, values_all, causal, lse_seq, grad_seq)

        self_gq, self_gk, self_gv = lax.map(
            self_backward, (query_self, key_self, value_self, lse_self, grad_self_out)
        )
        prefix_key_grad = from_heads(jnp.sum(self_gk[:, :, :PREFIX_LEN], axis=0)[None])
        prefix_value_grad = from_heads(jnp.sum(self_gv[:, :, :PREFIX_LEN], axis=0)[None])
        prefix_term = jnp.stack([prefix_key_grad, prefix_value_grad])
        self_stack = jnp.stack(
            [
                from_heads(self_gq).astype(jnp.bfloat16) * scale,
                from_heads(self_gk[:, :, PREFIX_LEN:]).astype(jnp.bfloat16),
                from_heads(self_gv[:, :, PREFIX_LEN:]).astype(jnp.bfloat16),
            ]
        )

        def input_term(first_row, row_count):
            return jnp.einsum("cte,cde->td", self_stack, self_w, preferred_element_type=jnp.float32)

        input_grads.append((grad_first + reduce_rows(input_term, own_rows)).astype(jnp.bfloat16))
        prefix_term = reduce_prefix(prefix_term)
        down_term, up_term = reduce_adapter_grads(down_term, up_term)
        prefix_acc = prefix_term if prefix_acc is None else prefix_acc + prefix_term
        down_acc = down_term if down_acc is None else down_acc + down_term
        up_acc = up_term if up_acc is None else up_acc + up_term
    return (
        jnp.stack(results)[:, None],
        jnp.stack(input_grads)[:, None],
        jnp.stack(memory_grads)[:, None],
        prefix_acc,
        down_acc,
        up_acc,
    )


F32 = jnp.float32
BF = jnp.bfloat16
EPS = 1e-05
LOG2E = 1.4426950408889634
TILE = 256
FEED_SPLIT = 2

BQF = 512
BQ = 512
PRE = 32
VMEM_BYTES = 60 * 2**20
NEG = -1e30
HBM = pl.BlockSpec(memory_space=pl.ANY)
LN2 = 0.6931471805599453


def dot_mm(a, b, ca, cb):
    return lax.dot_general(a, b, (((ca,), (cb,)), ((), ())), preferred_element_type=jnp.float32)


def pick_head(h, mat):
    rows = lax.broadcasted_iota(jnp.int32, mat.shape, 0)
    return jnp.where((rows // HEAD_DIM) == h, mat, jnp.zeros_like(mat))


def attend_pair(causal, n, q, k, v, pk, pv, p_ref, pp_ref):
    t = q.shape[0]
    s = k.shape[0]
    nb = t // BQF
    qt = q.T
    vt = v.T
    ones = jnp.ones((16, s), jnp.bfloat16)
    work = [(h, j) for h in range(2) for j in range(nb)]

    def scores(h, j):
        kk = (j + 1) * BQF if causal else s
        qb = pick_head(h, qt[:, j * BQF:(j + 1) * BQF])
        return dot_mm(k[:kk], qb, 1, 0), dot_mm(pk, qb, 1, 0) if causal else None

    res = {}
    ahead = scores(*work[0])
    for w, (h, j) in enumerate(work):
        st, sp = ahead
        if w + 1 < len(work):
            ahead = scores(*work[w + 1])
        kk = st.shape[0]
        js = slice(j * BQF, (j + 1) * BQF)
        if causal:
            krow = lax.broadcasted_iota(jnp.int32, (BQF, BQF), 0)
            qcol = lax.broadcasted_iota(jnp.int32, (BQF, BQF), 1)
            diag = jnp.where(krow <= qcol, st[kk - BQF:], NEG)
            st = jnp.concatenate([st[:kk - BQF], diag], axis=0) if kk > BQF else diag
            prow = lax.broadcasted_iota(jnp.int32, sp.shape, 0)
            sp = jnp.where(prow < n, sp, NEG)
            m = jnp.maximum(jnp.max(st, axis=0, keepdims=True), jnp.max(sp, axis=0, keepdims=True))
            pp = jnp.exp2(sp - m).astype(jnp.bfloat16)
            pp_ref[h, :, js] = pp
        else:
            krow = lax.broadcasted_iota(jnp.int32, st.shape, 0)
            st = jnp.where(krow < n, st, NEG)
            m = jnp.max(st, axis=0, keepdims=True)
        p = jnp.exp2(st - m).astype(jnp.bfloat16)
        p_ref[h, :kk, js] = p
        hs = slice(h * HEAD_DIM, (h + 1) * HEAD_DIM)
        ot = dot_mm(jnp.concatenate([vt[hs, :kk], ones[:, :kk]], axis=0), p, 1, 0)
        if causal:
            ot += dot_mm(jnp.concatenate([pv.T[hs], ones[:, :PRE]], axis=0), pp, 1, 0)
        il = 1.0 / ot[HEAD_DIM:HEAD_DIM + 1]
        res[h, j] = (ot[:HEAD_DIM] * il, il)
    ils = [jnp.concatenate([res[h, j][1] for j in range(nb)], axis=1) for h in range(2)]
    at = jnp.concatenate([jnp.concatenate([res[h, j][0] for j in range(nb)], axis=1) for h in range(2)], axis=0)
    return at.astype(jnp.bfloat16).T, jnp.concatenate(ils, axis=0)


def sum_terms(keep_hbm, give_hbm, down_ref, up_ref, keep, part, first, second, third, fourth, out2, out3, out4, near, send, recv):
    g = pl.program_id(0)
    last = pl.num_programs(0) - 1
    dp, y, z, side, over, up = axes_here()
    nz = lax.axis_size("adp")
    rows = part.shape[1] // nz
    wide = out3.shape[2]

    def far(src, dst, peer, i):
        return pltpu.make_async_remote_copy(src_ref=src, dst_ref=dst, send_sem=send.at[i], recv_sem=recv.at[i],
                                            device_id=peer, device_id_type=pl.DeviceIdType.MESH)

    load = pltpu.make_async_copy(keep_hbm, keep, near.at[0])
    core = far(give_hbm, first, side, 0)
    across = far(out2, second, over, 1)
    beside = far(out3, third, up, 2)
    along = [far(out4.at[k - 1], fourth.at[k - 1], {"adp": lax.rem(z + nz - k, nz)}, 2 + k) for k in range(1, nz)]

    @pl.when(g == 0)
    def _():
        meet([side, over, up] + [{"adp": lax.rem(z + k, nz)} for k in range(1, nz)])
        load.start()
        core.start()

    @pl.when(g == 1)
    def _():
        load.wait()
        core.wait_recv()
        out2[...] = (keep[:, 1] + first[:, 1].astype(jnp.float32)).astype(jnp.bfloat16)
        across.start()

    @pl.when(g == last // 2 + 1)
    def _():
        across.wait_recv()
        keep[:, 0] = keep[:, 0] + first[:, 0].astype(jnp.float32) + second[...].astype(jnp.float32)
        mine = pl.ds(pl.multiple_of(y * wide, wide), wide)
        other = pl.ds(pl.multiple_of((1 - y) * wide, wide), wide)
        out3[...] = keep[:, 0, :, other].astype(jnp.bfloat16)
        part[...] = keep[:, 0, :, mine]
        beside.start()

    @pl.when(g == last - 1)
    def _():
        beside.wait_recv()
        part[...] = part[...] + third[...].astype(jnp.float32)
        for k in range(1, nz):
            out4[k - 1] = part[:, k * rows:(k + 1) * rows].astype(jnp.bfloat16)
            along[k - 1].start()

    @pl.when(g == last)
    def _():
        total = part[:, :rows]
        for k in range(1, nz):
            along[k - 1].wait_recv()
            total = total + fourth[k - 1].astype(jnp.float32)
        down_ref[...] = total[0].T
        up_ref[...] = total[1]
        for c in [core, across, beside] + along:
            c.wait_send()


def attn_bwd_body(causal, q_ref, k_ref, v_ref, a_ref, da_ref, l_ref, p_ref, *rest):
    if causal:
        pp_ref, pre_ref, moved, _, dq_ref, dk_ref, dv_ref, dpre_ref, landed, sems = rest
        y = lax.axis_index("mp")
        carry = pltpu.make_async_remote_copy(
            src_ref=moved, dst_ref=landed.at[y], send_sem=sems.at[0], recv_sem=sems.at[1],
            device_id={"mp": 1 - y}, device_id_type=pl.DeviceIdType.MESH)

        @pl.when(pl.program_id(0) == 0)
        def _():
            meet([{"mp": 1 - y}])
            carry.start()
    else:
        pp_ref, pre_ref, dpre_ref = None, None, None
        keep_ref, give_ref, dq_ref, dk_ref, dv_ref, down_ref, up_ref = rest[:7]
        sum_terms(keep_ref, give_ref, down_ref, up_ref, *rest[7:])
    t = q_ref.shape[0]
    s = k_ref.shape[0]
    nb = t // BQ
    qt = q_ref[...].T
    kt = k_ref[...].T
    dat = da_ref[...].T.astype(jnp.float32)
    prod = dat * a_ref[...].T.astype(jnp.float32)
    pkt = pre_ref[0].T if causal else None
    work = [(h, j) for h in range(2) for j in range(nb)]
    head = {}
    for h in range(2):
        hs = slice(h * HEAD_DIM, (h + 1) * HEAD_DIM)
        il = l_ref[0, h:h + 1]
        head[h] = ((dat * il).astype(jnp.bfloat16), jnp.sum(prod[hs], axis=0, keepdims=True) * il)

    def soft_grad(h, j):
        js = slice(j * BQ, (j + 1) * BQ)
        kk = (j + 1) * BQ if causal else s
        dab = pick_head(h, head[h][0][:, js])
        return dot_mm(v_ref[:kk], dab, 1, 0), dot_mm(pre_ref[1], dab, 1, 0) if causal else None

    def add(tot, new):
        return new if tot is None else tot + new

    res = {}
    dpk = [None, None]
    dpv = [None, None]
    dkb = [[None] * nb, [None] * nb]
    dvb = [[None] * nb, [None] * nb]
    ahead = soft_grad(*work[0])
    for w, (h, j) in enumerate(work):
        dp, dpp = ahead
        if w + 1 < len(work):
            ahead = soft_grad(*work[w + 1])
        hs = slice(h * HEAD_DIM, (h + 1) * HEAD_DIM)
        js = slice(j * BQ, (j + 1) * BQ)
        kk = dp.shape[0]
        dl = head[h][1][:, js]
        dah = head[h][0][hs, js]
        p = p_ref[h, :kk, js]
        ds = (p.astype(jnp.float32) * (dp - dl)).astype(jnp.bfloat16)
        dq = dot_mm(kt[hs, :kk], ds, 1, 0)
        if causal:
            pp = pp_ref[h, :, js]
            dsp = (pp.astype(jnp.float32) * (dpp - dl)).astype(jnp.bfloat16)
            dq += dot_mm(pkt[hs], dsp, 1, 0)
            dpk[h] = add(dpk[h], dot_mm(qt[hs, js], dsp, 1, 1))
            dpv[h] = add(dpv[h], dot_mm(dah, pp, 1, 1))
        res[h, j] = dq
        dv = dot_mm(dah, p, 1, 1)
        dk = dot_mm(qt[hs, js], ds, 1, 1)
        if causal:
            for i in range(kk // BQ):
                dvb[h][i] = add(dvb[h][i], dv[:, i * BQ:(i + 1) * BQ])
                dkb[h][i] = add(dkb[h][i], dk[:, i * BQ:(i + 1) * BQ])
        else:
            dvb[h] = [add(dvb[h][0], dv)]
            dkb[h] = [add(dkb[h][0], dk)]
    both = lambda f: jnp.concatenate([f(0), f(1)], axis=0)
    dq_ref[...] = (both(lambda h: jnp.concatenate([res[h, j] for j in range(nb)], axis=1))
                   * HEAD_DIM ** -0.5).astype(jnp.bfloat16).T
    dk_ref[...] = (both(lambda h: jnp.concatenate(dkb[h], axis=1)) * LN2).astype(jnp.bfloat16).T
    dv_ref[...] = both(lambda h: jnp.concatenate(dvb[h], axis=1)).astype(jnp.bfloat16).T
    if causal:
        dpre_ref[0] = both(lambda h: dpk[h]).T * LN2
        dpre_ref[1] = both(lambda h: dpv[h]).T

        @pl.when(pl.program_id(0) == pl.num_programs(0) - 1)
        def _():
            carry.wait()


def attn_bwd(q, k, v, a, da, il, p, pp=None, pre=None, moved=None, landed=None, keep=None, give=None):
    t, w = q.shape
    s = k.shape[0]
    pairs = w // 128
    causal = pre is not None
    col = lambda g: (0, g)
    lead = lambda g: (g, 0, 0)
    tail = lambda g: (0, 0, g)
    fixed = lambda g: (0, 0)
    f32, bf = jnp.float32, jnp.bfloat16
    vm = pltpu.VMEM
    if not causal:
        nz = lax.axis_size("adp")
        bott = keep.shape[2]
        rows, wide = bott // nz, TILE // 2
    return pl.pallas_call(
        functools.partial(attn_bwd_body, causal),
        grid=(pairs,),
        in_specs=[
            pl.BlockSpec((t, 128), col), pl.BlockSpec((s, 128), col), pl.BlockSpec((s, 128), col),
            pl.BlockSpec((t, 128), col), pl.BlockSpec((t, 128), col),
            pl.BlockSpec((1, 2, t), lead), pl.BlockSpec((2, s, t), lead),
        ] + ([pl.BlockSpec((2, PRE, t), lead), pl.BlockSpec((2, PRE, 128), tail), HBM, HBM] if causal else [HBM, HBM]),
        out_specs=[
            pl.BlockSpec((t, 128), col), pl.BlockSpec((s, 128), col), pl.BlockSpec((s, 128), col),
        ] + ([pl.BlockSpec((2, PRE, 128), tail), HBM] if causal else [pl.BlockSpec((rows, wide), fixed)] * 2),
        out_shape=[
            jax.ShapeDtypeStruct((t, w), bf), jax.ShapeDtypeStruct((s, w), bf), jax.ShapeDtypeStruct((s, w), bf),
        ] + ([jax.ShapeDtypeStruct((2, PRE, w), f32), jax.ShapeDtypeStruct(landed.shape, bf)] if causal
           else [jax.ShapeDtypeStruct((rows, wide), f32)] * 2),
        scratch_shapes=[pltpu.SemaphoreType.DMA((2,))] if causal else [
            vm(keep.shape, f32), vm((2, bott, wide), f32), vm(keep.shape, bf), vm((2, bott, TILE), bf), vm((2, bott, wide), bf),
            vm((nz - 1, 2, rows, wide), bf), vm((2, bott, TILE), bf), vm((2, bott, wide), bf), vm((nz - 1, 2, rows, wide), bf),
            pltpu.SemaphoreType.DMA((1,)), pltpu.SemaphoreType.DMA((nz + 2,)), pltpu.SemaphoreType.DMA((nz + 2,))],
        input_output_aliases={10: 4} if causal else {},
        compiler_params=pltpu.CompilerParams(
            vmem_limit_bytes=VMEM_BYTES, collective_id=3 if causal else 5, has_side_effects=True),
        cost_estimate=pl.CostEstimate(flops=40 * t * s * w, bytes_accessed=4 * t * s * pairs, transcendentals=0),
    )(q, k, v, a, da, il, p, *((pp, pre, moved, landed) if causal else (keep, give)))


def gelu_pair(v):
    x = 1.0 + (0.3275911 * 0.5 ** 0.5) * jnp.abs(v)
    t = pl.reciprocal(x, approx=True)
    t = t * (2.0 - x * t)
    expo = jnp.exp2(v * v * (-0.5 * LOG2E))
    poly = 0.127414796 + t * (-0.142248368 + t * (0.7107068705 + t * (-0.7265760135 + t * 0.5307027145)))
    half = poly * t * expo
    cdf = jnp.where(v < 0.0, half, 1.0 - half)
    return v * cdf, cdf + v * expo * (2.0 * math.pi) ** -0.5


def normalize(z):
    centered = z - jnp.mean(z, axis=-1, keepdims=True)
    inv = lax.rsqrt(jnp.mean(centered * centered, axis=-1, keepdims=True) + EPS)
    return centered * inv, inv


def norm_back(e, u, inv, gain):
    w = e * gain
    return inv * (w - jnp.mean(w, axis=-1, keepdims=True) - u * jnp.mean(w * u, axis=-1, keepdims=True))


def stack_rows(refs):
    return jnp.concatenate([r[...] for r in refs], axis=0)


def stack_cols(refs):
    return jnp.concatenate([r[...] for r in refs], axis=1)


def nn(lhs, tiles):
    return dot_mm(lhs, stack_rows(tiles), 1, 0)


def nt(lhs, tiles):
    return dot_mm(lhs, stack_cols(tiles), 1, 1)


def place_cols(value_ref, dp):
    n = value_ref.shape[1] // TILE
    return jnp.concatenate(
        [value_ref[:, pl.ds(pl.multiple_of((dp ^ r) * TILE, TILE), TILE)] for r in range(n)], axis=1)


def unplace_store(out, value, dp):
    for r in range(value.shape[1] // TILE):
        out[:, pl.ds(pl.multiple_of((dp ^ r) * TILE, TILE), TILE)] = (
            value[:, r * TILE:(r + 1) * TILE].astype(out.dtype))


class Exchange:
    def __init__(self, buf, out, local, send, recv, half):
        self.refs = buf, out, local, send, recv
        self.count, self.tile = buf.shape[0], buf.shape[1]
        self.half = half
        self.y = lax.axis_index("mp")

    def copies(self, i):
        buf, out, local, send, recv = self.refs
        rows = pl.ds(i * self.tile % self.half, self.tile)
        dst = out.at[self.y, rows]
        far = pltpu.make_async_remote_copy(src_ref=buf.at[i], dst_ref=dst, send_sem=send.at[i], recv_sem=recv.at[i],
                                           device_id={"mp": 1 - self.y}, device_id_type=pl.DeviceIdType.MESH)
        return pltpu.make_async_copy(buf.at[i], dst, local.at[i]), far

    def here(self, i):
        return self.y == i * self.tile // self.half

    def buffer(self, i):
        return self.refs[0].at[i]

    def send(self, i):
        near, far = self.copies(i)

        @pl.when(self.here(i))
        def _():
            near.start()

        @pl.when(jnp.logical_not(self.here(i)))
        def _():
            far.start()

    def finish(self):
        for i in range(self.count):
            near, far = self.copies(i)

            @pl.when(self.here(i))
            def _():
                near.wait()
                far.wait_recv()

            @pl.when(jnp.logical_not(self.here(i)))
            def _():
                far.wait_send()


def tiled(weights, rows, consts, outs, body, tile, steps, exchange=None, scratch=(), flops=0):
    nw, nr, nc, no = len(weights), len(rows), len(consts), len(outs)
    picks = [c for _, _, c in weights]
    piece = [own.shape if c is None else own.shape[1:] for own, _, c in weights]
    more = 1 if exchange else 0

    def kernel(*refs):
        srcs, refs = refs[:2 * nw], refs[2 * nw:]
        row_refs, const_refs, out_refs = refs[:nr], refs[nr:nr + nc], refs[nr + nc:nr + nc + no]
        refs = refs[nr + nc + no:]
        result, refs = refs[:more], refs[more:]
        wv, sems, refs = refs[:nw], refs[nw], refs[nw + 1:]
        step = pl.program_id(0)
        ex = Exchange(refs[0], result[0], *refs[1:4], exchange[1]) if exchange else None
        own_scratch = refs[4 * more:]

        def copies(i):
            own, far, c = srcs[2 * i], srcs[2 * i + 1], picks[i]
            own = own if c is None else own.at[c]
            some = lambda s, rs: far.at[s, rs] if c is None else far.at[s, rs, c]
            yield pltpu.make_async_copy(own, wv[i].at[0, 0], sems.at[i, 0])
            yield pltpu.make_async_copy(some(0, pl.ds(1, 3)), wv[i].at[0, pl.ds(1, 3)], sems.at[i, 1])
            yield pltpu.make_async_copy(some(1, pl.ds(0, 4)), wv[i].at[1], sems.at[i, 2])

        @pl.when(step == 0)
        def _():
            for i in range(nw):
                for copy in copies(i):
                    copy.start()
            if exchange:
                meet([{"mp": 1 - lax.axis_index("mp")}])

        def need(i):
            @pl.when(step == 0)
            def _():
                for copy in copies(i):
                    copy.wait()

        def put(value):
            dp = lax.axis_index("dp")
            unplace_store(ex.buffer(step), value, dp)
            for i in range(steps):
                @pl.when(step == i)
                def _():
                    ex.send(i)

        body(wv, need, row_refs, const_refs, out_refs, own_scratch, put)
        if exchange:
            @pl.when(step == steps - 1)
            def _():
                ex.finish()

    whole = lambda a: pl.BlockSpec(a.shape, lambda i: (0,) * a.ndim, pipeline_mode=pl.Buffered(1))
    ex_out, ex_shape, ex_scratch = [], [], []
    if exchange:
        _, half, cols = exchange
        ex_out, ex_shape = [HBM], [jax.ShapeDtypeStruct((2, half, cols), BF)]
        ex_scratch = [pltpu.VMEM((steps, tile, cols), BF)] + [pltpu.SemaphoreType.DMA((steps,))] * 3
    return pl.pallas_call(
        kernel,
        grid=(steps,),
        in_specs=[HBM] * (2 * nw) + [spec for _, spec in rows] + [whole(c) for c in consts],
        out_specs=[pl.BlockSpec(shape, index) for _, _, shape, index in outs] + ex_out,
        out_shape=[jax.ShapeDtypeStruct(shape, dtype) for shape, dtype, _, _ in outs] + ex_shape,
        scratch_shapes=[pltpu.VMEM((2, 4) + tuple(p), BF) for p in piece] + [pltpu.SemaphoreType.DMA((nw, 3))]
        + ex_scratch + list(scratch),
        compiler_params=pltpu.CompilerParams(
            vmem_limit_bytes=VMEM_BYTES, **(dict(collective_id=exchange[0], has_side_effects=True) if exchange else {})),
        cost_estimate=pl.CostEstimate(flops=flops, bytes_accessed=16 * 2**20, transcendentals=0),
    )(*[a for own, far, _ in weights for a in (own, far)], *[r[0] for r in rows], *consts)


def last_gradient(wq, dz1, dq, dk, dv, dpre, own_w):
    t, d = dz1.shape
    half = t // 2
    nz = lax.axis_size("adp")
    tile = half // 2
    count = t // tile
    hw = d // 2

    def kernel(wq_ref, dz_ref, dq_ref, dk_ref, dv_ref, dpre_ref, out, sum_ref,
               wv, zv, lv, buf, pv, got, tot, zbuf, sems, local, send, recv, psend, precv):
        dp, y, z, side, over, up = axes_here()
        along = [{"adp": lax.rem(z + k, nz)} for k in range(1, nz)]

        def rows_of(i):
            return pl.multiple_of(jnp.where(i < count // 2, 1 - y, y) * half + (i % 2) * tile, tile)

        def loads(i):
            rows = pl.ds(rows_of(i), tile)
            yield pltpu.make_async_copy(dz_ref.at[rows], zv.at[i], sems.at[4 * i])
            for c, ref in enumerate((dq_ref, dk_ref, dv_ref)):
                yield pltpu.make_async_copy(ref.at[rows], lv.at[i, :, pl.ds(c * d, d)], sems.at[4 * i + 1 + c])

        weight = pltpu.make_async_copy(wq_ref, wv, sems.at[4 * count])
        pre = pltpu.make_async_copy(dpre_ref, pv, sems.at[4 * count + 1])
        pre.start()
        weight.start()
        for i in range(count):
            for c in loads(i):
                c.start()
        meet([side, over, up] + along)

        def far(src, dst, peer, i):
            return pltpu.make_async_remote_copy(src_ref=src, dst_ref=dst, send_sem=psend.at[i], recv_sem=precv.at[i],
                                                device_id=peer, device_id_type=pl.DeviceIdType.MESH)

        first = far(pv.at[:, :, pl.ds(hw, hw)], got.at[0], up, 0)
        second = far(tot.at[0], got.at[1], side, 1)
        third = far(tot.at[1], got.at[2], over, 2)
        ring = [far(zbuf.at[z], zbuf.at[z], peer, 3 + k) for k, peer in enumerate(along)]

        def fold(k):
            if k == 0:
                first.wait_recv()
                tot[0] = pv[:, :, :hw] + got[0]
                second.start()
            elif k == 1:
                second.wait_recv()
                tot[1] = tot[0] + got[1]
                third.start()
            elif k == 2:
                third.wait_recv()
                zbuf[z] = tot[1] + got[2]
                for c in ring:
                    c.start()
            else:
                for c in ring:
                    c.wait_recv()
                total = zbuf[0]
                for j in range(1, nz):
                    total = total + zbuf[j]
                sum_ref[...] = total

        pre.wait()
        first.start()
        weight.wait()
        moves = []
        for i in range(count):
            for c in loads(i):
                c.wait()
            lhs = lv[i]
            e = jnp.concatenate(
                [dot_mm(lhs, jnp.concatenate([wv[s, r, c] for c in range(3) for s in range(2)], axis=1), 1, 1)
                 for r in range(d // TILE)], axis=1)
            unplace_store(buf.at[i], zv[i] + e, dp)
            dst = out.at[y, pl.ds((i % 2) * tile, tile)]
            if i < count // 2:
                move = pltpu.make_async_remote_copy(
                    src_ref=buf.at[i], dst_ref=dst, send_sem=send.at[i], recv_sem=recv.at[i],
                    device_id=up, device_id_type=pl.DeviceIdType.MESH)
            else:
                move = pltpu.make_async_copy(buf.at[i], dst, local.at[i])
            move.start()
            moves.append(move)
            if 1 <= i:
                fold(i - 1)
        fold(3)
        for c in [first, second, third] + ring:
            c.wait_send()
        for c in moves:
            c.wait()

    vm = pltpu.VMEM
    shape = jax.ShapeDtypeStruct
    dma = pltpu.SemaphoreType.DMA
    return pl.pallas_call(
        kernel,
        in_specs=[HBM] * 6,
        out_specs=[HBM, pl.BlockSpec(memory_space=pltpu.VMEM)],
        out_shape=[shape((2, half, d), BF), shape((2, PRE, hw), F32)],
        scratch_shapes=[vm(wq.shape, BF), vm((count, tile, d), F32), vm((count, tile, 3 * d), BF), vm((count, tile, d), BF),
                        vm((2, PRE, d), F32), vm((3, 2, PRE, hw), F32), vm((2, 2, PRE, hw), F32), vm((nz, 2, PRE, hw), F32),
                        dma((4 * count + 2,)), dma((count,)), dma((count,)), dma((count,)), dma((2 + nz,)), dma((2 + nz,))],
        compiler_params=pltpu.CompilerParams(collective_id=4, has_side_effects=True, vmem_limit_bytes=VMEM_BYTES),
        cost_estimate=pl.CostEstimate(flops=6 * t * d * d, bytes_accessed=2**24, transcendentals=0),
    )(wq, dz1, dq, dk, dv, dpre)


def by_rows(ref):
    return lambda s, r, j: ref.at[s, r, pl.ds(j * TILE, TILE)]


def by_cols(ref):
    return lambda s, r, j: ref.at[s, r, slice(None), pl.ds(j * TILE, TILE)]


def meet(peers):
    barrier = pltpu.get_barrier_semaphore()
    for peer in peers:
        pl.semaphore_signal(barrier, inc=1, device_id=peer, device_id_type=pl.DeviceIdType.MESH)
    pl.semaphore_wait(barrier, len(peers))


class Moves:
    def __init__(self, table, send, recv, local):
        self.table, self.send, self.recv, self.local = table, send, recv, local
        self.place = {}
        far = near = 0
        for name, (src, dst, peer) in table.items():
            if peer is None:
                self.place[name] = near
                near += 1
            else:
                self.place[name] = far
                far += 1

    def copy(self, name):
        src, dst, peer = self.table[name]
        i = self.place[name]
        if peer is None:
            return pltpu.make_async_copy(src, dst, self.local.at[i])
        return pltpu.make_async_remote_copy(src_ref=src, dst_ref=dst, send_sem=self.send.at[i], recv_sem=self.recv.at[i],
                                            device_id=peer, device_id_type=pl.DeviceIdType.MESH)

    def start(self, *names):
        for name in names:
            self.copy(name).start()

    def got(self, *names):
        for name in names:
            if self.table[name][2] is None:
                self.copy(name).wait()
            else:
                self.copy(name).wait_recv()

    def sent(self, *names):
        for name in names:
            self.copy(name).wait_send()


def axes_here():
    dp, y, z = lax.axis_index("dp"), lax.axis_index("mp"), lax.axis_index("adp")
    return dp, y, z, {"dp": dp ^ 1}, {"dp": dp ^ 2}, {"mp": 1 - y}


SPOTS = {"x": (0, 2), "y": (1, 0), "d": (1, 2)}


def plane_moves(table, tag, own, far, part, side, over, up):
    table[tag, "y"] = (part(own), part(far(1, 0)), up)
    table[tag, "x"] = (part(own), part(far(0, 2)), over)
    table[tag, "d"] = (part(far(1, 0)), part(far(1, 2)), over)
    for spot in "xyd":
        s, r = SPOTS[spot]
        table[tag, spot, "side"] = (part(far(s, r)), part(far(s, r ^ 1)), side)


def ring_moves(table, tag, own, far, quarter, z, nz, side, over, up, onward):
    first = quarter(z)
    table[tag, "y"] = (first(own), first(far(1, 0)), up)
    table[tag, "x"] = (first(own), first(far(0, 2)), over)
    table[tag, "d"] = (first(far(1, 0)), first(far(1, 2)), over)
    for spot in "xyd":
        s, r = SPOTS[spot]
        for k in range(nz):
            part = quarter(lax.rem(z + nz - k, nz))
            table[tag, spot, k, "side"] = (part(far(s, r)), part(far(s, r ^ 1)), side)
            if k + 1 < nz:
                table[tag, spot, k, "on"] = (part(far(s, r)), part(far(s, r)), onward)


def self_forward(inputs, memory, self_qkv, self_proj, cross_qkv, cross_proj, pre_own, ad_own):
    _, _, half, d = inputs.shape
    t = 2 * half
    nq, wrows, hw = self_qkv.shape
    nz = lax.axis_size("adp")
    prow = self_proj.shape[0]
    pairs = d // 128
    chunks = d // TILE
    qscale = HEAD_DIM ** -0.5 * LOG2E
    ring_tags = ("cq12", "co")
    plane_tags = ("so", "cq0")

    def moves(refs):
        (in_ref, mem_ref, own_ref, so_ref, cq_ref, co_ref, pre_ref, ad_ref,
         q_out, k_out, v_out, w_out, x_out, pre_out, bso, bcq, bco, mem_out, ada_ref, wv, xv, qs, ks, vs, pv) = refs
        dp, y, z, side, over, up = axes_here()
        onward = {"adp": lax.rem(z + 1, nz)}
        along = [{"adp": lax.rem(z + k, nz)} for k in range(1, nz)]
        rows = pl.ds(pl.multiple_of(y * half, half), half)
        table = {}
        table["w own"] = (own_ref, wv.at[0, 0], None)
        table["pre own"] = (pre_ref, pv.at[:, :, pl.ds(0, hw)], None)
        table["x own"] = (in_ref.at[y, 0], xv.at[rows], None)
        table["x up"] = (in_ref.at[1 - y, 0], xv.at[rows], up)
        table["pre up"] = (pre_ref, pv.at[:, :, pl.ds(hw, hw)], up)
        table["w", "side"] = (own_ref, wv.at[0, 1], side)
        table["w", "x"] = (own_ref, wv.at[0, 2], over)
        table["w", "x", "side"] = (wv.at[0, 2], wv.at[0, 3], side)
        quarter = lambda k: (slice(None), pl.ds(pl.multiple_of(lax.rem(z + nz - k, nz) * (wrows // nz), wrows // nz), wrows // nz))
        table["w", "y"] = (own_ref.at[quarter(0)], wv.at[(1, 0) + quarter(0)], up)
        for k in range(nz):
            beside, diagonal = wv.at[(1, 0) + quarter(k)], wv.at[(1, 2) + quarter(k)]
            table["w", "y", k, "side"] = (beside, wv.at[(1, 1) + quarter(k)], side)
            table["w", "d", k] = (beside, diagonal, over)
            table["w", "d", k, "side"] = (diagonal, wv.at[(1, 3) + quarter(k)], side)
            if k + 1 < nz:
                table["w", "y", k, "on"] = (beside, beside, onward)
        for k in range(1, nz):
            table["ad", k] = (ad_ref, ada_ref.at[k], along[k - 1])
        plane_moves(table, "so", so_ref, lambda s, r: bso.at[s, r], lambda ref: ref, side, over, up)
        plane_moves(table, "cq0", cq_ref, lambda s, r: bcq.at[s, r], lambda ref: ref.at[0], side, over, up)
        ring_moves(table, "cq12", cq_ref, lambda s, r: bcq.at[s, r],
                   lambda qz: lambda ref: ref.at[pl.ds(1, 2), pl.ds(pl.multiple_of(qz * (wrows // nz), wrows // nz), wrows // nz)],
                   z, nz, side, over, up, onward)
        ring_moves(table, "co", co_ref, lambda s, r: bco.at[s, r],
                   lambda qz: lambda ref: ref.at[pl.ds(pl.multiple_of(qz * (prow // nz), prow // nz), prow // nz)],
                   z, nz, side, over, up, onward)
        table["so", "side"] = (so_ref, bso.at[0, 1], side)
        table["cq", "side"] = (cq_ref, bcq.at[0, 1], side)
        table["co", "side"] = (co_ref, bco.at[0, 1], side)
        table["mem up"] = (mem_ref.at[1 - y, 0], mem_out, up)
        for name, s_, o_ in (("q", qs, q_out), ("k", ks, k_out), ("v", vs, v_out), ("w", wv, w_out), ("x", xv, x_out), ("pre", pv, pre_out)):
            table[name + " out"] = (s_, o_, None)
        return table, (side, over, up), along

    def count():
        rings = len(ring_tags) * (3 + 3 * nz + 3 * (nz - 1))
        planes = len(plane_tags) * 6
        return 1 + 1 + 4 + 4 * nz - 1 + planes + rings + (nz - 1) + 3 + 1, 9

    def kernel(in_ref, mem_ref, own_ref, so_ref, cq_ref, co_ref, pre_ref, ad_ref,
               a_ref, p_ref, pp_ref, l_ref, q_out, k_out, v_out, w_out, x_out, pre_out, bso, bcq, bco, mem_out, ada_ref,
               wv, xv, qs, ks, vs, pv, send, recv, local):
        g = pl.program_id(0)
        table, near_peers, along = moves((in_ref, mem_ref, own_ref, so_ref, cq_ref, co_ref, pre_ref, ad_ref,
                                          q_out, k_out, v_out, w_out, x_out, pre_out, bso, bcq, bco, mem_out, ada_ref,
                                          wv, xv, qs, ks, vs, pv))
        mv = Moves(table, send, recv, local)
        done = set()

        def got(*names):
            done.update(names)
            mv.got(*names)

        ads = [("ad", k) for k in range(1, nz)]
        outs = [n + " out" for n in ("q", "k", "v", "w", "x", "pre")]

        def pass_on(spot, k):
            if k >= nz:
                return
            for tag in ring_tags:
                got((tag, spot) if k == 0 else (tag, spot, k - 1, "on"))
                if k + 1 < nz:
                    mv.start((tag, spot, k, "on"))
                mv.start((tag, spot, k, "side"))

        @pl.when(g == 0)
        def _():
            meet(list(near_peers) + along)
            mv.start(("w", "y"), ("w", "x"), "pre up")
            mv.start(*[(tag, spot) for tag in ring_tags for spot in "yx"])
            mv.start("x up", *[(tag, "y") for tag in plane_tags])
            mv.start("mem up", ("w", "side"), "w own", "pre own", "x own")
            for k in range(nz):
                got(("w", "y") if k == 0 else ("w", "y", k - 1, "on"))
                if k + 1 < nz:
                    mv.start(("w", "y", k, "on"))
                mv.start(("w", "d", k), ("w", "y", k, "side"))
            pass_on("y", 0)
            pass_on("x", 0)
            mv.start(*[(tag, "d") for tag in ring_tags])
            mv.start(*[(tag, "x") for tag in plane_tags])
            got(("w", "x"))
            mv.start(("w", "x", "side"), ("so", "side"), ("cq", "side"), ("co", "side"))
            for k in range(nz):
                if 0 < k < nz - 1:
                    pass_on("y", k)
                    pass_on("x", k)
                got(("w", "d", k))
                mv.start(("w", "d", k, "side"))
            got("w own", "pre own", "pre up", "x own", "x up", ("w", "side"), ("w", "x", "side"))
            for k in range(nz):
                got(("w", "y", k, "side"), ("w", "d", k, "side"))
            for i in range(2):
                x = place_cols(xv.at[pl.ds(i * half, half)], lax.axis_index("dp"))
                for c, out in ((0, qs), (1, ks), (2, vs)):
                    for s in range(2):
                        w = jnp.concatenate([wv[s, r, c] for r in range(4)], axis=0)
                        o = dot_mm(x, w, 1, 0)
                        out[i * half:(i + 1) * half, s * hw:(s + 1) * hw] = (o * qscale if c == 0 else o).astype(BF)
                if i == 0:
                    pass_on("d", 0)
            if nz > 1:
                pass_on("y", nz - 1)
                pass_on("x", nz - 1)
            pass_on("d", 1)
            mv.start(*outs)

        for k in range(2, nz):
            @pl.when(g == 2 * (k - 1))
            def _():
                pass_on("d", k)
                if k == 2:
                    mv.start(*ads)

        @pl.when(g == 3)
        def _():
            for tag in plane_tags:
                got((tag, "y"), (tag, "x"))
                mv.start((tag, "d"), (tag, "y", "side"), (tag, "x", "side"))

        @pl.when(g > 0)
        def _():
            cs = pl.ds(pl.multiple_of((g - 1) * 128, 128), 128)
            a, il = attend_pair(True, PREFIX_LEN, qs[:, cs], ks[:, cs], vs[:, cs], pv[0, :, cs], pv[1, :, cs], p_ref, pp_ref)
            a_ref[...] = a
            l_ref[0] = il

        @pl.when(g == pairs)
        def _():
            for tag in plane_tags:
                got((tag, "d"))
                mv.start((tag, "d", "side"))
            far = [n for n, (_, _, peer) in table.items() if peer is not None]
            got(*[n for n in far if n not in done])
            got(*outs)
            mv.sent(*far)

    lead = lambda g: (jnp.maximum(g - 1, 0), 0, 0)
    col = lambda g: (0, jnp.maximum(g - 1, 0))
    shape = jax.ShapeDtypeStruct
    remotes, near = count()
    vm = pltpu.VMEM
    return pl.pallas_call(
        kernel,
        grid=(pairs + 1,),
        in_specs=[HBM] * 8,
        out_specs=[pl.BlockSpec((t, 128), col), pl.BlockSpec((2, t, t), lead), pl.BlockSpec((2, PRE, t), lead),
                   pl.BlockSpec((1, 2, t), lead)] + [HBM] * 11,
        out_shape=[
            shape((t, d), BF), shape((2 * pairs, t, t), BF), shape((2 * pairs, PRE, t), BF), shape((pairs, 2, t), F32),
            shape((t, d), BF), shape((t, d), BF), shape((t, d), BF), shape((2, 4) + self_qkv.shape, BF),
            shape((t, d), BF), shape((2, PRE, d), BF), shape((2, 4) + self_proj.shape, BF), shape((2, 4) + cross_qkv.shape, BF),
            shape((2, 4) + cross_proj.shape, BF), shape((half, d), BF), shape((nz,) + ad_own.shape, BF),
        ],
        scratch_shapes=[vm((2, 4) + self_qkv.shape, BF), vm((t, d), BF), vm((t, d), BF), vm((t, d), BF), vm((t, d), BF),
                        vm((2, PRE, d), BF), pltpu.SemaphoreType.DMA((remotes,)),
                        pltpu.SemaphoreType.DMA((remotes,)), pltpu.SemaphoreType.DMA((near,))],
        compiler_params=pltpu.CompilerParams(collective_id=0, has_side_effects=True, vmem_limit_bytes=VMEM_BYTES),
        cost_estimate=pl.CostEstimate(flops=10**11, bytes_accessed=10**8, transcendentals=0),
    )(inputs, memory, self_qkv, self_proj, cross_qkv, cross_proj, pre_own, ad_own)


def cross_forward(src_n, x_full, a, mem_mine, mem_got, self_proj, b_so, cross_qkv, b_cq, ad_col, cotangent, ffn_in, ffn_out, gain):
    t, d = x_full.shape
    half = t // 2
    nz = lax.axis_size("adp")
    pairs = d // 128
    chunks = d // TILE
    khead = self_proj.shape[0] // TILE
    kcol = cross_qkv.shape[2] // TILE
    nq = cross_qkv.shape[0]
    orow = ffn_out.shape[0]
    ihalf = ffn_in.shape[0] // 2
    qscale = HEAD_DIM ** -0.5 * LOG2E

    def moves(refs):
        ad_ref, cot_ref, fi_ref, fo_ref, q_out, k_out, v_out, cin, cout, ada_ref, cot_out, qs, ks, vs = refs
        dp, y, z, side, over, up = axes_here()
        onward = {"adp": lax.rem(z + 1, nz)}
        before = {"adp": lax.rem(z + nz - 1, nz)}
        table = {}
        for name, s_, o_ in (("q", qs, q_out), ("k", ks, k_out), ("v", vs, v_out)):
            table[name + " out"] = (s_, o_, None)
        ring_moves(table, "o", fo_ref, lambda s, r: cout.at[s, r],
                   lambda qz: lambda ref: ref.at[pl.ds(pl.multiple_of(qz * (orow // nz), orow // nz), orow // nz)],
                   z, nz, side, over, up, onward)
        table["o", "side"] = (fo_ref, cout.at[0, 1], side)
        table["i", "side"] = (fi_ref, cin.at[0, 1], side)
        table["i", "y"] = (fi_ref, cin.at[1, 0], up)
        table["i", "x"] = (fi_ref, cin.at[0, 2], over)
        one, two = pl.ds(0, ihalf), pl.ds(ihalf, ihalf)
        table["i", "d1"] = (cin.at[1, 0, one], cin.at[1, 2, one], over)
        table["i", "d2"] = (cin.at[0, 2, two], cin.at[1, 2, two], up)
        table["i", "y", "side"] = (cin.at[1, 0], cin.at[1, 1], side)
        table["i", "x", "side"] = (cin.at[0, 2], cin.at[0, 3], side)
        table["i", "d1", "side"] = (cin.at[1, 2, one], cin.at[1, 3, one], side)
        table["i", "d2", "side"] = (cin.at[1, 2, two], cin.at[1, 3, two], side)
        table["ad side"] = (ad_ref, ada_ref.at[1], side)
        table["ad over"] = (ad_ref, ada_ref.at[2], over)
        table["ad over side"] = (ada_ref.at[2], ada_ref.at[3], side)
        table["cot"] = (cot_ref.at[1 - y, 0], cot_out, up)
        return table, [side, over, up, onward, before]

    def kernel(n_ref, x_ref, a_in, gain_ref, memo_ref, memg_ref, so_ref, bso, cq_ref, bcq, ad_ref, cot_ref, fi_ref, fo_ref,
               ac_ref, p_ref, l_ref, u_ref, inv_ref, q_out, k_out, v_out, cin, cout, ada_ref, cot_out,
               sov, cqv, qs, ks, vs, send, recv, local, wsem):
        g = pl.program_id(0)
        dp, y = lax.axis_index("dp"), lax.axis_index("mp")
        table, peers = moves((ad_ref, cot_ref, fi_ref, fo_ref, q_out, k_out, v_out, cin, cout, ada_ref, cot_out, qs, ks, vs))
        mv = Moves(table, send, recv, local)
        done = set()

        def got(*names):
            done.update(names)
            mv.got(*names)

        def pass_on(spot, k):
            if k >= nz:
                return
            got(("o", spot) if k == 0 else ("o", spot, k - 1, "on"))
            if k + 1 < nz:
                mv.start(("o", spot, k, "on"))
            mv.start(("o", spot, k, "side"))

        outs = [n + " out" for n in ("q", "k", "v")]

        def loads():
            for i, (own, far, dst) in enumerate(((so_ref, bso, sov), (cq_ref, bcq, cqv))):
                yield pltpu.make_async_copy(own, dst.at[0, 0], wsem.at[i, 0])
                yield pltpu.make_async_copy(far.at[0, pl.ds(1, 3)], dst.at[0, pl.ds(1, 3)], wsem.at[i, 1])
                yield pltpu.make_async_copy(far.at[1], dst.at[1], wsem.at[i, 2])

        so = by_rows(sov)

        def project(i):
            rs = slice(i * half, (i + 1) * half)
            att = a_in[rs]
            z1 = place_cols(x_ref.at[pl.ds(i * half, half)], dp).astype(F32) + jnp.concatenate(
                [nn(att, [so(s, r, j) for s in range(2) for j in range(khead)]) for r in range(chunks)], axis=1)
            u, inv = normalize(z1)
            u_ref[rs] = u
            inv_ref[rs] = inv
            h = (u * gain_ref[...]).astype(BF)
            xm = jnp.where(y == i, place_cols(memo_ref, dp), place_cols(memg_ref, dp))
            for lhs, c, out in ((h, 0, qs), (xm, 1, ks), (xm, 2, vs)):
                for s in range(2):
                    for j in range(kcol):
                        o = nn(lhs, [cqv.at[s, r, c, :, pl.ds(j * TILE, TILE)] for r in range(4)])
                        cs = slice((s * kcol + j) * TILE, (s * kcol + j + 1) * TILE)
                        out[rs, cs] = (o * qscale if c == 0 else o).astype(BF)

        @pl.when(g == 0)
        def _():
            for c in loads():
                c.start()
            meet(peers)
            mv.start(("o", "y"), ("o", "x"), ("i", "y"), "cot", ("o", "side"), ("i", "side"), "ad side")
            pass_on("y", 0)
            mv.start(("o", "d"), ("i", "x"))
            pass_on("x", 0)
            for c in loads():
                c.wait()
            project(0)
            pass_on("d", 0)
            pass_on("y", 1)
            pass_on("x", 1)
            project(1)
            pass_on("d", 1)
            got(("i", "y"))
            mv.start(("i", "d1"), ("i", "y", "side"), "ad over")
            mv.start(*outs)

        for k in range(2, nz):
            @pl.when(g == 5 * k - 8)
            def _():
                pass_on("y", k)
                pass_on("x", k)

            @pl.when(g == 4 * k - 4)
            def _():
                pass_on("d", k)

        @pl.when(g == 3)
        def _():
            got(("i", "x"))
            mv.start(("i", "d2"), ("i", "x", "side"))

        @pl.when(g > 0)
        def _():
            cs = pl.ds(pl.multiple_of((g - 1) * 128, 128), 128)
            av, il = attend_pair(False, n_ref[0], qs[:, cs], ks[:, cs], vs[:, cs], None, None, p_ref, None)
            ac_ref[...] = av
            l_ref[0] = il

        @pl.when(g == pairs)
        def _():
            got("ad over")
            mv.start("ad over side")
            got(("i", "d1"))
            mv.start(("i", "d1", "side"))
            got(("i", "d2"))
            mv.start(("i", "d2", "side"))
            far = [n for n, (_, _, peer) in table.items() if peer is not None]
            got(*[n for n in far if n not in done])
            got(*outs)
            mv.sent(*far)

    lead = lambda g: (jnp.maximum(g - 1, 0), 0, 0)
    col = lambda g: (0, jnp.maximum(g - 1, 0))
    fixed = lambda g: (0, 0)
    shape = jax.ShapeDtypeStruct
    once = pl.Buffered(1)
    remotes = 3 + 3 * nz + 3 * (nz - 1) + 10 + 4
    near = 3
    vm = pltpu.VMEM
    whole = lambda *s: pl.BlockSpec(s, fixed, pipeline_mode=once)
    return pl.pallas_call(
        kernel,
        grid=(pairs + 1,),
        in_specs=[pl.BlockSpec(memory_space=pltpu.SMEM), whole(t, d), whole(t, d), whole(1, d), whole(half, d), whole(half, d)]
        + [HBM] * 8,
        out_specs=[pl.BlockSpec((t, 128), col), pl.BlockSpec((2, t, t), lead), pl.BlockSpec((1, 2, t), lead),
                   pl.BlockSpec((t, d), fixed), pl.BlockSpec((t, 1), fixed)] + [HBM] * 7,
        out_shape=[
            shape((t, d), BF), shape((2 * pairs, t, t), BF), shape((pairs, 2, t), F32), shape((t, d), F32), shape((t, 1), F32),
            shape((t, d), BF), shape((t, d), BF), shape((t, d), BF), shape((2, 4) + ffn_in.shape, BF), shape((2, 4) + ffn_out.shape, BF),
            shape((4,) + ad_col.shape, BF), shape((half, d), BF),
        ],
        scratch_shapes=[vm((2, 4) + self_proj.shape, BF), vm((2, 4) + cross_qkv.shape, BF), vm((t, d), BF), vm((t, d), BF), vm((t, d), BF),
                        pltpu.SemaphoreType.DMA((remotes,)), pltpu.SemaphoreType.DMA((remotes,)),
                        pltpu.SemaphoreType.DMA((near,)), pltpu.SemaphoreType.DMA((2, 3))],
        compiler_params=pltpu.CompilerParams(collective_id=1, has_side_effects=True, vmem_limit_bytes=VMEM_BYTES),
        cost_estimate=pl.CostEstimate(flops=10**11, bytes_accessed=10**8, transcendentals=0),
    )(src_n, x_full, a, gain, mem_mine, mem_got, self_proj, b_so, cross_qkv, b_cq, ad_col, cotangent, ffn_in, ffn_out)


def whole_sequences(inputs, memory, src_lengths, self_qkv, self_proj, cross_qkv, cross_proj, ffn_in, ffn_out,
                    norm_gains, prefix, adapter_down, adapter_up, cotangent):
    dp, y, z = lax.axis_index("dp"), lax.axis_index("mp"), lax.axis_index("adp")
    nz = lax.axis_size("adp")
    half, d = inputs.shape[2], inputs.shape[3]
    t = 2 * half
    chunks = d // TILE
    mine = lambda a: lax.dynamic_index_in_dim(a, y, 0, keepdims=False)[0]
    rel = lambda a: jnp.concatenate(
        [lax.dynamic_slice_in_dim(a, (dp ^ r) * TILE, TILE, axis=a.ndim - 1) for r in range(chunks)], axis=-1)

    ad_own = jnp.concatenate([adapter_down.T, adapter_up], axis=0)
    pre_own = jnp.pad(prefix, ((0, 0), (0, PRE - PREFIX_LEN), (0, 0)))
    src_n = lax.dynamic_index_in_dim(src_lengths, y, 0, keepdims=False).reshape(1)
    khead, kcol = self_proj.shape[0] // TILE, cross_qkv.shape[2] // TILE
    kin = ffn_in.shape[1] // TILE

    gains = rel(norm_gains.astype(F32))
    gain = [gains[i:i + 1] for i in range(3)]
    row = lambda i: (i, 0)
    hw = self_qkv.shape[2]

    a, p, pp, il, q, k, v, wq, x_full, pre_w, b_so, b_cq, b_co, mem_got, ad_col = self_forward(
        inputs, memory, self_qkv, self_proj, cross_qkv, cross_proj, pre_own, ad_own)
    ad_col = lax.dynamic_update_slice_in_dim(ad_col, ad_own[None], 0, axis=0)
    w_so, w_co = (self_proj, b_so, None), (cross_proj, b_co, None)
    w_cq = lambda c: (cross_qkv, b_cq, c)
    out_rows = lambda T, r, n: [T(s, r, j) for s in range(2) for j in range(n)]
    ac, p_c, il_c, u1, inv1, qc, kc, vc, c_in, c_out, ad_all, cot_got = cross_forward(
        src_n, x_full, a, mine(memory), mem_got, self_proj, b_so, cross_qkv, b_cq, ad_col, cotangent, ffn_in, ffn_out, gain[0])
    fixed = lambda i: (0, 0)
    spec = lambda shape, index: pl.BlockSpec(shape, index)
    held = lambda *shape: pl.BlockSpec(shape, lambda i: (0,) * len(shape), pipeline_mode=pl.Buffered(1))

    n_ad = ad_own.shape[0] // 2
    tile = half // FEED_SPLIT
    hid = 2 * kin

    def feed(W, need, rows, consts, outs, scr, put):
        dp, y = lax.axis_index("dp"), lax.axis_index("mp")
        ac_ref, u1_ref, cot_a, cot_b = rows
        act_ref, slope_ref, terms = scr
        g1, g2, g3 = consts[:3]
        co, fi, fo = by_rows(W[0]), by_cols(W[1]), by_rows(W[2])
        down = lambda r, kk: (consts[3].at[kk] if r == 0 else consts[4].at[r, kk]).at[pl.ds(0, n_ad)]
        upw = lambda r, kk: (consts[3].at[kk] if r == 0 else consts[4].at[r, kk]).at[pl.ds(n_ad, n_ad)]
        need(0)
        att = ac_ref[...]
        z2 = u1_ref[...] * g1[...] + jnp.concatenate(
            [nn(att, out_rows(co, r, khead)) for r in range(chunks)], axis=1)
        u2, inv2 = normalize(z2)
        h2 = u2 * g2[...]
        h2b = h2.astype(BF)
        need(1)
        order = [(s, j) for s in range(2) for j in range(kin)]
        acc = outs[0]
        down_t = jnp.concatenate([stack_cols([down(r, kk) for r in range(4)]) for kk in range(nz)], axis=0)
        up_m = jnp.concatenate([stack_cols([upw(r, kk) for r in range(4)]) for kk in range(nz)], axis=0)
        span = 256
        spans = [(s, j) for s in range(2) for j in range(kin * TILE // span)]

        def grow(i):
            s, j = spans[i]
            return nn(h2b, [W[1].at[s, r, slice(None), pl.ds(j * span, span)] for r in range(4)])

        def fall(i):
            s, j = spans[i]
            w = jnp.concatenate([W[2][s, r, j * span:(j + 1) * span] for r in range(4)], axis=1)
            return dot_mm(act_ref[:, i * span:(i + 1) * span], w, 1, 0)

        def bend(i, g):
            act, slope = gelu_pair(g)
            act_ref[:, i * span:(i + 1) * span] = act.astype(BF)
            slope_ref[:, i * span:(i + 1) * span] = slope.astype(BF)

        ahead = grow(0)
        g_a = dot_mm(h2b, down_t, 1, 1)
        act_a, slope_a = gelu_pair(g_a)
        act_a = act_a.astype(BF)
        need(2)
        for i in range(len(spans)):
            g = ahead
            if i + 1 < len(spans):
                ahead = grow(i + 1)
            if i == 1:
                acc[...] = h2 + fall(0)
            elif i > 1:
                acc[...] += fall(i - 1)
            bend(i, g)
        z3 = acc[...] + fall(len(spans) - 1) + 4.0 * dot_mm(act_a, up_m, 1, 0)
        u3, inv3 = normalize(z3)
        put(u3 * g3[...])
        in_own = pl.program_id(0) // (half // tile) == y
        cot = jnp.where(in_own, place_cols(cot_a, dp), place_cols(cot_b, dp)).astype(F32)
        dz3 = norm_back(cot, u3, inv3, g3[...])
        b3 = dz3.astype(BF)
        dga = (4.0 * dot_mm(b3, up_m, 1, 1) * slope_a).astype(BF)
        up_term = 4.0 * dot_mm(act_a, b3, 0, 0)
        down_term = dot_mm(dga, h2b, 0, 0)

        @pl.when(pl.program_id(0) == 0)
        def _():
            terms[0] = down_term
            terms[1] = up_term

        @pl.when(pl.program_id(0) > 0)
        def _():
            terms[0] += down_term
            terms[1] += up_term

        @pl.when(pl.program_id(0) == pl.num_programs(0) - 1)
        def _():
            for i in range(2):
                outs[2][:, i] = terms[:, :, 2 * i * TILE:(2 * i + 1) * TILE]
                outs[3][:, i] = terms[:, :, (2 * i + 1) * TILE:(2 * i + 2) * TILE].astype(BF)

        for i, (s, j) in enumerate(order):
            cs = slice(i * TILE, (i + 1) * TILE)
            df = nt(b3, [fo(s, r, j) for r in range(4)])
            slope_ref[:, cs] = (df * slope_ref[:, cs].astype(F32)).astype(BF)
        dg = slope_ref[...]
        dh2 = dz3 + dot_mm(dga, down_t, 1, 0) + jnp.concatenate(
            [nt(dg, out_rows(fi, r, kin)) for r in range(chunks)], axis=1)
        dz2 = norm_back(dh2, u2, inv2, g2[...])
        outs[0][...] = dz2
        dz2b = dz2.astype(BF)
        for s in range(2):
            for j in range(khead):
                i = s * khead + j
                outs[1][:, i * TILE:(i + 1) * TILE] = nt(dz2b, [co(s, r, j) for r in range(4)]).astype(BF)

    part = lambda i: (i % (half // tile), 0)
    dz2, dac, keep, give, result = tiled(
        [w_co, (ffn_in, c_in, None), (ffn_out, c_out, None)],
        [(ac, spec((tile, d), row)), (u1, spec((tile, d), row)), (mine(cotangent), spec((tile, d), part)),
         (cot_got, spec((tile, d), part))],
        gain + [ad_col, ad_all],
        [((t, d), F32, (tile, d), row), ((t, d), BF, (tile, d), row),
         ((2, 2, nz * n_ad, TILE), F32, (2, 2, nz * n_ad, TILE), lambda i: (0, 0, 0, 0)),
         ((2, 2, nz * n_ad, TILE), BF, (2, 2, nz * n_ad, TILE), lambda i: (0, 0, 0, 0))],
        feed, tile, t // tile, exchange=(2, half, d),
        scratch=[pltpu.VMEM((tile, hid * TILE), BF)] * 2 + [pltpu.VMEM((2, nz * n_ad, d), F32)], flops=4 * 2 * t * d * hid * TILE)

    dqc, dkc, dvc, down_grad, up_grad = attn_bwd(qc, kc, vc, ac, dac, il_c, p_c, keep=keep, give=give)

    def memory_back(sc, own, far, dk_ref, dv_ref, mine_ref, send_ref, wv, sems):
        def loads():
            yield pltpu.make_async_copy(own.at[pl.ds(1, 2)], wv.at[0, 0], sems.at[0])
            yield pltpu.make_async_copy(far.at[0, pl.ds(1, 3), pl.ds(1, 2)], wv.at[0, pl.ds(1, 3)], sems.at[1])
            yield pltpu.make_async_copy(far.at[1, pl.ds(0, 4), pl.ds(1, 2)], wv.at[1], sems.at[2])

        step = pl.program_id(0)

        @pl.when(step == 0)
        def _():
            for c in loads():
                c.start()
            for c in loads():
                c.wait()

        lhs = jnp.concatenate([dk_ref[...], dv_ref[...]], axis=1)
        e = jnp.concatenate(
            [dot_mm(lhs, jnp.concatenate([wv[s, r, c] for c in range(2) for s in range(2)], axis=1), 1, 1)
             for r in range(chunks)], axis=1)

        @pl.when(step == 0)
        def _():
            unplace_store(send_ref, e, sc[0])

        @pl.when(step == 1)
        def _():
            unplace_store(mine_ref.at[0], e, sc[0])

    turned = lambda i, sc: (jnp.where(i == 0, 1 - sc[1], sc[1]), 0)
    mem_mine, mem_send = pl.pallas_call(
        memory_back,
        grid_spec=pltpu.PrefetchScalarGridSpec(
            num_scalar_prefetch=1, grid=(2,),
            in_specs=[HBM, HBM, pl.BlockSpec((half, d), turned), pl.BlockSpec((half, d), turned)],
            out_specs=[pl.BlockSpec((1, half, d), lambda i, sc: (sc[1], 0, 0)), pl.BlockSpec((half, d), lambda i, sc: (0, 0))],
            scratch_shapes=[pltpu.VMEM((2, 4, 2) + cross_qkv.shape[1:], BF), pltpu.SemaphoreType.DMA((3,))]),
        out_shape=[jax.ShapeDtypeStruct((2, half, d), BF), jax.ShapeDtypeStruct((half, d), BF)],
        compiler_params=pltpu.CompilerParams(vmem_limit_bytes=VMEM_BYTES),
        cost_estimate=pl.CostEstimate(flops=4 * t * d * d, bytes_accessed=2**24, transcendentals=0),
    )(jnp.stack([dp, y]).astype(jnp.int32), cross_qkv, b_cq, dkc, dvc)

    def norm_back_self(W, need, rows, consts, outs, scr, put):
        dz2_ref, dqc_ref, u1_ref, inv_ref = rows
        cq, so = by_cols(W[0]), by_rows(W[1])
        need(0)
        dq_c = dqc_ref[...]
        e = dz2_ref[...] + jnp.concatenate([nt(dq_c, out_rows(cq, r, kcol)) for r in range(chunks)], axis=1)
        dz1 = norm_back(e, u1_ref[...], inv_ref[...], consts[0][...])
        outs[0][...] = dz1
        dz1b = dz1.astype(BF)
        need(1)
        for s in range(2):
            for j in range(khead):
                i = s * khead + j
                outs[1][:, i * TILE:(i + 1) * TILE] = nt(dz1b, [so(s, r, j) for r in range(4)]).astype(BF)

    dz1, da = tiled(
        [w_cq(0), w_so],
        [(dz2, spec((half, d), row)), (dqc, spec((half, d), row)), (u1, spec((half, d), row)), (inv1, spec((half, 1), row))],
        [gain[0]],
        [((t, d), F32, (half, d), row), ((t, d), BF, (half, d), row)], norm_back_self, half, 2,
        flops=4 * t * d * d)

    dq, dk, dv, dpre, memory_grad = attn_bwd(q, k, v, a, da, il, p, pp, pre_w, mem_send, mem_mine)
    input_grad, pre_sum = last_gradient(wq, dz1, dq, dk, dv, dpre, self_qkv)
    return result[:, None], input_grad[:, None], memory_grad[:, None], pre_sum[:, :PREFIX_LEN], down_grad, up_grad


def solution(mesh):
    by_sequence = mesh.shape["mp"] == MICRO and mesh.shape["dp"] == 4
    return jax.shard_map(
        whole_sequences if by_sequence else shards,
        mesh=mesh,
        in_specs=(
            P(None, ("dp", "adp"), "mp", None),
            P(None, ("dp", "adp"), "mp", None),
            P(None, ("dp", "adp"), None),
            P(None, "dp", "mp"),
            P("mp", "dp"),
            P(None, "dp", "mp"),
            P("mp", "dp"),
            P("dp", "mp"),
            P("mp", "dp"),
            P(),
            P(None, None, "mp"),
            P("dp", "adp"),
            P("adp", "dp"),
            P(None, ("dp", "adp"), "mp", None),
        ),
        out_specs=(
            P(None, ("dp", "adp"), "mp", None),
            P(None, ("dp", "adp"), "mp", None),
            P(None, ("dp", "adp"), "mp", None),
            P(None, None, "mp"),
            P(("dp", "mp"), "adp"),
            P("adp", ("dp", "mp")),
        ),
        check_vma=False,
    )
```

```python
import functools
import math

import jax
import jax.numpy as jnp
from jax import lax
from jax.experimental import pallas as pl
from jax.experimental.pallas import tpu as pltpu
from jax.sharding import PartitionSpec as P

HEAD_DIM = 64
PREFIX_LEN = 30
SEQ_LEN = 1024
SRC_MAX = 1024
SEQS_BLK = 1
MICRO = 2


eps = 1e-05


def exact_gelu(values):
    return jax.nn.gelu(values, approximate=False)


def norm_forward(residual, gain_row):
    centered = residual - jnp.mean(residual, axis=-1, keepdims=True)
    inv_std = lax.rsqrt(jnp.mean(centered * centered, axis=-1, keepdims=True) + eps)
    return centered * inv_std * gain_row


def norm_backward(upstream, residual, gain_row):
    centered = residual - jnp.mean(residual, axis=-1, keepdims=True)
    inv_std = lax.rsqrt(jnp.mean(centered * centered, axis=-1, keepdims=True) + eps)
    normed = centered * inv_std
    scaled = upstream * gain_row
    inner_mean = jnp.mean(scaled * normed, axis=-1, keepdims=True)
    return inv_std * (scaled - jnp.mean(scaled, axis=-1, keepdims=True) - normed * inner_mean)


def gelu_back(pre_act, upstream):
    return jax.vjp(exact_gelu, pre_act)[1](upstream)[0]


def matmul(left_mat, right_mat):
    return jnp.dot(left_mat, right_mat, preferred_element_type=jnp.float32)


def matmul_nt(left_mat, right_mat):
    return lax.dot_general(
        left_mat, right_mat, (((1,), (1,)), ((), ())), preferred_element_type=jnp.float32
    )


def matmul_tn(left_mat, right_mat):
    return lax.dot_general(
        left_mat, right_mat, (((0,), (0,)), ((), ())), preferred_element_type=jnp.float32
    )


def to_heads(rows_mat, seq_count, length):
    heads_here = rows_mat.shape[-1] // HEAD_DIM
    return rows_mat.reshape(seq_count, length, heads_here, HEAD_DIM).transpose(0, 2, 1, 3)


def from_heads(split_mat):
    seq_count, heads_here, length, head_width = split_mat.shape
    return split_mat.transpose(0, 2, 1, 3).reshape(seq_count * length, heads_here * head_width)


def causal_allowed():
    query_pos = lax.broadcasted_iota(jnp.int32, (SEQ_LEN, PREFIX_LEN + SEQ_LEN), 0)
    key_pos = lax.broadcasted_iota(jnp.int32, (SEQ_LEN, PREFIX_LEN + SEQ_LEN), 1)
    return (key_pos < PREFIX_LEN) | (key_pos - PREFIX_LEN <= query_pos)


def source_allowed(length):
    return lax.broadcasted_iota(jnp.int32, (SEQ_LEN, SRC_MAX), 1) < length


def attend_forward(queries, keys_all, values_all, allowed):
    scores = jnp.einsum("hqd,hkd->hqk", queries, keys_all, preferred_element_type=jnp.float32)
    scores = jnp.where(allowed, scores, -1e30)
    top_score = jnp.max(scores, axis=-1, keepdims=True)
    expo_scores = jnp.exp(scores - top_score)
    row_total = jnp.sum(expo_scores, axis=-1, keepdims=True)
    weights_low = (expo_scores / row_total).astype(jnp.bfloat16)
    mixed = jnp.einsum("hqk,hkd->hqd", weights_low, values_all, preferred_element_type=jnp.float32)
    return (mixed.astype(jnp.bfloat16), top_score + jnp.log(row_total))


def attend_backward(queries, keys_all, values_all, allowed, log_total, grad_out):
    scores = jnp.einsum("hqd,hkd->hqk", queries, keys_all, preferred_element_type=jnp.float32)
    scores = jnp.where(allowed, scores, -1e30)
    soft_weights = jnp.exp(scores - log_total)
    grad_soft = jnp.einsum("hqd,hkd->hqk", grad_out, values_all, preferred_element_type=jnp.float32)
    inner_sum = jnp.sum(soft_weights * grad_soft, axis=-1, keepdims=True)
    grad_scores = (soft_weights * (grad_soft - inner_sum)).astype(jnp.bfloat16)
    grad_query = jnp.einsum(
        "hqk,hkd->hqd", grad_scores, keys_all, preferred_element_type=jnp.float32
    )
    grad_keys = jnp.einsum("hqk,hqd->hkd", grad_scores, queries, preferred_element_type=jnp.float32)
    grad_values = jnp.einsum(
        "hqk,hqd->hkd",
        soft_weights.astype(jnp.bfloat16),
        grad_out,
        preferred_element_type=jnp.float32,
    )
    return (grad_query, grad_keys, grad_values)


def gather_rows(rows_low):
    return lax.all_gather(rows_low, "mp", axis=0, tiled=True)


def reduce_rows(term_fn, own_count):
    return lax.psum_scatter(
        term_fn(jnp.int32(0), own_count * lax.axis_size("mp")).astype(jnp.bfloat16),
        "mp",
        scatter_dimension=0,
        tiled=True,
    ).astype(jnp.float32)


def gather_adapter(rows_low):
    return lax.all_gather(rows_low, "adp", axis=0, tiled=True)


def reduce_adapter(term_fn, own_count):
    return lax.psum_scatter(
        term_fn(jnp.int32(0), own_count * lax.axis_size("adp")).astype(jnp.bfloat16),
        "adp",
        scatter_dimension=0,
        tiled=True,
    ).astype(jnp.float32)


def reduce_prefix(grad_prefix):
    return lax.psum(grad_prefix, ("dp", "adp"))


def reduce_adapter_grads(grad_down, grad_up):
    return (
        lax.psum_scatter(grad_down, ("dp", "mp"), scatter_dimension=0, tiled=True),
        lax.psum_scatter(grad_up, ("dp", "mp"), scatter_dimension=1, tiled=True),
    )


def shards(
    inputs,
    memory,
    src_lengths,
    self_qkv,
    self_proj,
    cross_qkv,
    cross_proj,
    ffn_in,
    ffn_out,
    norm_gains,
    prefix,
    adapter_down,
    adapter_up,
    cotangent,
):
    scale = HEAD_DIM ** (-0.5)
    own_rows = inputs.shape[2]
    gains = norm_gains.astype(jnp.float32)
    causal = causal_allowed()
    prefix_heads = to_heads(prefix, 2, PREFIX_LEN)
    prefix_keys = prefix_heads[0]
    prefix_values = prefix_heads[1]
    results = []
    input_grads = []
    memory_grads = []
    prefix_acc = None
    down_acc = None
    up_acc = None
    for micro_index in range(MICRO):
        self_w, self_o, cross_w, cross_o, down_w, up_w = (
            lax.all_gather(self_qkv, "dp", axis=1, tiled=True),
            lax.all_gather(self_proj, "dp", axis=1, tiled=True),
            lax.all_gather(cross_qkv, "dp", axis=1, tiled=True),
            lax.all_gather(cross_proj, "dp", axis=1, tiled=True),
            lax.all_gather(adapter_down, "dp", axis=0, tiled=True),
            lax.all_gather(adapter_up, "dp", axis=1, tiled=True),
        )
        ffn_first, ffn_second = (
            lax.all_gather(ffn_in, "dp", axis=0, tiled=True),
            lax.all_gather(ffn_out, "dp", axis=1, tiled=True),
        )
        x_rows = inputs[micro_index, 0]
        lengths_here = src_lengths[micro_index, 0]
        x_full = gather_rows(x_rows)
        mem_full = lax.all_gather(memory[micro_index, 0], "mp", axis=0, tiled=True)
        projected = jnp.einsum("td,cde->cte", x_full, self_w, preferred_element_type=jnp.float32)
        query_self = to_heads((projected[0] * scale).astype(jnp.bfloat16), SEQS_BLK, SEQ_LEN)
        key_self = to_heads(projected[1].astype(jnp.bfloat16), SEQS_BLK, SEQ_LEN)
        value_self = to_heads(projected[2].astype(jnp.bfloat16), SEQS_BLK, SEQ_LEN)

        def self_forward(packed):
            query_seq, key_seq, value_seq = packed
            keys_all = jnp.concatenate([prefix_keys, key_seq], axis=1)
            values_all = jnp.concatenate([prefix_values, value_seq], axis=1)
            return attend_forward(query_seq, keys_all, values_all, causal)

        attn_self, lse_self = lax.map(self_forward, (query_self, key_self, value_self))
        attn_rows = from_heads(attn_self)

        def self_term(first_row, row_count):
            return matmul(attn_rows, self_o)

        resid_one = x_rows.astype(jnp.float32) + reduce_rows(self_term, own_rows)
        normed_one = norm_forward(resid_one, gains[0])
        one_full = gather_rows(normed_one.astype(jnp.bfloat16))
        cross_query = to_heads(
            (matmul(one_full, cross_w[0]) * scale).astype(jnp.bfloat16), SEQS_BLK, SEQ_LEN
        )
        memory_proj = jnp.einsum(
            "td,cde->cte", mem_full, cross_w[1:], preferred_element_type=jnp.float32
        )
        cross_keys = to_heads(memory_proj[0].astype(jnp.bfloat16), SEQS_BLK, SRC_MAX)
        cross_values = to_heads(memory_proj[1].astype(jnp.bfloat16), SEQS_BLK, SRC_MAX)

        def cross_forward(packed):
            query_seq, key_seq, value_seq, length = packed
            return attend_forward(query_seq, key_seq, value_seq, source_allowed(length))

        attn_cross, lse_cross = lax.map(
            cross_forward, (cross_query, cross_keys, cross_values, lengths_here)
        )
        cross_rows = from_heads(attn_cross)

        def cross_term(first_row, row_count):
            return matmul(cross_rows, cross_o)

        resid_two = normed_one + reduce_rows(cross_term, own_rows)
        normed_two = norm_forward(resid_two, gains[1])
        two_low = normed_two.astype(jnp.bfloat16)
        two_full = gather_rows(two_low)
        hidden_pre = matmul(two_full, ffn_first)
        hidden_act = exact_gelu(hidden_pre).astype(jnp.bfloat16)

        def ffn_term(first_row, row_count):
            return matmul(hidden_act, ffn_second)

        ffn_rows = reduce_rows(ffn_term, own_rows)
        adapter_in = gather_adapter(two_low)
        adapter_pre = matmul(adapter_in, down_w)
        adapter_act = exact_gelu(adapter_pre).astype(jnp.bfloat16)

        def adapter_term(first_row, row_count):
            return matmul(adapter_act, up_w)

        adapter_rows = reduce_adapter(adapter_term, own_rows)
        resid_three = normed_two + ffn_rows + 4.0 * adapter_rows
        results.append(norm_forward(resid_three, gains[2]).astype(jnp.bfloat16))
        grad_three = norm_backward(
            cotangent[micro_index, 0].astype(jnp.float32), resid_three, gains[2]
        )
        grad_branch = grad_three.astype(jnp.bfloat16)
        grad_adapter = gather_adapter(grad_branch) * 4.0
        up_term = matmul_tn(adapter_act, grad_adapter)
        grad_adapter_pre = gelu_back(adapter_pre, matmul_nt(grad_adapter, up_w)).astype(
            jnp.bfloat16
        )
        down_term = matmul_tn(adapter_in, grad_adapter_pre)

        def adapter_back_term(first_row, row_count):
            return matmul_nt(grad_adapter_pre, down_w)

        adapter_back = reduce_adapter(adapter_back_term, own_rows)
        branch_full = gather_rows(grad_branch)
        grad_pre = gelu_back(hidden_pre, matmul_nt(branch_full, ffn_second)).astype(jnp.bfloat16)

        def ffn_back_term(first_row, row_count):
            return matmul_nt(grad_pre, ffn_first)

        ffn_back = reduce_rows(ffn_back_term, own_rows)
        grad_mid = norm_backward(grad_three + ffn_back + adapter_back, resid_two, gains[1])
        mid_full = gather_rows(grad_mid.astype(jnp.bfloat16))
        grad_cross_out = to_heads(
            matmul_nt(mid_full, cross_o).astype(jnp.bfloat16), SEQS_BLK, SEQ_LEN
        )

        def cross_backward(packed):
            query_seq, key_seq, value_seq, lse_seq, grad_seq, length = packed
            return attend_backward(
                query_seq, key_seq, value_seq, source_allowed(length), lse_seq, grad_seq
            )

        cross_gq, cross_gk, cross_gv = lax.map(
            cross_backward,
            (cross_query, cross_keys, cross_values, lse_cross, grad_cross_out, lengths_here),
        )
        cross_gq_rows = from_heads(cross_gq).astype(jnp.bfloat16) * scale

        def cross_query_term(first_row, row_count):
            return matmul_nt(cross_gq_rows, cross_w[0])

        grad_one = grad_mid + reduce_rows(cross_query_term, own_rows)
        memory_stack = jnp.stack(
            [from_heads(cross_gk).astype(jnp.bfloat16), from_heads(cross_gv).astype(jnp.bfloat16)]
        )
        memory_grads.append(
            lax.psum_scatter(
                jnp.einsum(
                    "cte,cde->td", memory_stack, cross_w[1:], preferred_element_type=jnp.float32
                ).astype(jnp.bfloat16),
                "mp",
                scatter_dimension=0,
                tiled=True,
            )
        )
        grad_first = norm_backward(grad_one, resid_one, gains[0])
        first_full = gather_rows(grad_first.astype(jnp.bfloat16))
        grad_self_out = to_heads(
            matmul_nt(first_full, self_o).astype(jnp.bfloat16), SEQS_BLK, SEQ_LEN
        )

        def self_backward(packed):
            query_seq, key_seq, value_seq, lse_seq, grad_seq = packed
            keys_all = jnp.concatenate([prefix_keys, key_seq], axis=1)
            values_all = jnp.concatenate([prefix_values, value_seq], axis=1)
            return attend_backward(query_seq, keys_all, values_all, causal, lse_seq, grad_seq)

        self_gq, self_gk, self_gv = lax.map(
            self_backward, (query_self, key_self, value_self, lse_self, grad_self_out)
        )
        prefix_key_grad = from_heads(jnp.sum(self_gk[:, :, :PREFIX_LEN], axis=0)[None])
        prefix_value_grad = from_heads(jnp.sum(self_gv[:, :, :PREFIX_LEN], axis=0)[None])
        prefix_term = jnp.stack([prefix_key_grad, prefix_value_grad])
        self_stack = jnp.stack(
            [
                from_heads(self_gq).astype(jnp.bfloat16) * scale,
                from_heads(self_gk[:, :, PREFIX_LEN:]).astype(jnp.bfloat16),
                from_heads(self_gv[:, :, PREFIX_LEN:]).astype(jnp.bfloat16),
            ]
        )

        def input_term(first_row, row_count):
            return jnp.einsum("cte,cde->td", self_stack, self_w, preferred_element_type=jnp.float32)

        input_grads.append((grad_first + reduce_rows(input_term, own_rows)).astype(jnp.bfloat16))
        prefix_term = reduce_prefix(prefix_term)
        down_term, up_term = reduce_adapter_grads(down_term, up_term)
        prefix_acc = prefix_term if prefix_acc is None else prefix_acc + prefix_term
        down_acc = down_term if down_acc is None else down_acc + down_term
        up_acc = up_term if up_acc is None else up_acc + up_term
    return (
        jnp.stack(results)[:, None],
        jnp.stack(input_grads)[:, None],
        jnp.stack(memory_grads)[:, None],
        prefix_acc,
        down_acc,
        up_acc,
    )


F32 = jnp.float32
BF = jnp.bfloat16
EPS = 1e-05
LOG2E = 1.4426950408889634
TILE = 256
FEED_SPLIT = 2

BQF = 512
BQ = 512
PRE = 32
VMEM_BYTES = 60 * 2**20
NEG = -1e30
HBM = pl.BlockSpec(memory_space=pl.ANY)
LN2 = 0.6931471805599453


def dot_mm(a, b, ca, cb):
    return lax.dot_general(a, b, (((ca,), (cb,)), ((), ())), preferred_element_type=jnp.float32)


def pick_head(h, mat):
    rows = lax.broadcasted_iota(jnp.int32, mat.shape, 0)
    return jnp.where((rows // HEAD_DIM) == h, mat, jnp.zeros_like(mat))


def attend_pair(causal, n, q, k, v, pk, pv, p_ref, pp_ref):
    t = q.shape[0]
    s = k.shape[0]
    nb = t // BQF
    qt = q.T
    vt = v.T
    ones = jnp.ones((16, s), jnp.bfloat16)
    work = [(h, j) for h in range(2) for j in range(nb)]

    def scores(h, j):
        kk = (j + 1) * BQF if causal else s
        qb = pick_head(h, qt[:, j * BQF:(j + 1) * BQF])
        return dot_mm(k[:kk], qb, 1, 0), dot_mm(pk, qb, 1, 0) if causal else None

    res = {}
    ahead = scores(*work[0])
    for w, (h, j) in enumerate(work):
        st, sp = ahead
        if w + 1 < len(work):
            ahead = scores(*work[w + 1])
        kk = st.shape[0]
        js = slice(j * BQF, (j + 1) * BQF)
        if causal:
            krow = lax.broadcasted_iota(jnp.int32, (BQF, BQF), 0)
            qcol = lax.broadcasted_iota(jnp.int32, (BQF, BQF), 1)
            diag = jnp.where(krow <= qcol, st[kk - BQF:], NEG)
            st = jnp.concatenate([st[:kk - BQF], diag], axis=0) if kk > BQF else diag
            prow = lax.broadcasted_iota(jnp.int32, sp.shape, 0)
            sp = jnp.where(prow < n, sp, NEG)
            m = jnp.maximum(jnp.max(st, axis=0, keepdims=True), jnp.max(sp, axis=0, keepdims=True))
            pp = jnp.exp2(sp - m).astype(jnp.bfloat16)
            pp_ref[h, :, js] = pp
        else:
            krow = lax.broadcasted_iota(jnp.int32, st.shape, 0)
            st = jnp.where(krow < n, st, NEG)
            m = jnp.max(st, axis=0, keepdims=True)
        p = jnp.exp2(st - m).astype(jnp.bfloat16)
        p_ref[h, :kk, js] = p
        hs = slice(h * HEAD_DIM, (h + 1) * HEAD_DIM)
        ot = dot_mm(jnp.concatenate([vt[hs, :kk], ones[:, :kk]], axis=0), p, 1, 0)
        if causal:
            ot += dot_mm(jnp.concatenate([pv.T[hs], ones[:, :PRE]], axis=0), pp, 1, 0)
        il = 1.0 / ot[HEAD_DIM:HEAD_DIM + 1]
        res[h, j] = (ot[:HEAD_DIM] * il, il)
    ils = [jnp.concatenate([res[h, j][1] for j in range(nb)], axis=1) for h in range(2)]
    at = jnp.concatenate([jnp.concatenate([res[h, j][0] for j in range(nb)], axis=1) for h in range(2)], axis=0)
    return at.astype(jnp.bfloat16).T, jnp.concatenate(ils, axis=0)


def sum_terms(keep_hbm, give_hbm, down_ref, up_ref, keep, part, first, second, third, fourth, out2, out3, out4, near, send, recv):
    g = pl.program_id(0)
    last = pl.num_programs(0) - 1
    dp, y, z, side, over, up = axes_here()
    nz = lax.axis_size("adp")
    rows = part.shape[1] // nz
    wide = out3.shape[2]

    def far(src, dst, peer, i):
        return pltpu.make_async_remote_copy(src_ref=src, dst_ref=dst, send_sem=send.at[i], recv_sem=recv.at[i],
                                            device_id=peer, device_id_type=pl.DeviceIdType.MESH)

    load = pltpu.make_async_copy(keep_hbm, keep, near.at[0])
    core = far(give_hbm, first, side, 0)
    across = far(out2, second, over, 1)
    beside = far(out3, third, up, 2)
    along = [far(out4.at[k - 1], fourth.at[k - 1], {"adp": lax.rem(z + nz - k, nz)}, 2 + k) for k in range(1, nz)]

    @pl.when(g == 0)
    def _():
        meet([side, over, up] + [{"adp": lax.rem(z + k, nz)} for k in range(1, nz)])
        load.start()
        core.start()

    @pl.when(g == 1)
    def _():
        load.wait()
        core.wait_recv()
        out2[...] = (keep[:, 1] + first[:, 1].astype(jnp.float32)).astype(jnp.bfloat16)
        across.start()

    @pl.when(g == last // 2 + 1)
    def _():
        across.wait_recv()
        keep[:, 0] = keep[:, 0] + first[:, 0].astype(jnp.float32) + second[...].astype(jnp.float32)
        mine = pl.ds(pl.multiple_of(y * wide, wide), wide)
        other = pl.ds(pl.multiple_of((1 - y) * wide, wide), wide)
        out3[...] = keep[:, 0, :, other].astype(jnp.bfloat16)
        part[...] = keep[:, 0, :, mine]
        beside.start()

    @pl.when(g == last - 1)
    def _():
        beside.wait_recv()
        part[...] = part[...] + third[...].astype(jnp.float32)
        for k in range(1, nz):
            out4[k - 1] = part[:, k * rows:(k + 1) * rows].astype(jnp.bfloat16)
            along[k - 1].start()

    @pl.when(g == last)
    def _():
        total = part[:, :rows]
        for k in range(1, nz):
            along[k - 1].wait_recv()
            total = total + fourth[k - 1].astype(jnp.float32)
        down_ref[...] = total[0].T
        up_ref[...] = total[1]
        for c in [core, across, beside] + along:
            c.wait_send()


def attn_bwd_body(causal, q_ref, k_ref, v_ref, a_ref, da_ref, l_ref, p_ref, *rest):
    if causal:
        pp_ref, pre_ref, moved, _, dq_ref, dk_ref, dv_ref, dpre_ref, landed, sems = rest
        y = lax.axis_index("mp")
        carry = pltpu.make_async_remote_copy(
            src_ref=moved, dst_ref=landed.at[y], send_sem=sems.at[0], recv_sem=sems.at[1],
            device_id={"mp": 1 - y}, device_id_type=pl.DeviceIdType.MESH)

        @pl.when(pl.program_id(0) == 0)
        def _():
            meet([{"mp": 1 - y}])
            carry.start()
    else:
        pp_ref, pre_ref, dpre_ref = None, None, None
        keep_ref, give_ref, dq_ref, dk_ref, dv_ref, down_ref, up_ref = rest[:7]
        sum_terms(keep_ref, give_ref, down_ref, up_ref, *rest[7:])
    t = q_ref.shape[0]
    s = k_ref.shape[0]
    nb = t // BQ
    qt = q_ref[...].T
    kt = k_ref[...].T
    dat = da_ref[...].T.astype(jnp.float32)
    prod = dat * a_ref[...].T.astype(jnp.float32)
    pkt = pre_ref[0].T if causal else None
    work = [(h, j) for h in range(2) for j in range(nb)]
    head = {}
    for h in range(2):
        hs = slice(h * HEAD_DIM, (h + 1) * HEAD_DIM)
        il = l_ref[0, h:h + 1]
        head[h] = ((dat * il).astype(jnp.bfloat16), jnp.sum(prod[hs], axis=0, keepdims=True) * il)

    def soft_grad(h, j):
        js = slice(j * BQ, (j + 1) * BQ)
        kk = (j + 1) * BQ if causal else s
        dab = pick_head(h, head[h][0][:, js])
        return dot_mm(v_ref[:kk], dab, 1, 0), dot_mm(pre_ref[1], dab, 1, 0) if causal else None

    def add(tot, new):
        return new if tot is None else tot + new

    res = {}
    dpk = [None, None]
    dpv = [None, None]
    dkb = [[None] * nb, [None] * nb]
    dvb = [[None] * nb, [None] * nb]
    ahead = soft_grad(*work[0])
    for w, (h, j) in enumerate(work):
        dp, dpp = ahead
        if w + 1 < len(work):
            ahead = soft_grad(*work[w + 1])
        hs = slice(h * HEAD_DIM, (h + 1) * HEAD_DIM)
        js = slice(j * BQ, (j + 1) * BQ)
        kk = dp.shape[0]
        dl = head[h][1][:, js]
        dah = head[h][0][hs, js]
        p = p_ref[h, :kk, js]
        ds = (p.astype(jnp.float32) * (dp - dl)).astype(jnp.bfloat16)
        dq = dot_mm(kt[hs, :kk], ds, 1, 0)
        if causal:
            pp = pp_ref[h, :, js]
            dsp = (pp.astype(jnp.float32) * (dpp - dl)).astype(jnp.bfloat16)
            dq += dot_mm(pkt[hs], dsp, 1, 0)
            dpk[h] = add(dpk[h], dot_mm(qt[hs, js], dsp, 1, 1))
            dpv[h] = add(dpv[h], dot_mm(dah, pp, 1, 1))
        res[h, j] = dq
        dv = dot_mm(dah, p, 1, 1)
        dk = dot_mm(qt[hs, js], ds, 1, 1)
        if causal:
            for i in range(kk // BQ):
                dvb[h][i] = add(dvb[h][i], dv[:, i * BQ:(i + 1) * BQ])
                dkb[h][i] = add(dkb[h][i], dk[:, i * BQ:(i + 1) * BQ])
        else:
            dvb[h] = [add(dvb[h][0], dv)]
            dkb[h] = [add(dkb[h][0], dk)]
    both = lambda f: jnp.concatenate([f(0), f(1)], axis=0)
    dq_ref[...] = (both(lambda h: jnp.concatenate([res[h, j] for j in range(nb)], axis=1))
                   * HEAD_DIM ** -0.5).astype(jnp.bfloat16).T
    dk_ref[...] = (both(lambda h: jnp.concatenate(dkb[h], axis=1)) * LN2).astype(jnp.bfloat16).T
    dv_ref[...] = both(lambda h: jnp.concatenate(dvb[h], axis=1)).astype(jnp.bfloat16).T
    if causal:
        dpre_ref[0] = both(lambda h: dpk[h]).T * LN2
        dpre_ref[1] = both(lambda h: dpv[h]).T

        @pl.when(pl.program_id(0) == pl.num_programs(0) - 1)
        def _():
            carry.wait()


def attn_bwd(q, k, v, a, da, il, p, pp=None, pre=None, moved=None, landed=None, keep=None, give=None):
    t, w = q.shape
    s = k.shape[0]
    pairs = w // 128
    causal = pre is not None
    col = lambda g: (0, g)
    lead = lambda g: (g, 0, 0)
    tail = lambda g: (0, 0, g)
    fixed = lambda g: (0, 0)
    f32, bf = jnp.float32, jnp.bfloat16
    vm = pltpu.VMEM
    if not causal:
        nz = lax.axis_size("adp")
        bott = keep.shape[2]
        rows, wide = bott // nz, TILE // 2
    return pl.pallas_call(
        functools.partial(attn_bwd_body, causal),
        grid=(pairs,),
        in_specs=[
            pl.BlockSpec((t, 128), col), pl.BlockSpec((s, 128), col), pl.BlockSpec((s, 128), col),
            pl.BlockSpec((t, 128), col), pl.BlockSpec((t, 128), col),
            pl.BlockSpec((1, 2, t), lead), pl.BlockSpec((2, s, t), lead),
        ] + ([pl.BlockSpec((2, PRE, t), lead), pl.BlockSpec((2, PRE, 128), tail), HBM, HBM] if causal else [HBM, HBM]),
        out_specs=[
            pl.BlockSpec((t, 128), col), pl.BlockSpec((s, 128), col), pl.BlockSpec((s, 128), col),
        ] + ([pl.BlockSpec((2, PRE, 128), tail), HBM] if causal else [pl.BlockSpec((rows, wide), fixed)] * 2),
        out_shape=[
            jax.ShapeDtypeStruct((t, w), bf), jax.ShapeDtypeStruct((s, w), bf), jax.ShapeDtypeStruct((s, w), bf),
        ] + ([jax.ShapeDtypeStruct((2, PRE, w), f32), jax.ShapeDtypeStruct(landed.shape, bf)] if causal
           else [jax.ShapeDtypeStruct((rows, wide), f32)] * 2),
        scratch_shapes=[pltpu.SemaphoreType.DMA((2,))] if causal else [
            vm(keep.shape, f32), vm((2, bott, wide), f32), vm(keep.shape, bf), vm((2, bott, TILE), bf), vm((2, bott, wide), bf),
            vm((nz - 1, 2, rows, wide), bf), vm((2, bott, TILE), bf), vm((2, bott, wide), bf), vm((nz - 1, 2, rows, wide), bf),
            pltpu.SemaphoreType.DMA((1,)), pltpu.SemaphoreType.DMA((nz + 2,)), pltpu.SemaphoreType.DMA((nz + 2,))],
        input_output_aliases={10: 4} if causal else {},
        compiler_params=pltpu.CompilerParams(
            vmem_limit_bytes=VMEM_BYTES, collective_id=3 if causal else 5, has_side_effects=True),
        cost_estimate=pl.CostEstimate(flops=40 * t * s * w, bytes_accessed=4 * t * s * pairs, transcendentals=0),
    )(q, k, v, a, da, il, p, *((pp, pre, moved, landed) if causal else (keep, give)))


def gelu_pair(v):
    x = 1.0 + (0.3275911 * 0.5 ** 0.5) * jnp.abs(v)
    t = pl.reciprocal(x, approx=True)
    t = t * (2.0 - x * t)
    expo = jnp.exp2(v * v * (-0.5 * LOG2E))
    poly = 0.127414796 + t * (-0.142248368 + t * (0.7107068705 + t * (-0.7265760135 + t * 0.5307027145)))
    half = poly * t * expo
    cdf = jnp.where(v < 0.0, half, 1.0 - half)
    return v * cdf, cdf + v * expo * (2.0 * math.pi) ** -0.5


def normalize(z):
    centered = z - jnp.mean(z, axis=-1, keepdims=True)
    inv = lax.rsqrt(jnp.mean(centered * centered, axis=-1, keepdims=True) + EPS)
    return centered * inv, inv


def norm_back(e, u, inv, gain):
    w = e * gain
    return inv * (w - jnp.mean(w, axis=-1, keepdims=True) - u * jnp.mean(w * u, axis=-1, keepdims=True))


def stack_rows(refs):
    return jnp.concatenate([r[...] for r in refs], axis=0)


def stack_cols(refs):
    return jnp.concatenate([r[...] for r in refs], axis=1)


def nn(lhs, tiles):
    return dot_mm(lhs, stack_rows(tiles), 1, 0)


def nt(lhs, tiles):
    return dot_mm(lhs, stack_cols(tiles), 1, 1)


def place_cols(value_ref, dp):
    n = value_ref.shape[1] // TILE
    return jnp.concatenate(
        [value_ref[:, pl.ds(pl.multiple_of((dp ^ r) * TILE, TILE), TILE)] for r in range(n)], axis=1)


def unplace_store(out, value, dp):
    for r in range(value.shape[1] // TILE):
        out[:, pl.ds(pl.multiple_of((dp ^ r) * TILE, TILE), TILE)] = (
            value[:, r * TILE:(r + 1) * TILE].astype(out.dtype))


class Exchange:
    def __init__(self, buf, out, local, send, recv, half):
        self.refs = buf, out, local, send, recv
        self.count, self.tile = buf.shape[0], buf.shape[1]
        self.half = half
        self.y = lax.axis_index("mp")

    def copies(self, i):
        buf, out, local, send, recv = self.refs
        rows = pl.ds(i * self.tile % self.half, self.tile)
        dst = out.at[self.y, rows]
        far = pltpu.make_async_remote_copy(src_ref=buf.at[i], dst_ref=dst, send_sem=send.at[i], recv_sem=recv.at[i],
                                           device_id={"mp": 1 - self.y}, device_id_type=pl.DeviceIdType.MESH)
        return pltpu.make_async_copy(buf.at[i], dst, local.at[i]), far

    def here(self, i):
        return self.y == i * self.tile // self.half

    def buffer(self, i):
        return self.refs[0].at[i]

    def send(self, i):
        near, far = self.copies(i)

        @pl.when(self.here(i))
        def _():
            near.start()

        @pl.when(jnp.logical_not(self.here(i)))
        def _():
            far.start()

    def finish(self):
        for i in range(self.count):
            near, far = self.copies(i)

            @pl.when(self.here(i))
            def _():
                near.wait()
                far.wait_recv()

            @pl.when(jnp.logical_not(self.here(i)))
            def _():
                far.wait_send()


def tiled(weights, rows, consts, outs, body, tile, steps, exchange=None, scratch=(), flops=0):
    nw, nr, nc, no = len(weights), len(rows), len(consts), len(outs)
    picks = [c for _, _, c in weights]
    piece = [own.shape if c is None else own.shape[1:] for own, _, c in weights]
    more = 1 if exchange else 0

    def kernel(*refs):
        srcs, refs = refs[:2 * nw], refs[2 * nw:]
        row_refs, const_refs, out_refs = refs[:nr], refs[nr:nr + nc], refs[nr + nc:nr + nc + no]
        refs = refs[nr + nc + no:]
        result, refs = refs[:more], refs[more:]
        wv, sems, refs = refs[:nw], refs[nw], refs[nw + 1:]
        step = pl.program_id(0)
        ex = Exchange(refs[0], result[0], *refs[1:4], exchange[1]) if exchange else None
        own_scratch = refs[4 * more:]

        def copies(i):
            own, far, c = srcs[2 * i], srcs[2 * i + 1], picks[i]
            own = own if c is None else own.at[c]
            some = lambda s, rs: far.at[s, rs] if c is None else far.at[s, rs, c]
            yield pltpu.make_async_copy(own, wv[i].at[0, 0], sems.at[i, 0])
            yield pltpu.make_async_copy(some(0, pl.ds(1, 3)), wv[i].at[0, pl.ds(1, 3)], sems.at[i, 1])
            yield pltpu.make_async_copy(some(1, pl.ds(0, 4)), wv[i].at[1], sems.at[i, 2])

        @pl.when(step == 0)
        def _():
            for i in range(nw):
                for copy in copies(i):
                    copy.start()
            if exchange:
                meet([{"mp": 1 - lax.axis_index("mp")}])

        def need(i):
            @pl.when(step == 0)
            def _():
                for copy in copies(i):
                    copy.wait()

        def put(value):
            dp = lax.axis_index("dp")
            unplace_store(ex.buffer(step), value, dp)
            for i in range(steps):
                @pl.when(step == i)
                def _():
                    ex.send(i)

        body(wv, need, row_refs, const_refs, out_refs, own_scratch, put)
        if exchange:
            @pl.when(step == steps - 1)
            def _():
                ex.finish()

    whole = lambda a: pl.BlockSpec(a.shape, lambda i: (0,) * a.ndim, pipeline_mode=pl.Buffered(1))
    ex_out, ex_shape, ex_scratch = [], [], []
    if exchange:
        _, half, cols = exchange
        ex_out, ex_shape = [HBM], [jax.ShapeDtypeStruct((2, half, cols), BF)]
        ex_scratch = [pltpu.VMEM((steps, tile, cols), BF)] + [pltpu.SemaphoreType.DMA((steps,))] * 3
    return pl.pallas_call(
        kernel,
        grid=(steps,),
        in_specs=[HBM] * (2 * nw) + [spec for _, spec in rows] + [whole(c) for c in consts],
        out_specs=[pl.BlockSpec(shape, index) for _, _, shape, index in outs] + ex_out,
        out_shape=[jax.ShapeDtypeStruct(shape, dtype) for shape, dtype, _, _ in outs] + ex_shape,
        scratch_shapes=[pltpu.VMEM((2, 4) + tuple(p), BF) for p in piece] + [pltpu.SemaphoreType.DMA((nw, 3))]
        + ex_scratch + list(scratch),
        compiler_params=pltpu.CompilerParams(
            vmem_limit_bytes=VMEM_BYTES, **(dict(collective_id=exchange[0], has_side_effects=True) if exchange else {})),
        cost_estimate=pl.CostEstimate(flops=flops, bytes_accessed=16 * 2**20, transcendentals=0),
    )(*[a for own, far, _ in weights for a in (own, far)], *[r[0] for r in rows], *consts)


def last_gradient(wq, dz1, dq, dk, dv, dpre, own_w):
    t, d = dz1.shape
    half = t // 2
    nz = lax.axis_size("adp")
    tile = half // 2
    count = t // tile
    hw = d // 2

    def kernel(wq_ref, dz_ref, dq_ref, dk_ref, dv_ref, dpre_ref, out, sum_ref,
               wv, zv, lv, buf, pv, got, tot, zbuf, sems, local, send, recv, psend, precv):
        dp, y, z, side, over, up = axes_here()
        along = [{"adp": lax.rem(z + k, nz)} for k in range(1, nz)]

        def rows_of(i):
            return pl.multiple_of(jnp.where(i < count // 2, 1 - y, y) * half + (i % 2) * tile, tile)

        def loads(i):
            rows = pl.ds(rows_of(i), tile)
            yield pltpu.make_async_copy(dz_ref.at[rows], zv.at[i], sems.at[4 * i])
            for c, ref in enumerate((dq_ref, dk_ref, dv_ref)):
                yield pltpu.make_async_copy(ref.at[rows], lv.at[i, :, pl.ds(c * d, d)], sems.at[4 * i + 1 + c])

        weight = pltpu.make_async_copy(wq_ref, wv, sems.at[4 * count])
        pre = pltpu.make_async_copy(dpre_ref, pv, sems.at[4 * count + 1])
        pre.start()
        weight.start()
        for i in range(count):
            for c in loads(i):
                c.start()
        meet([side, over, up] + along)

        def far(src, dst, peer, i):
            return pltpu.make_async_remote_copy(src_ref=src, dst_ref=dst, send_sem=psend.at[i], recv_sem=precv.at[i],
                                                device_id=peer, device_id_type=pl.DeviceIdType.MESH)

        first = far(pv.at[:, :, pl.ds(hw, hw)], got.at[0], up, 0)
        second = far(tot.at[0], got.at[1], side, 1)
        third = far(tot.at[1], got.at[2], over, 2)
        ring = [far(zbuf.at[z], zbuf.at[z], peer, 3 + k) for k, peer in enumerate(along)]

        def fold(k):
            if k == 0:
                first.wait_recv()
                tot[0] = pv[:, :, :hw] + got[0]
                second.start()
            elif k == 1:
                second.wait_recv()
                tot[1] = tot[0] + got[1]
                third.start()
            elif k == 2:
                third.wait_recv()
                zbuf[z] = tot[1] + got[2]
                for c in ring:
                    c.start()
            else:
                for c in ring:
                    c.wait_recv()
                total = zbuf[0]
                for j in range(1, nz):
                    total = total + zbuf[j]
                sum_ref[...] = total

        pre.wait()
        first.start()
        weight.wait()
        moves = []
        for i in range(count):
            for c in loads(i):
                c.wait()
            lhs = lv[i]
            e = jnp.concatenate(
                [dot_mm(lhs, jnp.concatenate([wv[s, r, c] for c in range(3) for s in range(2)], axis=1), 1, 1)
                 for r in range(d // TILE)], axis=1)
            unplace_store(buf.at[i], zv[i] + e, dp)
            dst = out.at[y, pl.ds((i % 2) * tile, tile)]
            if i < count // 2:
                move = pltpu.make_async_remote_copy(
                    src_ref=buf.at[i], dst_ref=dst, send_sem=send.at[i], recv_sem=recv.at[i],
                    device_id=up, device_id_type=pl.DeviceIdType.MESH)
            else:
                move = pltpu.make_async_copy(buf.at[i], dst, local.at[i])
            move.start()
            moves.append(move)
            if 1 <= i:
                fold(i - 1)
        fold(3)
        for c in [first, second, third] + ring:
            c.wait_send()
        for c in moves:
            c.wait()

    vm = pltpu.VMEM
    shape = jax.ShapeDtypeStruct
    dma = pltpu.SemaphoreType.DMA
    return pl.pallas_call(
        kernel,
        in_specs=[HBM] * 6,
        out_specs=[HBM, pl.BlockSpec(memory_space=pltpu.VMEM)],
        out_shape=[shape((2, half, d), BF), shape((2, PRE, hw), F32)],
        scratch_shapes=[vm(wq.shape, BF), vm((count, tile, d), F32), vm((count, tile, 3 * d), BF), vm((count, tile, d), BF),
                        vm((2, PRE, d), F32), vm((3, 2, PRE, hw), F32), vm((2, 2, PRE, hw), F32), vm((nz, 2, PRE, hw), F32),
                        dma((4 * count + 2,)), dma((count,)), dma((count,)), dma((count,)), dma((2 + nz,)), dma((2 + nz,))],
        compiler_params=pltpu.CompilerParams(collective_id=4, has_side_effects=True, vmem_limit_bytes=VMEM_BYTES),
        cost_estimate=pl.CostEstimate(flops=6 * t * d * d, bytes_accessed=2**24, transcendentals=0),
    )(wq, dz1, dq, dk, dv, dpre)


def by_rows(ref):
    return lambda s, r, j: ref.at[s, r, pl.ds(j * TILE, TILE)]


def by_cols(ref):
    return lambda s, r, j: ref.at[s, r, slice(None), pl.ds(j * TILE, TILE)]


def meet(peers):
    barrier = pltpu.get_barrier_semaphore()
    for peer in peers:
        pl.semaphore_signal(barrier, inc=1, device_id=peer, device_id_type=pl.DeviceIdType.MESH)
    pl.semaphore_wait(barrier, len(peers))


class Moves:
    def __init__(self, table, send, recv, local):
        self.table, self.send, self.recv, self.local = table, send, recv, local
        self.place = {}
        far = near = 0
        for name, (src, dst, peer) in table.items():
            if peer is None:
                self.place[name] = near
                near += 1
            else:
                self.place[name] = far
                far += 1

    def copy(self, name):
        src, dst, peer = self.table[name]
        i = self.place[name]
        if peer is None:
            return pltpu.make_async_copy(src, dst, self.local.at[i])
        return pltpu.make_async_remote_copy(src_ref=src, dst_ref=dst, send_sem=self.send.at[i], recv_sem=self.recv.at[i],
                                            device_id=peer, device_id_type=pl.DeviceIdType.MESH)

    def start(self, *names):
        for name in names:
            self.copy(name).start()

    def got(self, *names):
        for name in names:
            if self.table[name][2] is None:
                self.copy(name).wait()
            else:
                self.copy(name).wait_recv()

    def sent(self, *names):
        for name in names:
            self.copy(name).wait_send()


def axes_here():
    dp, y, z = lax.axis_index("dp"), lax.axis_index("mp"), lax.axis_index("adp")
    return dp, y, z, {"dp": dp ^ 1}, {"dp": dp ^ 2}, {"mp": 1 - y}


SPOTS = {"x": (0, 2), "y": (1, 0), "d": (1, 2)}


def plane_moves(table, tag, own, far, part, side, over, up):
    table[tag, "y"] = (part(own), part(far(1, 0)), up)
    table[tag, "x"] = (part(own), part(far(0, 2)), over)
    table[tag, "d"] = (part(far(1, 0)), part(far(1, 2)), over)
    for spot in "xyd":
        s, r = SPOTS[spot]
        table[tag, spot, "side"] = (part(far(s, r)), part(far(s, r ^ 1)), side)


def ring_moves(table, tag, own, far, quarter, z, nz, side, over, up, onward):
    first = quarter(z)
    table[tag, "y"] = (first(own), first(far(1, 0)), up)
    table[tag, "x"] = (first(own), first(far(0, 2)), over)
    table[tag, "d"] = (first(far(1, 0)), first(far(1, 2)), over)
    for spot in "xyd":
        s, r = SPOTS[spot]
        for k in range(nz):
            part = quarter(lax.rem(z + nz - k, nz))
            table[tag, spot, k, "side"] = (part(far(s, r)), part(far(s, r ^ 1)), side)
            if k + 1 < nz:
                table[tag, spot, k, "on"] = (part(far(s, r)), part(far(s, r)), onward)


def self_forward(inputs, memory, self_qkv, self_proj, cross_qkv, cross_proj, pre_own, ad_own):
    _, _, half, d = inputs.shape
    t = 2 * half
    nq, wrows, hw = self_qkv.shape
    nz = lax.axis_size("adp")
    prow = self_proj.shape[0]
    pairs = d // 128
    chunks = d // TILE
    qscale = HEAD_DIM ** -0.5 * LOG2E
    ring_tags = ("cq12", "co")
    plane_tags = ("so", "cq0")

    def moves(refs):
        (in_ref, mem_ref, own_ref, so_ref, cq_ref, co_ref, pre_ref, ad_ref,
         q_out, k_out, v_out, w_out, x_out, pre_out, bso, bcq, bco, mem_out, ada_ref, wv, xv, qs, ks, vs, pv) = refs
        dp, y, z, side, over, up = axes_here()
        onward = {"adp": lax.rem(z + 1, nz)}
        along = [{"adp": lax.rem(z + k, nz)} for k in range(1, nz)]
        rows = pl.ds(pl.multiple_of(y * half, half), half)
        table = {}
        table["w own"] = (own_ref, wv.at[0, 0], None)
        table["pre own"] = (pre_ref, pv.at[:, :, pl.ds(0, hw)], None)
        table["x own"] = (in_ref.at[y, 0], xv.at[rows], None)
        table["x up"] = (in_ref.at[1 - y, 0], xv.at[rows], up)
        table["pre up"] = (pre_ref, pv.at[:, :, pl.ds(hw, hw)], up)
        table["w", "side"] = (own_ref, wv.at[0, 1], side)
        table["w", "x"] = (own_ref, wv.at[0, 2], over)
        table["w", "x", "side"] = (wv.at[0, 2], wv.at[0, 3], side)
        quarter = lambda k: (slice(None), pl.ds(pl.multiple_of(lax.rem(z + nz - k, nz) * (wrows // nz), wrows // nz), wrows // nz))
        table["w", "y"] = (own_ref.at[quarter(0)], wv.at[(1, 0) + quarter(0)], up)
        for k in range(nz):
            beside, diagonal = wv.at[(1, 0) + quarter(k)], wv.at[(1, 2) + quarter(k)]
            table["w", "y", k, "side"] = (beside, wv.at[(1, 1) + quarter(k)], side)
            table["w", "d", k] = (beside, diagonal, over)
            table["w", "d", k, "side"] = (diagonal, wv.at[(1, 3) + quarter(k)], side)
            if k + 1 < nz:
                table["w", "y", k, "on"] = (beside, beside, onward)
        for k in range(1, nz):
            table["ad", k] = (ad_ref, ada_ref.at[k], along[k - 1])
        plane_moves(table, "so", so_ref, lambda s, r: bso.at[s, r], lambda ref: ref, side, over, up)
        plane_moves(table, "cq0", cq_ref, lambda s, r: bcq.at[s, r], lambda ref: ref.at[0], side, over, up)
        ring_moves(table, "cq12", cq_ref, lambda s, r: bcq.at[s, r],
                   lambda qz: lambda ref: ref.at[pl.ds(1, 2), pl.ds(pl.multiple_of(qz * (wrows // nz), wrows // nz), wrows // nz)],
                   z, nz, side, over, up, onward)
        ring_moves(table, "co", co_ref, lambda s, r: bco.at[s, r],
                   lambda qz: lambda ref: ref.at[pl.ds(pl.multiple_of(qz * (prow // nz), prow // nz), prow // nz)],
                   z, nz, side, over, up, onward)
        table["so", "side"] = (so_ref, bso.at[0, 1], side)
        table["cq", "side"] = (cq_ref, bcq.at[0, 1], side)
        table["co", "side"] = (co_ref, bco.at[0, 1], side)
        table["mem up"] = (mem_ref.at[1 - y, 0], mem_out, up)
        for name, s_, o_ in (("q", qs, q_out), ("k", ks, k_out), ("v", vs, v_out), ("w", wv, w_out), ("x", xv, x_out), ("pre", pv, pre_out)):
            table[name + " out"] = (s_, o_, None)
        return table, (side, over, up), along

    def count():
        rings = len(ring_tags) * (3 + 3 * nz + 3 * (nz - 1))
        planes = len(plane_tags) * 6
        return 1 + 1 + 4 + 4 * nz - 1 + planes + rings + (nz - 1) + 3 + 1, 9

    def kernel(in_ref, mem_ref, own_ref, so_ref, cq_ref, co_ref, pre_ref, ad_ref,
               a_ref, p_ref, pp_ref, l_ref, q_out, k_out, v_out, w_out, x_out, pre_out, bso, bcq, bco, mem_out, ada_ref,
               wv, xv, qs, ks, vs, pv, send, recv, local):
        g = pl.program_id(0)
        table, near_peers, along = moves((in_ref, mem_ref, own_ref, so_ref, cq_ref, co_ref, pre_ref, ad_ref,
                                          q_out, k_out, v_out, w_out, x_out, pre_out, bso, bcq, bco, mem_out, ada_ref,
                                          wv, xv, qs, ks, vs, pv))
        mv = Moves(table, send, recv, local)
        done = set()

        def got(*names):
            done.update(names)
            mv.got(*names)

        ads = [("ad", k) for k in range(1, nz)]
        outs = [n + " out" for n in ("q", "k", "v", "w", "x", "pre")]

        def pass_on(spot, k):
            if k >= nz:
                return
            for tag in ring_tags:
                got((tag, spot) if k == 0 else (tag, spot, k - 1, "on"))
                if k + 1 < nz:
                    mv.start((tag, spot, k, "on"))
                mv.start((tag, spot, k, "side"))

        @pl.when(g == 0)
        def _():
            meet(list(near_peers) + along)
            mv.start(("w", "y"), ("w", "x"), "pre up")
            mv.start(*[(tag, spot) for tag in ring_tags for spot in "yx"])
            mv.start("x up", *[(tag, "y") for tag in plane_tags])
            mv.start("mem up", ("w", "side"), "w own", "pre own", "x own")
            for k in range(nz):
                got(("w", "y") if k == 0 else ("w", "y", k - 1, "on"))
                if k + 1 < nz:
                    mv.start(("w", "y", k, "on"))
                mv.start(("w", "d", k), ("w", "y", k, "side"))
            pass_on("y", 0)
            pass_on("x", 0)
            mv.start(*[(tag, "d") for tag in ring_tags])
            mv.start(*[(tag, "x") for tag in plane_tags])
            got(("w", "x"))
            mv.start(("w", "x", "side"), ("so", "side"), ("cq", "side"), ("co", "side"))
            for k in range(nz):
                if 0 < k < nz - 1:
                    pass_on("y", k)
                    pass_on("x", k)
                got(("w", "d", k))
                mv.start(("w", "d", k, "side"))
            got("w own", "pre own", "pre up", "x own", "x up", ("w", "side"), ("w", "x", "side"))
            for k in range(nz):
                got(("w", "y", k, "side"), ("w", "d", k, "side"))
            for i in range(2):
                x = place_cols(xv.at[pl.ds(i * half, half)], lax.axis_index("dp"))
                for c, out in ((0, qs), (1, ks), (2, vs)):
                    for s in range(2):
                        w = jnp.concatenate([wv[s, r, c] for r in range(4)], axis=0)
                        o = dot_mm(x, w, 1, 0)
                        out[i * half:(i + 1) * half, s * hw:(s + 1) * hw] = (o * qscale if c == 0 else o).astype(BF)
                if i == 0:
                    pass_on("d", 0)
            if nz > 1:
                pass_on("y", nz - 1)
                pass_on("x", nz - 1)
            pass_on("d", 1)
            mv.start(*outs)

        for k in range(2, nz):
            @pl.when(g == 2 * (k - 1))
            def _():
                pass_on("d", k)
                if k == 2:
                    mv.start(*ads)

        @pl.when(g == 3)
        def _():
            for tag in plane_tags:
                got((tag, "y"), (tag, "x"))
                mv.start((tag, "d"), (tag, "y", "side"), (tag, "x", "side"))

        @pl.when(g > 0)
        def _():
            cs = pl.ds(pl.multiple_of((g - 1) * 128, 128), 128)
            a, il = attend_pair(True, PREFIX_LEN, qs[:, cs], ks[:, cs], vs[:, cs], pv[0, :, cs], pv[1, :, cs], p_ref, pp_ref)
            a_ref[...] = a
            l_ref[0] = il

        @pl.when(g == pairs)
        def _():
            for tag in plane_tags:
                got((tag, "d"))
                mv.start((tag, "d", "side"))
            far = [n for n, (_, _, peer) in table.items() if peer is not None]
            got(*[n for n in far if n not in done])
            got(*outs)
            mv.sent(*far)

    lead = lambda g: (jnp.maximum(g - 1, 0), 0, 0)
    col = lambda g: (0, jnp.maximum(g - 1, 0))
    shape = jax.ShapeDtypeStruct
    remotes, near = count()
    vm = pltpu.VMEM
    return pl.pallas_call(
        kernel,
        grid=(pairs + 1,),
        in_specs=[HBM] * 8,
        out_specs=[pl.BlockSpec((t, 128), col), pl.BlockSpec((2, t, t), lead), pl.BlockSpec((2, PRE, t), lead),
                   pl.BlockSpec((1, 2, t), lead)] + [HBM] * 11,
        out_shape=[
            shape((t, d), BF), shape((2 * pairs, t, t), BF), shape((2 * pairs, PRE, t), BF), shape((pairs, 2, t), F32),
            shape((t, d), BF), shape((t, d), BF), shape((t, d), BF), shape((2, 4) + self_qkv.shape, BF),
            shape((t, d), BF), shape((2, PRE, d), BF), shape((2, 4) + self_proj.shape, BF), shape((2, 4) + cross_qkv.shape, BF),
            shape((2, 4) + cross_proj.shape, BF), shape((half, d), BF), shape((nz,) + ad_own.shape, BF),
        ],
        scratch_shapes=[vm((2, 4) + self_qkv.shape, BF), vm((t, d), BF), vm((t, d), BF), vm((t, d), BF), vm((t, d), BF),
                        vm((2, PRE, d), BF), pltpu.SemaphoreType.DMA((remotes,)),
                        pltpu.SemaphoreType.DMA((remotes,)), pltpu.SemaphoreType.DMA((near,))],
        compiler_params=pltpu.CompilerParams(collective_id=0, has_side_effects=True, vmem_limit_bytes=VMEM_BYTES),
        cost_estimate=pl.CostEstimate(flops=10**11, bytes_accessed=10**8, transcendentals=0),
    )(inputs, memory, self_qkv, self_proj, cross_qkv, cross_proj, pre_own, ad_own)


def cross_forward(src_n, x_full, a, memory, mem_got, self_proj, b_so, cross_qkv, b_cq, ad_col, cotangent, ffn_in, ffn_out, gain):
    t, d = x_full.shape
    half = t // 2
    nz = lax.axis_size("adp")
    pairs = d // 128
    chunks = d // TILE
    khead = self_proj.shape[0] // TILE
    kcol = cross_qkv.shape[2] // TILE
    nq = cross_qkv.shape[0]
    orow = ffn_out.shape[0]
    ihalf = ffn_in.shape[0] // 2
    qscale = HEAD_DIM ** -0.5 * LOG2E

    def moves(refs):
        ad_ref, cot_ref, fi_ref, fo_ref, q_out, k_out, v_out, cin, cout, ada_ref, cot_out, qs, ks, vs = refs
        dp, y, z, side, over, up = axes_here()
        onward = {"adp": lax.rem(z + 1, nz)}
        before = {"adp": lax.rem(z + nz - 1, nz)}
        table = {}
        for name, s_, o_ in (("q", qs, q_out), ("k", ks, k_out), ("v", vs, v_out)):
            table[name + " out"] = (s_, o_, None)
        ring_moves(table, "o", fo_ref, lambda s, r: cout.at[s, r],
                   lambda qz: lambda ref: ref.at[pl.ds(pl.multiple_of(qz * (orow // nz), orow // nz), orow // nz)],
                   z, nz, side, over, up, onward)
        table["o", "side"] = (fo_ref, cout.at[0, 1], side)
        table["i", "side"] = (fi_ref, cin.at[0, 1], side)
        table["i", "y"] = (fi_ref, cin.at[1, 0], up)
        table["i", "x"] = (fi_ref, cin.at[0, 2], over)
        one, two = pl.ds(0, ihalf), pl.ds(ihalf, ihalf)
        table["i", "d1"] = (cin.at[1, 0, one], cin.at[1, 2, one], over)
        table["i", "d2"] = (cin.at[0, 2, two], cin.at[1, 2, two], up)
        table["i", "y", "side"] = (cin.at[1, 0], cin.at[1, 1], side)
        table["i", "x", "side"] = (cin.at[0, 2], cin.at[0, 3], side)
        table["i", "d1", "side"] = (cin.at[1, 2, one], cin.at[1, 3, one], side)
        table["i", "d2", "side"] = (cin.at[1, 2, two], cin.at[1, 3, two], side)
        table["ad side"] = (ad_ref, ada_ref.at[1], side)
        table["ad over"] = (ad_ref, ada_ref.at[2], over)
        table["ad over side"] = (ada_ref.at[2], ada_ref.at[3], side)
        table["cot"] = (cot_ref.at[1 - y, 0], cot_out, up)
        return table, [side, over, up, onward, before]

    def kernel(n_ref, x_ref, a_in, gain_ref, memg_ref, mem_ref, so_ref, bso, cq_ref, bcq, ad_ref, cot_ref, fi_ref, fo_ref,
               ac_ref, p_ref, l_ref, u_ref, inv_ref, q_out, k_out, v_out, cin, cout, ada_ref, cot_out,
               sov, cqv, memo_ref, qs, ks, vs, send, recv, local, wsem):
        g = pl.program_id(0)
        dp, y = lax.axis_index("dp"), lax.axis_index("mp")
        table, peers = moves((ad_ref, cot_ref, fi_ref, fo_ref, q_out, k_out, v_out, cin, cout, ada_ref, cot_out, qs, ks, vs))
        mv = Moves(table, send, recv, local)
        done = set()

        def got(*names):
            done.update(names)
            mv.got(*names)

        def pass_on(spot, k):
            if k >= nz:
                return
            got(("o", spot) if k == 0 else ("o", spot, k - 1, "on"))
            if k + 1 < nz:
                mv.start(("o", spot, k, "on"))
            mv.start(("o", spot, k, "side"))

        outs = [n + " out" for n in ("q", "k", "v")]

        def loads():
            yield pltpu.make_async_copy(mem_ref.at[y, 0], memo_ref, wsem.at[2, 0])
            for i, (own, far, dst) in enumerate(((so_ref, bso, sov), (cq_ref, bcq, cqv))):
                yield pltpu.make_async_copy(own, dst.at[0, 0], wsem.at[i, 0])
                yield pltpu.make_async_copy(far.at[0, pl.ds(1, 3)], dst.at[0, pl.ds(1, 3)], wsem.at[i, 1])
                yield pltpu.make_async_copy(far.at[1], dst.at[1], wsem.at[i, 2])

        so = by_rows(sov)

        def project(i):
            rs = slice(i * half, (i + 1) * half)
            att = a_in[rs]
            z1 = place_cols(x_ref.at[pl.ds(i * half, half)], dp).astype(F32) + jnp.concatenate(
                [nn(att, [so(s, r, j) for s in range(2) for j in range(khead)]) for r in range(chunks)], axis=1)
            u, inv = normalize(z1)
            u_ref[rs] = u
            inv_ref[rs] = inv
            h = (u * gain_ref[...]).astype(BF)
            xm = jnp.where(y == i, place_cols(memo_ref, dp), place_cols(memg_ref, dp))
            for lhs, c, out in ((h, 0, qs), (xm, 1, ks), (xm, 2, vs)):
                for s in range(2):
                    for j in range(kcol):
                        o = nn(lhs, [cqv.at[s, r, c, :, pl.ds(j * TILE, TILE)] for r in range(4)])
                        cs = slice((s * kcol + j) * TILE, (s * kcol + j + 1) * TILE)
                        out[rs, cs] = (o * qscale if c == 0 else o).astype(BF)

        @pl.when(g == 0)
        def _():
            for c in loads():
                c.start()
            meet(peers)
            mv.start(("o", "y"), ("o", "x"), ("i", "y"), "cot", ("o", "side"), ("i", "side"), "ad side")
            pass_on("y", 0)
            mv.start(("o", "d"), ("i", "x"))
            pass_on("x", 0)
            for c in loads():
                c.wait()
            project(0)
            pass_on("d", 0)
            pass_on("y", 1)
            pass_on("x", 1)
            project(1)
            pass_on("d", 1)
            got(("i", "y"))
            mv.start(("i", "d1"), ("i", "y", "side"), "ad over")
            mv.start(*outs)

        for k in range(2, nz):
            @pl.when(g == 5 * k - 8)
            def _():
                pass_on("y", k)
                pass_on("x", k)

            @pl.when(g == 4 * k - 4)
            def _():
                pass_on("d", k)

        @pl.when(g == 3)
        def _():
            got(("i", "x"))
            mv.start(("i", "d2"), ("i", "x", "side"))

        @pl.when(g > 0)
        def _():
            cs = pl.ds(pl.multiple_of((g - 1) * 128, 128), 128)
            av, il = attend_pair(False, n_ref[0], qs[:, cs], ks[:, cs], vs[:, cs], None, None, p_ref, None)
            ac_ref[...] = av
            l_ref[0] = il

        @pl.when(g == pairs)
        def _():
            got("ad over")
            mv.start("ad over side")
            got(("i", "d1"))
            mv.start(("i", "d1", "side"))
            got(("i", "d2"))
            mv.start(("i", "d2", "side"))
            far = [n for n, (_, _, peer) in table.items() if peer is not None]
            got(*[n for n in far if n not in done])
            got(*outs)
            mv.sent(*far)

    lead = lambda g: (jnp.maximum(g - 1, 0), 0, 0)
    col = lambda g: (0, jnp.maximum(g - 1, 0))
    fixed = lambda g: (0, 0)
    shape = jax.ShapeDtypeStruct
    once = pl.Buffered(1)
    remotes = 3 + 3 * nz + 3 * (nz - 1) + 10 + 4
    near = 3
    vm = pltpu.VMEM
    whole = lambda *s: pl.BlockSpec(s, fixed, pipeline_mode=once)
    return pl.pallas_call(
        kernel,
        grid=(pairs + 1,),
        in_specs=[pl.BlockSpec(memory_space=pltpu.SMEM), whole(t, d), whole(t, d), whole(1, d), whole(half, d)]
        + [HBM] * 9,
        out_specs=[pl.BlockSpec((t, 128), col), pl.BlockSpec((2, t, t), lead), pl.BlockSpec((1, 2, t), lead),
                   pl.BlockSpec((t, d), fixed), pl.BlockSpec((t, 1), fixed)] + [HBM] * 7,
        out_shape=[
            shape((t, d), BF), shape((2 * pairs, t, t), BF), shape((pairs, 2, t), F32), shape((t, d), F32), shape((t, 1), F32),
            shape((t, d), BF), shape((t, d), BF), shape((t, d), BF), shape((2, 4) + ffn_in.shape, BF), shape((2, 4) + ffn_out.shape, BF),
            shape((4,) + ad_col.shape, BF), shape((half, d), BF),
        ],
        scratch_shapes=[vm((2, 4) + self_proj.shape, BF), vm((2, 4) + cross_qkv.shape, BF), vm((half, d), BF), vm((t, d), BF), vm((t, d), BF), vm((t, d), BF),
                        pltpu.SemaphoreType.DMA((remotes,)), pltpu.SemaphoreType.DMA((remotes,)),
                        pltpu.SemaphoreType.DMA((near,)), pltpu.SemaphoreType.DMA((3, 3))],
        compiler_params=pltpu.CompilerParams(collective_id=1, has_side_effects=True, vmem_limit_bytes=VMEM_BYTES),
        cost_estimate=pl.CostEstimate(flops=10**11, bytes_accessed=10**8, transcendentals=0),
    )(src_n, x_full, a, gain, mem_got, memory, self_proj, b_so, cross_qkv, b_cq, ad_col, cotangent, ffn_in, ffn_out)


def whole_sequences(inputs, memory, src_lengths, self_qkv, self_proj, cross_qkv, cross_proj, ffn_in, ffn_out,
                    norm_gains, prefix, adapter_down, adapter_up, cotangent):
    dp, y, z = lax.axis_index("dp"), lax.axis_index("mp"), lax.axis_index("adp")
    nz = lax.axis_size("adp")
    half, d = inputs.shape[2], inputs.shape[3]
    t = 2 * half
    chunks = d // TILE
    rel = lambda a: jnp.concatenate(
        [lax.dynamic_slice_in_dim(a, (dp ^ r) * TILE, TILE, axis=a.ndim - 1) for r in range(chunks)], axis=-1)

    ad_own = jnp.concatenate([adapter_down.T, adapter_up], axis=0)
    pre_own = jnp.pad(prefix, ((0, 0), (0, PRE - PREFIX_LEN), (0, 0)))
    src_n = lax.dynamic_index_in_dim(src_lengths, y, 0, keepdims=False).reshape(1)
    khead, kcol = self_proj.shape[0] // TILE, cross_qkv.shape[2] // TILE
    kin = ffn_in.shape[1] // TILE

    gains = rel(norm_gains.astype(F32))
    gain = [gains[i:i + 1] for i in range(3)]
    row = lambda i: (i, 0)
    hw = self_qkv.shape[2]

    a, p, pp, il, q, k, v, wq, x_full, pre_w, b_so, b_cq, b_co, mem_got, ad_col = self_forward(
        inputs, memory, self_qkv, self_proj, cross_qkv, cross_proj, pre_own, ad_own)
    ad_col = lax.dynamic_update_slice_in_dim(ad_col, ad_own[None], 0, axis=0)
    w_so, w_co = (self_proj, b_so, None), (cross_proj, b_co, None)
    w_cq = lambda c: (cross_qkv, b_cq, c)
    out_rows = lambda T, r, n: [T(s, r, j) for s in range(2) for j in range(n)]
    ac, p_c, il_c, u1, inv1, qc, kc, vc, c_in, c_out, ad_all, cot_got = cross_forward(
        src_n, x_full, a, memory, mem_got, self_proj, b_so, cross_qkv, b_cq, ad_col, cotangent, ffn_in, ffn_out, gain[0])
    fixed = lambda i: (0, 0)
    spec = lambda shape, index: pl.BlockSpec(shape, index)
    held = lambda *shape: pl.BlockSpec(shape, lambda i: (0,) * len(shape), pipeline_mode=pl.Buffered(1))

    n_ad = ad_own.shape[0] // 2
    tile = half // FEED_SPLIT
    hid = 2 * kin

    def feed(W, need, rows, consts, outs, scr, put):
        dp, y = lax.axis_index("dp"), lax.axis_index("mp")
        ac_ref, u1_ref, cot_hbm, cot_b = rows
        act_ref, slope_ref, terms, cot_own, cot_sem = scr
        cot_a = cot_own.at[pl.ds(pl.multiple_of(lax.rem(pl.program_id(0), half // tile) * tile, tile), tile)]
        cot_load = pltpu.make_async_copy(cot_hbm.at[y, 0], cot_own, cot_sem.at[0])

        @pl.when(pl.program_id(0) == 0)
        def _():
            cot_load.start()

        g1, g2, g3 = consts[:3]
        co, fi, fo = by_rows(W[0]), by_cols(W[1]), by_rows(W[2])
        down = lambda r, kk: (consts[3].at[kk] if r == 0 else consts[4].at[r, kk]).at[pl.ds(0, n_ad)]
        upw = lambda r, kk: (consts[3].at[kk] if r == 0 else consts[4].at[r, kk]).at[pl.ds(n_ad, n_ad)]
        need(0)
        att = ac_ref[...]
        z2 = u1_ref[...] * g1[...] + jnp.concatenate(
            [nn(att, out_rows(co, r, khead)) for r in range(chunks)], axis=1)
        u2, inv2 = normalize(z2)
        h2 = u2 * g2[...]
        h2b = h2.astype(BF)
        need(1)
        order = [(s, j) for s in range(2) for j in range(kin)]
        acc = outs[0]
        down_t = jnp.concatenate([stack_cols([down(r, kk) for r in range(4)]) for kk in range(nz)], axis=0)
        up_m = jnp.concatenate([stack_cols([upw(r, kk) for r in range(4)]) for kk in range(nz)], axis=0)
        span = 256
        spans = [(s, j) for s in range(2) for j in range(kin * TILE // span)]

        def grow(i):
            s, j = spans[i]
            return nn(h2b, [W[1].at[s, r, slice(None), pl.ds(j * span, span)] for r in range(4)])

        def fall(i):
            s, j = spans[i]
            w = jnp.concatenate([W[2][s, r, j * span:(j + 1) * span] for r in range(4)], axis=1)
            return dot_mm(act_ref[:, i * span:(i + 1) * span], w, 1, 0)

        def bend(i, g):
            act, slope = gelu_pair(g)
            act_ref[:, i * span:(i + 1) * span] = act.astype(BF)
            slope_ref[:, i * span:(i + 1) * span] = slope.astype(BF)

        ahead = grow(0)
        g_a = dot_mm(h2b, down_t, 1, 1)
        act_a, slope_a = gelu_pair(g_a)
        act_a = act_a.astype(BF)
        need(2)
        for i in range(len(spans)):
            g = ahead
            if i + 1 < len(spans):
                ahead = grow(i + 1)
            if i == 1:
                acc[...] = h2 + fall(0)
            elif i > 1:
                acc[...] += fall(i - 1)
            bend(i, g)
        z3 = acc[...] + fall(len(spans) - 1) + 4.0 * dot_mm(act_a, up_m, 1, 0)
        u3, inv3 = normalize(z3)
        put(u3 * g3[...])

        @pl.when(pl.program_id(0) == 0)
        def _():
            cot_load.wait()

        in_own = pl.program_id(0) // (half // tile) == y
        cot = jnp.where(in_own, place_cols(cot_a, dp), place_cols(cot_b, dp)).astype(F32)
        dz3 = norm_back(cot, u3, inv3, g3[...])
        b3 = dz3.astype(BF)
        dga = (4.0 * dot_mm(b3, up_m, 1, 1) * slope_a).astype(BF)
        up_term = 4.0 * dot_mm(act_a, b3, 0, 0)
        down_term = dot_mm(dga, h2b, 0, 0)

        @pl.when(pl.program_id(0) == 0)
        def _():
            terms[0] = down_term
            terms[1] = up_term

        @pl.when(pl.program_id(0) > 0)
        def _():
            terms[0] += down_term
            terms[1] += up_term

        @pl.when(pl.program_id(0) == pl.num_programs(0) - 1)
        def _():
            for i in range(2):
                outs[2][:, i] = terms[:, :, 2 * i * TILE:(2 * i + 1) * TILE]
                outs[3][:, i] = terms[:, :, (2 * i + 1) * TILE:(2 * i + 2) * TILE].astype(BF)

        for i, (s, j) in enumerate(order):
            cs = slice(i * TILE, (i + 1) * TILE)
            df = nt(b3, [fo(s, r, j) for r in range(4)])
            slope_ref[:, cs] = (df * slope_ref[:, cs].astype(F32)).astype(BF)
        dg = slope_ref[...]
        dh2 = dz3 + dot_mm(dga, down_t, 1, 0) + jnp.concatenate(
            [nt(dg, out_rows(fi, r, kin)) for r in range(chunks)], axis=1)
        dz2 = norm_back(dh2, u2, inv2, g2[...])
        outs[0][...] = dz2
        dz2b = dz2.astype(BF)
        for s in range(2):
            for j in range(khead):
                i = s * khead + j
                outs[1][:, i * TILE:(i + 1) * TILE] = nt(dz2b, [co(s, r, j) for r in range(4)]).astype(BF)

    part = lambda i: (i % (half // tile), 0)
    dz2, dac, keep, give, result = tiled(
        [w_co, (ffn_in, c_in, None), (ffn_out, c_out, None)],
        [(ac, spec((tile, d), row)), (u1, spec((tile, d), row)), (cotangent, HBM),
         (cot_got, spec((tile, d), part))],
        gain + [ad_col, ad_all],
        [((t, d), F32, (tile, d), row), ((t, d), BF, (tile, d), row),
         ((2, 2, nz * n_ad, TILE), F32, (2, 2, nz * n_ad, TILE), lambda i: (0, 0, 0, 0)),
         ((2, 2, nz * n_ad, TILE), BF, (2, 2, nz * n_ad, TILE), lambda i: (0, 0, 0, 0))],
        feed, tile, t // tile, exchange=(2, half, d),
        scratch=[pltpu.VMEM((tile, hid * TILE), BF)] * 2 + [pltpu.VMEM((2, nz * n_ad, d), F32), pltpu.VMEM((half, d), BF), pltpu.SemaphoreType.DMA((1,))],
        flops=4 * 2 * t * d * hid * TILE)

    dqc, dkc, dvc, down_grad, up_grad = attn_bwd(qc, kc, vc, ac, dac, il_c, p_c, keep=keep, give=give)

    def memory_back(sc, own, far, dk_ref, dv_ref, mine_ref, send_ref, wv, sems):
        def loads():
            yield pltpu.make_async_copy(own.at[pl.ds(1, 2)], wv.at[0, 0], sems.at[0])
            yield pltpu.make_async_copy(far.at[0, pl.ds(1, 3), pl.ds(1, 2)], wv.at[0, pl.ds(1, 3)], sems.at[1])
            yield pltpu.make_async_copy(far.at[1, pl.ds(0, 4), pl.ds(1, 2)], wv.at[1], sems.at[2])

        step = pl.program_id(0)

        @pl.when(step == 0)
        def _():
            for c in loads():
                c.start()
            for c in loads():
                c.wait()

        lhs = jnp.concatenate([dk_ref[...], dv_ref[...]], axis=1)
        e = jnp.concatenate(
            [dot_mm(lhs, jnp.concatenate([wv[s, r, c] for c in range(2) for s in range(2)], axis=1), 1, 1)
             for r in range(chunks)], axis=1)

        @pl.when(step == 0)
        def _():
            unplace_store(send_ref, e, sc[0])

        @pl.when(step == 1)
        def _():
            unplace_store(mine_ref.at[0], e, sc[0])

    turned = lambda i, sc: (jnp.where(i == 0, 1 - sc[1], sc[1]), 0)
    mem_mine, mem_send = pl.pallas_call(
        memory_back,
        grid_spec=pltpu.PrefetchScalarGridSpec(
            num_scalar_prefetch=1, grid=(2,),
            in_specs=[HBM, HBM, pl.BlockSpec((half, d), turned), pl.BlockSpec((half, d), turned)],
            out_specs=[pl.BlockSpec((1, half, d), lambda i, sc: (sc[1], 0, 0)), pl.BlockSpec((half, d), lambda i, sc: (0, 0))],
            scratch_shapes=[pltpu.VMEM((2, 4, 2) + cross_qkv.shape[1:], BF), pltpu.SemaphoreType.DMA((3,))]),
        out_shape=[jax.ShapeDtypeStruct((2, half, d), BF), jax.ShapeDtypeStruct((half, d), BF)],
        compiler_params=pltpu.CompilerParams(vmem_limit_bytes=VMEM_BYTES),
        cost_estimate=pl.CostEstimate(flops=4 * t * d * d, bytes_accessed=2**24, transcendentals=0),
    )(jnp.stack([dp, y]).astype(jnp.int32), cross_qkv, b_cq, dkc, dvc)

    def norm_back_self(W, need, rows, consts, outs, scr, put):
        dz2_ref, dqc_ref, u1_ref, inv_ref = rows
        cq, so = by_cols(W[0]), by_rows(W[1])
        need(0)
        dq_c = dqc_ref[...]
        e = dz2_ref[...] + jnp.concatenate([nt(dq_c, out_rows(cq, r, kcol)) for r in range(chunks)], axis=1)
        dz1 = norm_back(e, u1_ref[...], inv_ref[...], consts[0][...])
        outs[0][...] = dz1
        dz1b = dz1.astype(BF)
        need(1)
        for s in range(2):
            for j in range(khead):
                i = s * khead + j
                outs[1][:, i * TILE:(i + 1) * TILE] = nt(dz1b, [so(s, r, j) for r in range(4)]).astype(BF)

    dz1, da = tiled(
        [w_cq(0), w_so],
        [(dz2, spec((half, d), row)), (dqc, spec((half, d), row)), (u1, spec((half, d), row)), (inv1, spec((half, 1), row))],
        [gain[0]],
        [((t, d), F32, (half, d), row), ((t, d), BF, (half, d), row)], norm_back_self, half, 2,
        flops=4 * t * d * d)

    dq, dk, dv, dpre, memory_grad = attn_bwd(q, k, v, a, da, il, p, pp, pre_w, mem_send, mem_mine)
    input_grad, pre_sum = last_gradient(wq, dz1, dq, dk, dv, dpre, self_qkv)
    return result[:, None], input_grad[:, None], memory_grad[:, None], pre_sum[:, :PREFIX_LEN], down_grad, up_grad


def solution(mesh):
    by_sequence = mesh.shape["mp"] == MICRO and mesh.shape["dp"] == 4
    return jax.shard_map(
        whole_sequences if by_sequence else shards,
        mesh=mesh,
        in_specs=(
            P(None, ("dp", "adp"), "mp", None),
            P(None, ("dp", "adp"), "mp", None),
            P(None, ("dp", "adp"), None),
            P(None, "dp", "mp"),
            P("mp", "dp"),
            P(None, "dp", "mp"),
            P("mp", "dp"),
            P("dp", "mp"),
            P("mp", "dp"),
            P(),
            P(None, None, "mp"),
            P("dp", "adp"),
            P("adp", "dp"),
            P(None, ("dp", "adp"), "mp", None),
        ),
        out_specs=(
            P(None, ("dp", "adp"), "mp", None),
            P(None, ("dp", "adp"), "mp", None),
            P(None, ("dp", "adp"), "mp", None),
            P(None, None, "mp"),
            P(("dp", "mp"), "adp"),
            P("adp", ("dp", "mp")),
        ),
        check_vma=False,
    )
```
